32 devices in a mesh: ctx: 8 (over y, x, core), fsdp: 4 (over z).
Axes of the slice: x: 2, y: 2, z: 4, core: 2. Of those that a mesh axis runs over, the one named last changes fastest.
Arguments:
- inputs: bfloat16 [4096, 2048], P(('ctx', 'fsdp')), may hold values from -6 to 6
- attention_gain: float32 [2048], replicated, may hold values from 0.5 to 1.5
- qkv_weight: bfloat16 [2048, 3072], P('fsdp'), may hold values from -0.125 to 0.125
- query_gain: float32 [64], replicated, may hold values from 0.1 to 1.9
- key_gain: float32 [64], replicated, may hold values from 0.1 to 1.9
- out_weight: bfloat16 [2048, 2048], P('fsdp'), may hold values from -1.5 to 1.5
- mlp_gain: float32 [2048], replicated, may hold values from 0.5 to 1.5
- gate_up_weight: bfloat16 [2048, 16384], P('fsdp'), may hold values from -0.125 to 0.125
- down_weight: bfloat16 [8192, 2048], P('fsdp'), may hold values from -0.0625 to 0.0625
- cotangent: bfloat16 [4096, 2048], P(('ctx', 'fsdp')), may hold values from -6 to 6
Outputs:
- outputs: bfloat16 [4096, 2048], P(('ctx', 'fsdp'))
- grad_inputs: bfloat16 [4096, 2048], P(('ctx', 'fsdp'))
- grad_attention_gain: float32 [2048], replicated
- grad_qkv_weight: float32 [2048, 3072], P('fsdp')
- grad_query_gain: float32 [64], replicated
- grad_key_gain: float32 [64], replicated
- grad_out_weight: float32 [2048, 2048], P('fsdp')
- grad_mlp_gain: float32 [2048], replicated
- grad_gate_up_weight: float32 [2048, 16384], P('fsdp')
- grad_down_weight: float32 [8192, 2048], P('fsdp')
The draws below stay inside these ranges and needn't reach their ends.
All inputs are finite; a program needn't handle non-finite values.
Results may differ from the reference program's by a relative error of at most 0.023.
Values may be sent and summed in bfloat16 or wider, within the bound.
No kernel may reach another device: no remote copies, remote signals or barrier semaphores. Data moves between devices by JAX's collectives and lax.ppermute only.
A program may use at most 640 MiB of HBM per device.

```python
import jax
import jax.numpy as jnp
from jax import lax

D = 2048
HEADS = 32
KV_HEADS = 8
HEAD_DIM = 64
FF = 8192
LENGTH = 4096
QKV = 3072


def steps_of(stream_key, extent, shards, smallest, top_value):
    level = 1.0
    for position, blocks in shards:
        draws = jax.random.uniform(jax.random.fold_in(jax.random.fold_in(stream_key, 6), position), (blocks,), jnp.float32, smallest / len(shards), top_value / len(shards))
        level = level * jnp.repeat(jnp.exp(draws), extent[position] // blocks).reshape((-1,) + (1,) * (len(extent) - 1 - position))
    return level


def centred(rng, extent, width, reach, pieces=(), kind=jnp.bfloat16):
    values = width * jax.random.normal(rng, extent, jnp.float32)
    if pieces:
        values = values * steps_of(rng, extent, pieces, -0.22, 0.18)
    return jnp.clip(values, -reach, reach).astype(kind)


def setup_inputs(seed: int = 0) -> dict:
    streams_of = jax.random.split(jax.random.key(seed), 11)
    inputs = centred(streams_of[0], (LENGTH, D), 1.0, 6.0, ((0, 32),))
    attention_gain = jnp.clip(1.0 + 0.1 * jax.random.normal(streams_of[1], (D,), jnp.float32), 0.5, 1.5)
    qkv_weight = centred(streams_of[2], (D, QKV), D ** -0.5, 0.125, ((0, 4),))
    query_gain = jnp.clip(1.0 + 0.18 * jax.random.normal(streams_of[3], (HEAD_DIM,), jnp.float32), 0.1, 1.9)
    key_gain = jnp.clip(1.0 + 0.18 * jax.random.normal(streams_of[4], (HEAD_DIM,), jnp.float32), 0.1, 1.9)
    out_weight = centred(streams_of[5], (HEADS * HEAD_DIM, D), 16 ** -0.5, 1.5, ((0, 4),))
    mlp_gain = jnp.clip(1.0 + 0.1 * jax.random.normal(streams_of[6], (D,), jnp.float32), 0.5, 1.5)
    gate_up_weight = centred(streams_of[7], (D, 2 * FF), D ** -0.5, 0.125, ((0, 4),))
    down_weight = centred(streams_of[8], (FF, D), FF ** -0.5, 0.0625, ((0, 4),))
    cotangent = centred(streams_of[9], (LENGTH, D), 1.0, 6.0, ((0, 32),))
    return {"inputs": inputs, "attention_gain": attention_gain, "qkv_weight": qkv_weight, "query_gain": query_gain, "key_gain": key_gain, "out_weight": out_weight, "mlp_gain": mlp_gain, "gate_up_weight": gate_up_weight, "down_weight": down_weight, "cotangent": cotangent}


@jax.custom_vjp
def low(v):
    return lax.optimization_barrier(v.astype(jnp.bfloat16)).astype(jnp.float32)

@jax.custom_vjp
def low_back(v):
    return v

def low_keep(v):
    return (low(v), None)

def low_pass(kept, grad):
    return (grad,)

def back_keep(v):
    return (v, None)

def back_low(kept, grad):
    return (low(grad),)
low.defvjp(low_keep, low_pass)
low_back.defvjp(back_keep, back_low)
epsilon = 1e-05
theta = 1000000.0
negative = -1e+30

def matmul(left, right):
    return jnp.dot(left, right, precision=lax.Precision.HIGHEST)

def rms_scale(values, gain):
    return values * lax.rsqrt(lax.optimization_barrier(jnp.mean(values * values, axis=-1, keepdims=True)) + epsilon) * gain

def rotate(values, positions):
    half_dim = values.shape[-1] // 2
    frequency = theta ** (-jnp.arange(half_dim, dtype=jnp.float32) * 2.0 / values.shape[-1])
    angles = positions.astype(jnp.float32)[:, None] * frequency[None, :]
    cosine = jnp.cos(angles)[:, None, :]
    sine_part = jnp.sin(angles)[:, None, :]
    lower_half = values[..., :half_dim]
    upper_half = values[..., half_dim:]
    return jnp.concatenate([lower_half * cosine - upper_half * sine_part, upper_half * cosine + lower_half * sine_part], axis=-1)

def attention_inputs(qkv_rows, query_gain, key_gain, positions):
    row_count = qkv_rows.shape[0]
    query_width = HEADS * HEAD_DIM
    key_width = KV_HEADS * HEAD_DIM
    queries = qkv_rows[:, :query_width].reshape(row_count, HEADS, HEAD_DIM)
    key_rows = qkv_rows[:, query_width:query_width + key_width].reshape(row_count, KV_HEADS, HEAD_DIM)
    value_rows = qkv_rows[:, query_width + key_width:].reshape(row_count, KV_HEADS, HEAD_DIM)
    return (rotate(rms_scale(queries, query_gain), positions), rotate(rms_scale(key_rows, key_gain), positions), value_rows)

def swiglu(gate_up):
    hidden_width = gate_up.shape[1] // 2
    return jax.nn.silu(gate_up[:, :hidden_width]) * gate_up[:, hidden_width:]

def attend(queries, key_rows, value_rows):
    length = queries.shape[0]
    group_size = HEADS // KV_HEADS
    key_rep = jnp.repeat(key_rows, group_size, axis=1)
    value_rep = jnp.repeat(value_rows, group_size, axis=1)
    row_block = 128 if length % 128 == 0 else length
    key_positions = jnp.arange(length, dtype=jnp.int32)
    score_scale = HEAD_DIM ** (-0.5)

    def one_block(block_item):
        query_block, first_row = block_item
        scores = low_back(jnp.einsum('qhd,khd->hqk', query_block, key_rep, precision=lax.Precision.HIGHEST) * score_scale)
        row_positions = first_row + jnp.arange(row_block, dtype=jnp.int32)
        visible = key_positions[None, None, :] <= row_positions[None, :, None]
        masked = jnp.where(visible, scores, negative)
        log_total = jax.nn.logsumexp(masked, axis=-1, keepdims=True)
        probabilities = low(jnp.exp(masked - log_total))
        return jnp.einsum('hqk,khd->qhd', probabilities, value_rep, precision=lax.Precision.HIGHEST)
    query_blocks = queries.reshape(length // row_block, row_block, HEADS, HEAD_DIM)
    first_rows = jnp.arange(length // row_block, dtype=jnp.int32) * row_block
    attended = lax.map(jax.checkpoint(one_block), (query_blocks, first_rows))
    return attended.reshape(length, HEADS * HEAD_DIM)

def forward(inputs, attention_gain, qkv_weight, query_gain, key_gain, out_weight, mlp_gain, gate_up_weight, down_weight):
    length = inputs.shape[0]
    positions = jnp.arange(length, dtype=jnp.int32)
    normed_attn = low(rms_scale(inputs, attention_gain))
    qkv_rows = low_back(matmul(normed_attn, qkv_weight))
    queries, key_rows, value_rows = attention_inputs(qkv_rows, query_gain, key_gain, positions)
    attended = low(low_back(attend(low(queries), low(key_rows), low(value_rows))))
    hidden_mid = inputs + low_back(matmul(attended, out_weight))
    normed_mlp = low(rms_scale(hidden_mid, mlp_gain))
    gate_up = low_back(matmul(normed_mlp, gate_up_weight))
    activated = low(swiglu(gate_up))
    return hidden_mid + low_back(matmul(activated, down_weight))

def reference(inputs, attention_gain, qkv_weight, query_gain, key_gain, out_weight, mlp_gain, gate_up_weight, down_weight, cotangent):
    arguments = (inputs, attention_gain, qkv_weight, query_gain, key_gain, out_weight, mlp_gain, gate_up_weight, down_weight)
    arguments = tuple((entry.astype(jnp.float32) for entry in arguments))
    result, pull_back = jax.vjp(forward, *arguments)
    grads = pull_back(cotangent.astype(jnp.float32))
    return (result.astype(jnp.bfloat16), grads[0].astype(jnp.bfloat16), grads[1], grads[2], grads[3], grads[4], grads[5], grads[6], grads[7], grads[8])
```

```python
import functools

import jax
import jax.numpy as jnp
from jax import lax
from jax.experimental import pallas as pl
from jax.experimental.pallas import tpu as pltpu
from jax.sharding import PartitionSpec as P

HEADS = 32
KV_HEADS = 8
HEAD_DIM = 64
GROUP = HEADS // KV_HEADS
GROUP_WIDTH = GROUP * HEAD_DIM

epsilon = 1e-05
theta = 1000000.0
score_scale = HEAD_DIM ** (-0.5)

f32 = jnp.float32
bf16 = jnp.bfloat16

CELL = KV_HEADS

NN = (((1,), (0,)), ((), ()))
NT = (((1,), (1,)), ((), ()))
TN = (((0,), (0,)), ((), ()))


def dot(left, right, dims=NN):
    return lax.dot_general(left, right, dims, preferred_element_type=f32)


def rms_scale(values, gain):
    return values * lax.rsqrt(jnp.mean(values * values, axis=-1, keepdims=True) + epsilon) * gain


def xor_send(values, distance):
    count = lax.axis_size("ctx")
    return lax.ppermute(values, "ctx", [(i, i ^ distance) for i in range(count)])


def cell_send(values, step):
    count = lax.axis_size("ctx")
    return lax.ppermute(values, "ctx", [(i, (i + step * CELL) % count) for i in range(count)])


def fsdp_send(values, step):
    count = lax.axis_size("fsdp")
    return lax.ppermute(values, "fsdp", [(i, (i + step) % count) for i in range(count)])


def pair_send(values, step, pair):
    count = lax.axis_size("fsdp")
    return lax.ppermute(
        values, "fsdp", [(i, i // pair * pair + (i % pair + step) % pair) for i in range(count)]
    )


def gather_cell(shard):
    half = shard.shape[0] // 2
    from_x = xor_send(shard, 2)
    from_y = xor_send(shard, 4)
    own_twin = xor_send(shard, 1)
    corner = jnp.concatenate([xor_send(from_y[:half], 2), xor_send(from_x[half:], 4)], axis=0)
    return [
        shard,
        own_twin,
        from_x,
        xor_send(from_x, 1),
        from_y,
        xor_send(from_y, 1),
        corner,
        xor_send(corner, 1),
    ]


def blank(shape, dtype):
    return pl.pallas_call(
        lambda ref: None,
        out_specs=pl.BlockSpec(memory_space=pl.ANY),
        out_shape=jax.ShapeDtypeStruct(shape, dtype),
        cost_estimate=pl.CostEstimate(flops=0, bytes_accessed=0, transcendentals=0),
    )()


def add_low(left, right):
    return (left.astype(f32) + right.astype(f32)).astype(bf16)


def reduce_cell(pieces):
    corner = add_low(pieces[6], xor_send(pieces[7], 1))
    at_x = add_low(pieces[2], xor_send(pieces[3], 1))
    at_y = add_low(pieces[4], xor_send(pieces[5], 1))
    own = add_low(pieces[0], xor_send(pieces[1], 1))
    half = corner.shape[0] // 2
    over_x = xor_send(corner[:half], 2)
    over_y = xor_send(corner[half:], 4)
    at_y = jnp.concatenate([add_low(at_y[:half], over_x), at_y[half:]], axis=0)
    at_x = jnp.concatenate([at_x[:half], add_low(at_x[half:], over_y)], axis=0)
    return (
        own.astype(f32) + xor_send(at_x, 2).astype(f32) + xor_send(at_y, 4).astype(f32)
    )


def stack_heads(block):
    return jnp.concatenate(
        [block[:, i * HEAD_DIM : (i + 1) * HEAD_DIM] for i in range(GROUP)], axis=0
    )


def unstack_heads(turned, rows):
    return jnp.concatenate([turned[:, i * rows : (i + 1) * rows].T for i in range(GROUP)], axis=1)


def fill_turned(place_ref, kv_ref, turned_ref, chunk):
    @pl.when(pl.program_id(0) == 0)
    def _():
        def turn(n, _):
            start = pl.multiple_of(n * chunk, chunk)
            turned_ref[:, pl.ds(start, chunk)] = kv_ref[pl.ds(start, chunk), :].T
            return 0

        lax.fori_loop(0, (place_ref[1] + 1) * CELL, turn, 0)


def visible_keys(place_ref, chunk, rows):
    key_at = lax.broadcasted_iota(jnp.int32, (chunk, GROUP * rows), 0)
    row_at = lax.broadcasted_iota(jnp.int32, (chunk, GROUP * rows), 1) % rows
    return key_at <= row_at + place_ref[0] * rows


def attention_kernel(chunk, place_ref, q_ref, kv_ref, out_ref, log_ref, turned_ref):
    rows = q_ref.shape[0]
    fill_turned(place_ref, kv_ref, turned_ref, chunk)
    queries = stack_heads(q_ref[...].astype(f32) * score_scale).astype(bf16)
    queries = jnp.concatenate([queries, jnp.zeros_like(queries)], axis=1)

    def step(n, running, masked):
        total, summed = running
        start = pl.multiple_of(n * chunk, chunk)
        weights = jnp.exp(dot(kv_ref[pl.ds(start, chunk), :], queries, NT))
        if masked:
            weights = jnp.where(visible_keys(place_ref, chunk, rows), weights, 0.0)
        return (
            total + jnp.sum(weights, axis=0, keepdims=True),
            summed + dot(turned_ref[:, pl.ds(start, chunk)], weights.astype(bf16)),
        )

    last = place_ref[1] * CELL + pl.program_id(0)
    running = (
        jnp.zeros((1, GROUP * rows), f32),
        jnp.zeros((2 * HEAD_DIM, GROUP * rows), f32),
    )
    running = lax.fori_loop(0, last, lambda n, r: step(n, r, False), running)
    total, summed = step(last, running, True)
    out_ref[...] = unstack_heads(summed[HEAD_DIM:] / total, rows)
    log_ref[...] = jnp.log(total)[None]


def attention(place, queries, keys_values, rows, chunk):
    count = queries.shape[0] // rows
    keys = keys_values.shape[0]
    return pl.pallas_call(
        functools.partial(attention_kernel, chunk),
        grid_spec=pltpu.PrefetchScalarGridSpec(
            num_scalar_prefetch=1,
            grid=(count,),
            in_specs=[
                pl.BlockSpec((rows, GROUP_WIDTH), lambda i, place: (i, 0)),
                pl.BlockSpec((keys, 2 * HEAD_DIM), lambda i, place: (0, 0)),
            ],
            out_specs=[
                pl.BlockSpec((rows, GROUP_WIDTH), lambda i, place: (i, 0)),
                pl.BlockSpec((1, 1, GROUP * rows), lambda i, place: (i, 0, 0)),
            ],
            scratch_shapes=[pltpu.VMEM((2 * HEAD_DIM, keys), bf16)],
        ),
        out_shape=[
            jax.ShapeDtypeStruct(queries.shape, f32),
            jax.ShapeDtypeStruct((count, 1, GROUP * rows), f32),
        ],
        compiler_params=pltpu.CompilerParams(vmem_limit_bytes=48 * 1024 * 1024),
        cost_estimate=pl.CostEstimate(
            flops=4 * HEADS * HEAD_DIM * rows * keys * 4,
            bytes_accessed=8 * 1024 * 1024,
            transcendentals=GROUP * rows * keys * 4,
        ),
    )(place, queries, keys_values)


def attention_grad_kernel(
    chunk, place_ref, q_ref, grad_ref, out_ref, log_ref, kv_ref, q_grad_ref, kv_grad_ref, turned_ref
):
    rows = q_ref.shape[0]
    fill_turned(place_ref, kv_ref, turned_ref, chunk)

    @pl.when(pl.program_id(0) == 0)
    def _():
        kv_grad_ref[...] = jnp.zeros_like(kv_grad_ref)

    queries = stack_heads(q_ref[...].astype(f32) * score_scale).astype(bf16)
    queries = jnp.concatenate([queries, jnp.zeros_like(queries)], axis=1)
    grads = stack_heads(grad_ref[...])
    row_delta = jnp.sum((grads.astype(f32) * stack_heads(out_ref[...])).T, axis=0, keepdims=True)
    grads = jnp.concatenate([jnp.zeros_like(grads), grads], axis=1)
    log_total = log_ref[0]

    def step(n, summed, masked):
        start = pl.multiple_of(n * chunk, chunk)
        block = kv_ref[pl.ds(start, chunk), :]
        weights = jnp.exp(dot(block, queries, NT) - log_total)
        if masked:
            weights = jnp.where(visible_keys(place_ref, chunk, rows), weights, 0.0)
        score_grad = (weights * (dot(block, grads, NT) - row_delta)).astype(bf16)
        kv_grad_ref[pl.ds(start, chunk), :] += dot(score_grad, queries) + dot(
            weights.astype(bf16), grads
        )
        return summed + dot(turned_ref[:, pl.ds(start, chunk)], score_grad)

    last = place_ref[1] * CELL + pl.program_id(0)
    summed = jnp.zeros((2 * HEAD_DIM, GROUP * rows), f32)
    summed = lax.fori_loop(0, last, lambda n, r: step(n, r, False), summed)
    summed = step(last, summed, True)
    q_grad_ref[...] = unstack_heads(summed[:HEAD_DIM] * score_scale, rows)


def attention_grad(place, queries, out_grad, attended, log_total, keys_values, rows, chunk):
    count = queries.shape[0] // rows
    keys = keys_values.shape[0]
    row_spec = pl.BlockSpec((rows, GROUP_WIDTH), lambda i, place: (i, 0))
    whole_spec = pl.BlockSpec((keys, 2 * HEAD_DIM), lambda i, place: (0, 0))
    return pl.pallas_call(
        functools.partial(attention_grad_kernel, chunk),
        grid_spec=pltpu.PrefetchScalarGridSpec(
            num_scalar_prefetch=1,
            grid=(count,),
            in_specs=[
                row_spec,
                row_spec,
                row_spec,
                pl.BlockSpec((1, 1, GROUP * rows), lambda i, place: (i, 0, 0)),
                whole_spec,
            ],
            out_specs=[row_spec, whole_spec],
            scratch_shapes=[pltpu.VMEM((2 * HEAD_DIM, keys), bf16)],
        ),
        out_shape=[
            jax.ShapeDtypeStruct(queries.shape, f32),
            jax.ShapeDtypeStruct(keys_values.shape, f32),
        ],
        compiler_params=pltpu.CompilerParams(vmem_limit_bytes=56 * 1024 * 1024),
        cost_estimate=pl.CostEstimate(
            flops=10 * HEADS * HEAD_DIM * rows * keys * 4,
            bytes_accessed=8 * 1024 * 1024,
            transcendentals=GROUP * rows * keys * 4,
        ),
    )(place, queries, out_grad, attended, log_total, keys_values)


def place_kernel(block_at, place_ref, shard_ref, *refs):
    refs[-1][...] = shard_ref[...].astype(f32)


def place_columns(whole, shape, shard, unit, place, block_at):
    rows, columns = shard.shape
    in_specs = [pl.BlockSpec((rows, unit), lambda g, place: (0, g))]
    operands = [place, shard]
    aliases = {}
    if whole is not None:
        in_specs.append(pl.BlockSpec(memory_space=pl.ANY))
        operands.append(whole)
        aliases = {2: 0}
    return pl.pallas_call(
        functools.partial(place_kernel, block_at),
        grid_spec=pltpu.PrefetchScalarGridSpec(
            num_scalar_prefetch=1,
            grid=(columns // unit,),
            in_specs=in_specs,
            out_specs=pl.BlockSpec((rows, unit), lambda g, place: (0, block_at(g, place))),
        ),
        out_shape=jax.ShapeDtypeStruct(shape, f32),
        input_output_aliases=aliases,
        cost_estimate=pl.CostEstimate(
            flops=0, bytes_accessed=6 * rows * columns, transcendentals=0
        ),
    )(*operands)


def body(
    inputs,
    attention_gain,
    qkv_weight,
    query_gain,
    key_gain,
    out_weight,
    mlp_gain,
    gate_up_weight,
    down_weight,
    cotangent,
):
    rows, width = inputs.shape
    fsdp_count = lax.axis_size("fsdp")
    cell_count = lax.axis_size("ctx") // CELL
    pair = 2 if fsdp_count % 2 == 0 else 1
    pair_count = fsdp_count // pair
    fsdp_here = lax.axis_index("fsdp")
    ctx_here = lax.axis_index("ctx")
    head = ctx_here % CELL
    cell = ctx_here // CELL
    in_pair = fsdp_here % pair
    pair_here = fsdp_here // pair
    weight_rows = qkv_weight.shape[0]
    query_width = HEADS * HEAD_DIM
    key_width = KV_HEADS * HEAD_DIM
    hidden_width = gate_up_weight.shape[1] // 2
    unit = hidden_width // (fsdp_count * CELL)
    place = jnp.stack([fsdp_here, cell]).astype(jnp.int32)

    def block(values, index, size, axis=0):
        return lax.dynamic_slice_in_dim(values, index * size, size, axis)

    def put(whole, part, index, axis=0):
        return lax.dynamic_update_slice_in_dim(whole, part, index * part.shape[axis], axis)

    def peer(distance):
        return jnp.bitwise_xor(head, distance)

    def cell_rows(shards):
        whole = blank((CELL * shards[0].shape[0],) + shards[0].shape[1:], shards[0].dtype)
        for distance, shard in enumerate(shards):
            whole = put(whole, shard, peer(distance))
        return whole

    def cell_pieces(values, axis=0):
        size = values.shape[axis] // CELL
        return [block(values, peer(distance), size, axis) for distance in range(CELL)]

    def fsdp_gather(shard):
        whole = blank((fsdp_count * shard.shape[0],) + shard.shape[1:], shard.dtype)
        whole = put(whole, shard, fsdp_here)
        for step in range(1, fsdp_count):
            whole = put(whole, fsdp_send(shard, step), (fsdp_here - step) % fsdp_count)
        return whole

    def cell_sum(values):
        total = values.astype(f32)
        for step in range(1, cell_count):
            total = total + cell_send(values.astype(bf16), step).astype(f32)
        return total

    def fsdp_reduce(values, size):
        total = block(values, fsdp_here, size).astype(f32)
        for step in range(1, fsdp_count):
            piece = block(values, (fsdp_here + step) % fsdp_count, size).astype(bf16)
            total = total + fsdp_send(piece, step).astype(f32)
        return cell_sum(total)

    def cell_turn(values, split_axis, join_axis):
        groups = None
        if cell_count > 1:
            groups = [[c * CELL + i for i in range(CELL)] for c in range(cell_count)]
        return lax.all_to_all(
            values, "ctx", split_axis, join_axis, axis_index_groups=groups, tiled=True
        )

    blocks_here = cell * CELL + jnp.arange(CELL, dtype=jnp.int32)
    positions = (
        ((blocks_here * fsdp_count + fsdp_here) * rows)[:, None]
        + jnp.arange(rows, dtype=jnp.int32)[None, :]
    ).reshape(-1)
    cell_tokens = CELL * rows
    half_dim = HEAD_DIM // 2
    frequency = theta ** (-jnp.arange(half_dim, dtype=f32) * 2.0 / HEAD_DIM)
    angles = positions.astype(f32)[:, None] * frequency[None, :]
    cosine = jnp.cos(angles)[:, None, :]
    sine = jnp.sin(angles)[:, None, :]

    def rotate(values):
        lower = values[..., :half_dim]
        upper = values[..., half_dim:]
        return jnp.concatenate(
            [lower * cosine - upper * sine, upper * cosine + lower * sine], axis=-1
        )

    def attention_inputs(values, q_gain, k_gain):
        queries = values[:, :GROUP_WIDTH].reshape(cell_tokens, GROUP, HEAD_DIM)
        key_rows = values[:, GROUP_WIDTH : GROUP_WIDTH + HEAD_DIM].reshape(
            cell_tokens, 1, HEAD_DIM
        )
        return (
            rotate(rms_scale(queries, q_gain)).reshape(cell_tokens, GROUP_WIDTH),
            rotate(rms_scale(key_rows, k_gain)).reshape(cell_tokens, HEAD_DIM),
            values[:, GROUP_WIDTH + HEAD_DIM :],
        )

    source = inputs.astype(f32)
    normed_attn_own = rms_scale(source, attention_gain).astype(bf16)
    normed_attn = cell_rows(gather_cell(normed_attn_own))
    qkv_columns = fsdp_gather(
        jnp.concatenate(
            [
                block(qkv_weight[:, :query_width], head, GROUP_WIDTH, 1),
                block(qkv_weight[:, query_width : query_width + key_width], head, HEAD_DIM, 1),
                block(qkv_weight[:, query_width + key_width :], head, HEAD_DIM, 1),
            ],
            axis=1,
        )
    )
    out_columns = fsdp_gather(block(out_weight, head, width // CELL, 1))
    out_rows = cell_turn(out_columns, 0, 1)

    def owner_columns(owner):
        return jnp.concatenate(
            [
                lax.dynamic_slice_in_dim(
                    gate_up_weight,
                    side * hidden_width + ((p * pair + owner) * CELL + head) * unit,
                    unit,
                    1,
                )
                for side in range(2)
                for p in range(pair_count)
            ],
            axis=1,
        )

    unit_columns = [owner_columns((in_pair + j) % pair) for j in range(pair)]
    local_units = pair_count * unit
    gate_up_mine = blank((width, 2 * local_units), bf16)
    gate_up_mine = put(gate_up_mine, unit_columns[0], fsdp_here)
    for step in range(1, fsdp_count):
        gate_up_mine = put(
            gate_up_mine,
            fsdp_send(unit_columns[step % pair], step),
            (fsdp_here - step) % fsdp_count,
        )
    down_own = block(down_weight, head, unit)
    down_mine = put(blank((local_units, width), bf16), down_own, pair_here)
    for step in range(1, pair_count):
        down_mine = put(
            down_mine, fsdp_send(down_own, step * pair), (pair_here - step) % pair_count
        )

    qkv_rows = dot(normed_attn, qkv_columns)
    query_rot, key_rot, value_rows = attention_inputs(qkv_rows, query_gain, key_gain)
    query_low = query_rot.astype(bf16)
    kv_own = jnp.concatenate([key_rot, value_rows], axis=1).astype(bf16)
    kv_own = kv_own.reshape(CELL, 1, rows, 2 * HEAD_DIM)
    kv_cells = blank((CELL, fsdp_count, rows, 2 * HEAD_DIM), bf16)
    kv_cells = put(kv_cells, kv_own, fsdp_here, 1)
    for step in range(1, fsdp_count):
        kv_cells = put(
            kv_cells, fsdp_send(kv_own, step), (fsdp_here - step) % fsdp_count, 1
        )
    chunk = fsdp_count * rows
    kv_cells = kv_cells.reshape(CELL * chunk, 2 * HEAD_DIM)
    if cell_count > 1:
        kv_all = put(
            blank((cell_count * CELL * chunk, 2 * HEAD_DIM), bf16), kv_cells, cell
        )
        for step in range(1, cell_count):
            kv_all = put(kv_all, cell_send(kv_cells, step), (cell - step) % cell_count)
    else:
        kv_all = kv_cells
    attended, log_total = attention(place, query_low, kv_all, rows, chunk)
    attended_low = attended.astype(bf16)
    out_partial = dot(attended_low, out_rows).astype(bf16)
    hidden_mid = source + reduce_cell(cell_pieces(out_partial))
    normed_mlp_own = rms_scale(hidden_mid, mlp_gain).astype(bf16)

    def pair_parts(own):
        shards = [own] + [pair_send(own, -j, pair) for j in range(1, pair)]
        return [cell_rows(gather_cell(shard)) for shard in shards]

    def pair_reduce(partials):
        total = None
        for j in reversed(range(pair)):
            summed = reduce_cell(cell_pieces(partials[j]))
            if j:
                summed = pair_send(summed.astype(bf16), j, pair).astype(f32)
            total = summed if total is None else total + summed
        return total

    cotangent_parts = pair_parts(cotangent)
    normed_parts = pair_parts(normed_mlp_own)
    gate_weight = gate_up_mine[:, :local_units]
    up_weight = gate_up_mine[:, local_units:]
    branch_partials, grad_partials, active_parts, gate_grads = [], [], [], []
    for j in range(pair):
        gate = dot(normed_parts[j], gate_weight)
        up = dot(normed_parts[j], up_weight)
        logistic = jax.nn.sigmoid(gate)
        active_low = (gate * logistic * up).astype(bf16)
        act_grad = dot(cotangent_parts[j], down_mine, NT)
        gate_part = act_grad * up * (logistic * (1.0 + gate * (1.0 - logistic)))
        up_part = act_grad * (gate * logistic)
        gate_grad = jnp.concatenate([gate_part.astype(bf16), up_part.astype(bf16)], axis=1)
        grad_partials.append(dot(gate_grad, gate_up_mine, NT).astype(bf16))
        branch_partials.append(dot(active_low, down_mine).astype(bf16))
        active_parts.append(active_low)
        gate_grads.append(gate_grad)
    normed_grad = pair_reduce(grad_partials)
    mid_part, mlp_gain_grad = jax.vjp(rms_scale, hidden_mid, mlp_gain)[1](normed_grad)
    hidden_grad = cotangent.astype(f32) + mid_part
    branch_grad = cell_rows(gather_cell(hidden_grad.astype(bf16)))

    down_partial = sum(dot(active_parts[j], cotangent_parts[j], TN) for j in range(pair))
    gate_up_partial = sum(dot(normed_parts[j], gate_grads[j], TN) for j in range(pair))
    gate_up_partial = gate_up_partial.astype(bf16)

    out_grad = dot(branch_grad, out_rows, NT).astype(bf16)
    query_grad, kv_grad = attention_grad(
        place, query_low, out_grad, attended, log_total, kv_all, rows, chunk
    )
    kv_grad = kv_grad.astype(bf16)
    if cell_count > 1:
        kv_grad_cell = block(kv_grad, cell, CELL * chunk).astype(f32)
        for step in range(1, cell_count):
            piece = block(kv_grad, (cell + step) % cell_count, CELL * chunk)
            kv_grad_cell = kv_grad_cell + cell_send(piece, step).astype(f32)
        kv_grad = kv_grad_cell.astype(bf16)
    kv_grad = kv_grad.reshape(CELL, fsdp_count, rows, 2 * HEAD_DIM)
    kv_total = block(kv_grad, fsdp_here, 1, 1).astype(f32)
    for step in range(1, fsdp_count):
        piece = block(kv_grad, (fsdp_here + step) % fsdp_count, 1, 1)
        kv_total = kv_total + fsdp_send(piece, step).astype(f32)
    kv_total = kv_total.reshape(cell_tokens, 2 * HEAD_DIM)
    pull_back = jax.vjp(attention_inputs, qkv_rows, query_gain, key_gain)[1]
    qkv_grad, query_gain_grad, key_gain_grad = pull_back(
        (query_grad, kv_total[:, :HEAD_DIM], kv_total[:, HEAD_DIM:])
    )
    qkv_grad_low = qkv_grad.astype(bf16)
    attn_partial = dot(qkv_grad_low, qkv_columns, NT).astype(bf16)
    attn_normed_grad = reduce_cell(cell_pieces(attn_partial))
    source_part, attention_gain_grad = jax.vjp(rms_scale, source, attention_gain)[1](
        attn_normed_grad
    )
    grad_inputs = (hidden_grad + source_part).astype(bf16)
    gain_sums = lax.psum(
        (attention_gain_grad, query_gain_grad, key_gain_grad, mlp_gain_grad), ("ctx", "fsdp")
    )

    outputs = (hidden_mid + pair_reduce(branch_partials)).astype(bf16)

    down_total = block(down_partial, pair_here, unit)
    for step in range(1, pair_count):
        piece = block(down_partial, (pair_here + step) % pair_count, unit).astype(bf16)
        down_total = down_total + fsdp_send(piece, step * pair).astype(f32)
    down_total = cell_sum(down_total).astype(bf16)
    grad_down = blank((CELL * unit, width), f32)
    for distance, shard in enumerate(gather_cell(down_total)):
        grad_down = put(grad_down, shard.astype(f32), peer(distance))

    pair_rows = pair * weight_rows
    gate_up_total = block(gate_up_partial, pair_here, pair_rows).astype(f32)
    for step in range(1, pair_count):
        piece = block(gate_up_partial, (pair_here + step) % pair_count, pair_rows)
        gate_up_total = gate_up_total + fsdp_send(piece, step * pair).astype(f32)
    gate_up_total = cell_sum(gate_up_total).astype(bf16)
    grad_gate_up = None
    for j in range(pair):
        part = block(gate_up_total, (in_pair + j) % pair, weight_rows)
        if j:
            part = pair_send(part, j, pair)
        owner = (in_pair - j) % pair
        for distance, shard in enumerate(gather_cell(part)):
            grad_gate_up = place_columns(
                grad_gate_up,
                gate_up_weight.shape,
                shard,
                unit,
                jnp.stack([owner, peer(distance)]).astype(jnp.int32),
                lambda g, at: (
                    (g // pair_count) * (hidden_width // unit)
                    + ((g % pair_count) * pair + at[0]) * CELL
                    + at[1]
                ),
            )

    out_partial_grad = dot(attended_low, branch_grad, TN).astype(bf16)
    out_total = fsdp_reduce(cell_turn(out_partial_grad, 1, 0), weight_rows).astype(bf16)
    grad_out = blank((weight_rows, width), f32)
    for distance, shard in enumerate(gather_cell(out_total)):
        grad_out = put(grad_out, shard.astype(f32), peer(distance), 1)

    qkv_partial = dot(normed_attn, qkv_grad_low, TN).astype(bf16)
    qkv_total = fsdp_reduce(qkv_partial, weight_rows).astype(bf16)
    stacked = cell_rows([shard[None] for shard in gather_cell(qkv_total)])
    side = stacked.transpose(1, 0, 2)
    grad_qkv = jnp.concatenate(
        [
            side[:, :, :GROUP_WIDTH].reshape(weight_rows, query_width),
            side[:, :, GROUP_WIDTH : GROUP_WIDTH + HEAD_DIM].reshape(weight_rows, key_width),
            side[:, :, GROUP_WIDTH + HEAD_DIM :].reshape(weight_rows, key_width),
        ],
        axis=1,
    ).astype(f32)

    return (
        outputs,
        grad_inputs,
        gain_sums[0],
        grad_qkv,
        gain_sums[1],
        gain_sums[2],
        grad_out,
        gain_sums[3],
        grad_gate_up,
        grad_down,
    )


def solution(mesh):
    return jax.shard_map(
        body,
        mesh=mesh,
        in_specs=(
            P(("ctx", "fsdp"), None),
            P(),
            P("fsdp", None),
            P(),
            P(),
            P("fsdp", None),
            P(),
            P("fsdp", None),
            P("fsdp", None),
            P(("ctx", "fsdp"), None),
        ),
        out_specs=(
            P(("ctx", "fsdp"), None),
            P(("ctx", "fsdp"), None),
            P(),
            P("fsdp", None),
            P(),
            P(),
            P("fsdp", None),
            P(),
            P("fsdp", None),
            P("fsdp", None),
        ),
        check_vma=False,
    )
```

```python
import functools

import jax
import jax.numpy as jnp
from jax import lax
from jax.experimental import pallas as pl
from jax.experimental.pallas import tpu as pltpu
from jax.sharding import PartitionSpec as P

HEADS = 32
KV_HEADS = 8
HEAD_DIM = 64
GROUP = HEADS // KV_HEADS
GROUP_WIDTH = GROUP * HEAD_DIM

epsilon = 1e-05
theta = 1000000.0
score_scale = HEAD_DIM ** (-0.5)

f32 = jnp.float32
bf16 = jnp.bfloat16

CELL = KV_HEADS

NN = (((1,), (0,)), ((), ()))
NT = (((1,), (1,)), ((), ()))
TN = (((0,), (0,)), ((), ()))


def dot(left, right, dims=NN):
    return lax.dot_general(left, right, dims, preferred_element_type=f32)


def rms_scale(values, gain):
    return values * lax.rsqrt(jnp.mean(values * values, axis=-1, keepdims=True) + epsilon) * gain


def xor_send(values, distance):
    count = lax.axis_size("ctx")
    return lax.ppermute(values, "ctx", [(i, i ^ distance) for i in range(count)])


def cell_send(values, step):
    count = lax.axis_size("ctx")
    return lax.ppermute(values, "ctx", [(i, (i + step * CELL) % count) for i in range(count)])


def fsdp_send(values, step):
    count = lax.axis_size("fsdp")
    return lax.ppermute(values, "fsdp", [(i, (i + step) % count) for i in range(count)])


def pair_send(values, step, pair):
    count = lax.axis_size("fsdp")
    return lax.ppermute(
        values, "fsdp", [(i, i // pair * pair + (i % pair + step) % pair) for i in range(count)]
    )


def fsdp_relay(shard):
    count = lax.axis_size("fsdp")
    return [shard] + [fsdp_send(shard, step) for step in range(1, count)]


def fsdp_collect(piece_for):
    count = lax.axis_size("fsdp")
    total = piece_for(0).astype(f32)
    for step in range(1, count):
        total = total + fsdp_send(piece_for(step), step).astype(f32)
    return total


def round_send(values, odd_round):
    count = lax.axis_size("ctx")
    pairs = []
    for i in range(count):
        pairs.append((i, i ^ (2 if i % 2 == odd_round else 4)))
    return lax.ppermute(values, "ctx", pairs)


def add_low(left, right):
    return (left.astype(f32) + right.astype(f32)).astype(bf16)


def after(values, event):
    return lax.optimization_barrier((values, event))[0]


class Steps:
    def __init__(self):
        self.event = None
        self.jobs = []

    def begin(self, values):
        return values if self.event is None else after(values, self.event)

    def run(self, parts, spare=0):
        jobs, self.jobs = self.jobs[:spare], self.jobs[spare:]
        results = [function(self.begin(values)) for function, values in parts]
        results += [start(self.begin) for start, _ in jobs]
        results = lax.optimization_barrier(results)
        for (_, finish), value in zip(jobs, results[len(parts) :]):
            finish(value)
        self.event = results[0]
        return results[: len(parts)]

    def drain(self, done):
        while self.jobs and not done():
            self.run([(lambda v: v, self.event)], 2)


def first_round(values):
    return round_send(values, 0)


def second_round(values):
    return round_send(values, 1)


def twin_send(values):
    return xor_send(values, 1)


def rows_joined(*parts):
    return jnp.concatenate(parts, axis=0)


def gather_cell(shard):
    two = rows_joined(shard, first_round(shard))
    mine = rows_joined(two, second_round(two))
    return mine, twin_send(mine)


def reduce_first(mine, from_twin):
    half = mine.shape[0] // 2
    total = add_low(mine, from_twin)
    return total[:half], total[half:]


def reduce_second(kept, received):
    half = kept.shape[0] // 2
    total = add_low(kept, received)
    return total[:half], total[half:]


def reduce_cell(mine, other):
    kept, sent = reduce_first(mine, twin_send(other))
    kept, sent = reduce_second(kept, second_round(sent))
    return kept.astype(f32) + first_round(sent).astype(f32)


def sum_everywhere(values):
    for axis in ("ctx", "fsdp"):
        count = lax.axis_size(axis)
        if count & (count - 1):
            values = lax.psum(values, axis)
            continue
        distance = 1
        while distance < count:
            values = values + lax.ppermute(
                values, axis, [(i, i ^ distance) for i in range(count)]
            )
            distance *= 2
    return values


def blank(shape, dtype):
    return pl.pallas_call(
        lambda ref: None,
        out_specs=pl.BlockSpec(memory_space=pl.ANY),
        out_shape=jax.ShapeDtypeStruct(shape, dtype),
        cost_estimate=pl.CostEstimate(flops=0, bytes_accessed=0, transcendentals=0),
    )()


def cost(flops, moved, transcendentals=0):
    return pl.CostEstimate(
        flops=int(flops), bytes_accessed=int(moved), transcendentals=int(transcendentals)
    )


def own(i, place):
    slot = i % 4
    other = i // 4
    swapped = (place[2] + other) % 2
    return slot // 2 * (4 - 2 * swapped) + slot % 2 * (2 + 2 * swapped) + other


def token_block(i, place):
    return jnp.bitwise_xor(own(i, place), place[2])


def even_block(i):
    return jnp.minimum(i, 3)


def odd_block(i):
    return jnp.maximum(i - 4, 0)


def swap_halves(values):
    lane = lax.broadcasted_iota(jnp.int32, values.shape, 1) % HEAD_DIM
    return jnp.where(
        lane < HEAD_DIM // 2,
        pltpu.roll(values, values.shape[1] - HEAD_DIM // 2, 1),
        pltpu.roll(values, HEAD_DIM // 2, 1),
    )


def head_mean(values):
    first = lax.broadcasted_iota(jnp.int32, values.shape, 1) < HEAD_DIM
    low = jnp.sum(jnp.where(first, values, 0.0), axis=1, keepdims=True)
    high = jnp.sum(jnp.where(first, 0.0, values), axis=1, keepdims=True)
    return jnp.where(first, low, high) * (1.0 / HEAD_DIM)


def project_kernel(fsdp_count, place_ref, even_ref, odd_ref, angle_ref, gain_ref, *refs):
    weight_refs, (rows_ref, q_ref, kv_ref) = refs[:fsdp_count], refs[fsdp_count:]
    depth = weight_refs[0].shape[0]

    def project(left_ref):
        total = None
        for step in range(fsdp_count):
            owner = lax.rem(place_ref[0] - step + fsdp_count, fsdp_count)
            left = left_ref[:, pl.ds(pl.multiple_of(owner * depth, depth), depth)]
            term = dot(left, weight_refs[step][...])
            total = term if total is None else total + term
        rows_ref[...] = total

    @pl.when(pl.program_id(0) < 4)
    def _():
        project(even_ref)

    @pl.when(pl.program_id(0) >= 4)
    def _():
        project(odd_ref)

    cosine = angle_ref[:, : 2 * HEAD_DIM]
    sine = angle_ref[:, 2 * HEAD_DIM :]
    wide = 2 * HEAD_DIM
    for group in range(GROUP_WIDTH // wide + 1):
        values = rows_ref[:, group * wide : (group + 1) * wide]
        last = group == GROUP_WIDTH // wide
        normed = values * lax.rsqrt(head_mean(values * values) + epsilon)
        normed = normed * gain_ref[int(last) : int(last) + 1, :]
        turned = normed * cosine + swap_halves(normed) * sine
        if last:
            lane = lax.broadcasted_iota(jnp.int32, values.shape, 1)
            kv_ref[...] = jnp.where(lane < HEAD_DIM, turned, values).astype(bf16)
        else:
            q_ref[:, group * wide : (group + 1) * wide] = turned.astype(bf16)


def project(place, even, odd, angles, gains, weights, rows):
    count = CELL
    fsdp_count = len(weights)
    width = even.shape[1]
    columns = weights[0].shape[1]
    return pl.pallas_call(
        functools.partial(project_kernel, fsdp_count),
        grid_spec=pltpu.PrefetchScalarGridSpec(
            num_scalar_prefetch=1,
            grid=(count,),
            in_specs=[
                pl.BlockSpec((rows, width), lambda i, place: (even_block(i), 0)),
                pl.BlockSpec((rows, width), lambda i, place: (odd_block(i), 0)),
                pl.BlockSpec((rows, 4 * HEAD_DIM), lambda i, place: (token_block(i, place), 0)),
                pl.BlockSpec((8, 2 * HEAD_DIM), lambda i, place: (0, 0)),
            ]
            + [pl.BlockSpec(w.shape, lambda i, place: (0, 0)) for w in weights],
            out_specs=[
                pl.BlockSpec((rows, columns), lambda i, place: (token_block(i, place), 0)),
                pl.BlockSpec((rows, GROUP_WIDTH), lambda i, place: (token_block(i, place), 0)),
                pl.BlockSpec((rows, 2 * HEAD_DIM), lambda i, place: (token_block(i, place), 0)),
            ],
        ),
        out_shape=[
            jax.ShapeDtypeStruct((count * rows, columns), f32),
            jax.ShapeDtypeStruct((count * rows, GROUP_WIDTH), bf16),
            jax.ShapeDtypeStruct((count * rows, 2 * HEAD_DIM), bf16),
        ],
        compiler_params=pltpu.CompilerParams(vmem_limit_bytes=40 * 1024 * 1024),
        cost_estimate=cost(2 * count * rows * width * columns, 8e6),
    )(place, even, odd, angles, gains, *weights)


def project_grad_kernel(
    fsdp_count,
    place_ref,
    even_ref,
    odd_ref,
    angle_ref,
    gain_ref,
    rows_ref,
    q_even_ref,
    q_odd_ref,
    kv_ref,
    *refs,
):
    weight_refs = refs[:fsdp_count]
    (grad_even_ref, grad_odd_ref, part_even_ref, part_odd_ref, head_gain_ref, gain_grad_ref) = refs[
        fsdp_count:
    ]
    depth = weight_refs[0].shape[0]
    step_here = pl.program_id(0)

    @pl.when(step_here == 0)
    def _():
        head_gain_ref[...] = jnp.zeros_like(head_gain_ref)
        gain_grad_ref[...] = jnp.zeros_like(gain_grad_ref)

    cosine = angle_ref[:, : 2 * HEAD_DIM]
    sine = angle_ref[:, 2 * HEAD_DIM :]
    wide = 2 * HEAD_DIM
    pieces = []
    for group in range(GROUP_WIDTH // wide + 1):
        last = group == GROUP_WIDTH // wide
        values = rows_ref[:, group * wide : (group + 1) * wide]
        at = pl.ds(group * wide, wide)
        if last:
            grad = kv_ref[...]
        else:
            grad = jnp.where(step_here < 4, q_even_ref[:, at], q_odd_ref[:, at])
        scale = lax.rsqrt(head_mean(values * values) + epsilon)
        gain = gain_ref[int(last) : int(last) + 1, :]
        unturned = grad * cosine + swap_halves(grad * sine)
        head_gain_ref[int(last) : int(last) + 1, :] += jnp.sum(
            unturned * values * scale, axis=0, keepdims=True
        )
        scaled = unturned * gain
        piece = scale * scaled - values * (scale * scale * scale) * head_mean(scaled * values)
        if last:
            lane = lax.broadcasted_iota(jnp.int32, values.shape, 1)
            piece = jnp.where(lane < HEAD_DIM, piece, grad)
        pieces.append(piece.astype(bf16))
    low = jnp.concatenate(pieces, axis=1)

    def finish(normed_ref, grad_out_ref, part_ref):
        grad_out_ref[...] = low
        for step in range(fsdp_count):
            owner = lax.rem(place_ref[0] - step + fsdp_count, fsdp_count)
            at = pl.ds(pl.multiple_of(owner * depth, depth), depth)
            part = dot(low, weight_refs[step][...], NT)
            part_ref[:, at] = part.astype(bf16)
            gain_grad_ref[0:1, at] += jnp.sum(
                part * normed_ref[:, at].astype(f32), axis=0, keepdims=True
            )

    @pl.when(step_here < 4)
    def _():
        finish(even_ref, grad_even_ref, part_even_ref)

    @pl.when(step_here >= 4)
    def _():
        finish(odd_ref, grad_odd_ref, part_odd_ref)


def project_grad(place, even, odd, angles, gains, qkv_rows, query_grad, kv_grad, weights, rows):
    count = CELL
    fsdp_count = len(weights)
    width = even.shape[1]
    columns = weights[0].shape[1]

    def by_token(size):
        return pl.BlockSpec((rows, size), lambda i, place: (token_block(i, place), 0))

    def halves(size):
        return [
            pl.BlockSpec((rows, size), lambda i, place: (even_block(i), 0)),
            pl.BlockSpec((rows, size), lambda i, place: (odd_block(i), 0)),
        ]

    return pl.pallas_call(
        functools.partial(project_grad_kernel, fsdp_count),
        grid_spec=pltpu.PrefetchScalarGridSpec(
            num_scalar_prefetch=1,
            grid=(count,),
            in_specs=halves(width)
            + [
                by_token(4 * HEAD_DIM),
                pl.BlockSpec((8, 2 * HEAD_DIM), lambda i, place: (0, 0)),
                by_token(columns),
                *halves(GROUP_WIDTH),
                by_token(2 * HEAD_DIM),
            ]
            + [pl.BlockSpec(w.shape, lambda i, place: (0, 0)) for w in weights],
            out_specs=halves(columns)
            + halves(width)
            + [
                pl.BlockSpec((8, 2 * HEAD_DIM), lambda i, place: (0, 0)),
                pl.BlockSpec((8, width), lambda i, place: (0, 0)),
            ],
        ),
        out_shape=[
            jax.ShapeDtypeStruct((4 * rows, columns), bf16),
            jax.ShapeDtypeStruct((4 * rows, columns), bf16),
            jax.ShapeDtypeStruct((4 * rows, width), bf16),
            jax.ShapeDtypeStruct((4 * rows, width), bf16),
            jax.ShapeDtypeStruct((8, 2 * HEAD_DIM), f32),
            jax.ShapeDtypeStruct((8, width), f32),
        ],
        compiler_params=pltpu.CompilerParams(vmem_limit_bytes=40 * 1024 * 1024),
        cost_estimate=cost(2 * count * rows * width * columns, 12e6),
    )(place, even, odd, angles, gains, qkv_rows, *query_grad, kv_grad, *weights)


def stack_heads(block):
    return jnp.concatenate(
        [block[:, i * HEAD_DIM : (i + 1) * HEAD_DIM] for i in range(GROUP)], axis=0
    )


def unstack_heads(turned, rows):
    return jnp.concatenate([turned[:, i * rows : (i + 1) * rows].T for i in range(GROUP)], axis=1)


def fill_turned(place_ref, kv_ref, turned_ref, chunk):
    @pl.when(pl.program_id(0) == 0)
    def _():
        def turn(n, _):
            start = pl.multiple_of(n * chunk, chunk)
            turned_ref[:, pl.ds(start, chunk)] = kv_ref[pl.ds(start, chunk), :].T
            return 0

        lax.fori_loop(0, (place_ref[1] + 1) * CELL, turn, 0)


def visible_keys(place_ref, chunk, rows):
    key_at = lax.broadcasted_iota(jnp.int32, (chunk, GROUP * rows), 0)
    row_at = lax.broadcasted_iota(jnp.int32, (chunk, GROUP * rows), 1) % rows
    return key_at <= row_at + place_ref[0] * rows


def attention_kernel(
    chunk, place_ref, q_ref, kv_ref, even_ref, odd_ref, log_ref, turned_ref
):
    rows = q_ref.shape[0]
    fill_turned(place_ref, kv_ref, turned_ref, chunk)
    queries = stack_heads(q_ref[...].astype(f32) * score_scale).astype(bf16)
    queries = jnp.concatenate([queries, jnp.zeros_like(queries)], axis=1)

    def step(n, running, masked):
        total, summed = running
        start = pl.multiple_of(n * chunk, chunk)
        weights = jnp.exp(dot(kv_ref[pl.ds(start, chunk), :], queries, NT))
        if masked:
            weights = jnp.where(visible_keys(place_ref, chunk, rows), weights, 0.0)
        return (
            total + jnp.sum(weights, axis=0, keepdims=True),
            summed + dot(turned_ref[:, pl.ds(start, chunk)], weights.astype(bf16)),
        )

    last = place_ref[1] * CELL + token_block(pl.program_id(0), place_ref)
    running = (
        jnp.zeros((1, GROUP * rows), f32),
        jnp.zeros((2 * HEAD_DIM, GROUP * rows), f32),
    )
    running = lax.fori_loop(0, last, lambda n, r: step(n, r, False), running)
    total, summed = step(last, running, True)
    result = unstack_heads(summed[HEAD_DIM:] / total, rows).astype(bf16)

    @pl.when(pl.program_id(0) < 4)
    def _():
        even_ref[...] = result

    @pl.when(pl.program_id(0) >= 4)
    def _():
        odd_ref[...] = result

    log_ref[...] = jnp.log(total)[None]


def attention(place, queries, keys_values, rows, chunk):
    count = queries.shape[0] // rows
    keys = keys_values.shape[0]
    half = jax.ShapeDtypeStruct((4 * rows, GROUP_WIDTH), bf16)
    return pl.pallas_call(
        functools.partial(attention_kernel, chunk),
        grid_spec=pltpu.PrefetchScalarGridSpec(
            num_scalar_prefetch=1,
            grid=(count,),
            in_specs=[
                pl.BlockSpec((rows, GROUP_WIDTH), lambda i, place: (token_block(i, place), 0)),
                pl.BlockSpec((keys, 2 * HEAD_DIM), lambda i, place: (0, 0)),
            ],
            out_specs=[
                pl.BlockSpec((rows, GROUP_WIDTH), lambda i, place: (even_block(i), 0)),
                pl.BlockSpec((rows, GROUP_WIDTH), lambda i, place: (odd_block(i), 0)),
                pl.BlockSpec((1, 1, GROUP * rows), lambda i, place: (i, 0, 0)),
            ],
            scratch_shapes=[pltpu.VMEM((2 * HEAD_DIM, keys), bf16)],
        ),
        out_shape=[half, half, jax.ShapeDtypeStruct((count, 1, GROUP * rows), f32)],
        compiler_params=pltpu.CompilerParams(vmem_limit_bytes=40 * 1024 * 1024),
        cost_estimate=cost(16e9, 8e6, 1e7),
    )(place, queries, keys_values)


def attention_grad_kernel(
    chunk,
    other,
    place_ref,
    q_ref,
    branch_ref,
    out_ref,
    log_ref,
    weight_ref,
    kv_ref,
    *refs,
):
    q_grad_ref, kv_grad_ref, turned_ref = refs[-3:]
    rows = q_ref.shape[0]
    fill_turned(place_ref, kv_ref, turned_ref, chunk)

    @pl.when(pl.program_id(0) == 0)
    def _():
        kv_grad_ref[...] = refs[0][...] if other else jnp.zeros_like(kv_grad_ref)

    queries = stack_heads(q_ref[...].astype(f32) * score_scale).astype(bf16)
    queries = jnp.concatenate([queries, jnp.zeros_like(queries)], axis=1)
    out_grad = dot(branch_ref[...], weight_ref[...], NT).astype(bf16)
    grads = stack_heads(out_grad)
    attended = stack_heads(out_ref[...]).astype(f32)
    row_delta = jnp.sum((grads.astype(f32) * attended).T, axis=0, keepdims=True)
    grads = jnp.concatenate([jnp.zeros_like(grads), grads], axis=1)
    log_total = log_ref[0]

    def step(n, summed, masked):
        start = pl.multiple_of(n * chunk, chunk)
        block = kv_ref[pl.ds(start, chunk), :]
        weights = jnp.exp(dot(block, queries, NT) - log_total)
        if masked:
            weights = jnp.where(visible_keys(place_ref, chunk, rows), weights, 0.0)
        score_grad = (weights * (dot(block, grads, NT) - row_delta)).astype(bf16)
        kv_grad_ref[pl.ds(start, chunk), :] += dot(score_grad, queries) + dot(
            weights.astype(bf16), grads
        )
        return summed + dot(turned_ref[:, pl.ds(start, chunk)], score_grad)

    last = place_ref[1] * CELL + token_block(pl.program_id(0) + 4 * other, place_ref)
    summed = jnp.zeros((2 * HEAD_DIM, GROUP * rows), f32)
    summed = lax.fori_loop(0, last, lambda n, r: step(n, r, False), summed)
    summed = step(last, summed, True)
    q_grad_ref[...] = unstack_heads(summed[:HEAD_DIM] * score_scale, rows)


def attention_grad(
    place, queries, branch, attended, log_total, weight, keys_values, rows, chunk, other, kv_grad=None
):
    keys = keys_values.shape[0]
    width = weight.shape[1]
    whole_spec = pl.BlockSpec((keys, 2 * HEAD_DIM), lambda i, place: (0, 0))
    added = [] if kv_grad is None else [kv_grad]
    return pl.pallas_call(
        functools.partial(attention_grad_kernel, chunk, other),
        grid_spec=pltpu.PrefetchScalarGridSpec(
            num_scalar_prefetch=1,
            grid=(4,),
            in_specs=[
                pl.BlockSpec(
                    (rows, GROUP_WIDTH), lambda i, place: (token_block(i + 4 * other, place), 0)
                ),
                pl.BlockSpec((rows, width), lambda i, place: (i, 0)),
                pl.BlockSpec((rows, GROUP_WIDTH), lambda i, place: (i, 0)),
                pl.BlockSpec((1, 1, GROUP * rows), lambda i, place: (i + 4 * other, 0, 0)),
                pl.BlockSpec(weight.shape, lambda i, place: (0, 0)),
                whole_spec,
            ]
            + [whole_spec] * len(added),
            out_specs=[
                pl.BlockSpec((rows, GROUP_WIDTH), lambda i, place: (i, 0)),
                whole_spec,
            ],
            scratch_shapes=[pltpu.VMEM((2 * HEAD_DIM, keys), bf16)],
        ),
        out_shape=[
            jax.ShapeDtypeStruct((4 * rows, GROUP_WIDTH), f32),
            jax.ShapeDtypeStruct(keys_values.shape, f32),
        ],
        compiler_params=pltpu.CompilerParams(vmem_limit_bytes=48 * 1024 * 1024),
        cost_estimate=cost(18e9, 12e6, 5e6),
    )(place, queries, branch, attended, log_total, weight, keys_values, *added)


def feed_kernel(
    normed_ref, outer_ref, weight_ref, down_ref, active_ref, gate_grad_ref, part_ref, branch_ref
):
    units = active_ref.shape[1]
    both = dot(normed_ref[...], weight_ref[...])
    gate = both[:, :units]
    up = both[:, units:]
    act_grad = dot(outer_ref[...], down_ref[...], NT)
    logistic = 1.0 / (1.0 + jnp.exp(-gate))
    silu = gate * logistic
    active_ref[...] = (silu * up).astype(bf16)
    gate_part = act_grad * up * (logistic * (1.0 + gate * (1.0 - logistic)))
    gate_grad_ref[:, :units] = gate_part.astype(bf16)
    gate_grad_ref[:, units:] = (act_grad * silu).astype(bf16)
    part_ref[...] = dot(gate_grad_ref[...], weight_ref[...], NT).astype(bf16)
    branch_ref[...] = dot(active_ref[...], down_ref[...]).astype(bf16)


def feed(normed, outer, weight, down):
    tokens, width = normed.shape
    columns = weight.shape[1]
    rows = 256 if tokens % 256 == 0 else tokens

    def by_row(size):
        return pl.BlockSpec((rows, size), lambda i: (i, 0))

    def low(size):
        return jax.ShapeDtypeStruct((tokens, size), bf16)

    return pl.pallas_call(
        feed_kernel,
        grid=(tokens // rows,),
        in_specs=[
            by_row(width),
            by_row(width),
            pl.BlockSpec(weight.shape, lambda i: (0, 0)),
            pl.BlockSpec(down.shape, lambda i: (0, 0)),
        ],
        out_specs=[by_row(columns // 2), by_row(columns), by_row(width), by_row(width)],
        out_shape=[low(columns // 2), low(columns), low(width), low(width)],
        compiler_params=pltpu.CompilerParams(vmem_limit_bytes=48 * 1024 * 1024),
        cost_estimate=cost(6 * tokens * width * columns, 16e6, tokens * columns),
    )(normed, outer, weight, down)


def weight_grad_kernel(count, place_ref, *refs):
    total = None
    for left_ref, right_ref in zip(refs[:count], refs[count : 2 * count]):
        term = dot(left_ref[...], right_ref[...], TN)
        total = term if total is None else total + term
    refs[-1][...] = total.astype(bf16)


def weight_grad(lefts, rights, first, size, column, columns):
    tokens = lefts[0].shape[0]
    tile = min(512, size)
    tiles = size // tile
    place = jnp.stack([first * tiles]).astype(jnp.int32)
    return pl.pallas_call(
        functools.partial(weight_grad_kernel, len(lefts)),
        grid_spec=pltpu.PrefetchScalarGridSpec(
            num_scalar_prefetch=1,
            grid=(tiles,),
            in_specs=[pl.BlockSpec((tokens, tile), lambda i, at: (0, at[0] + i))] * len(lefts)
            + [pl.BlockSpec((tokens, columns), lambda i, at: (0, column))] * len(rights),
            out_specs=pl.BlockSpec((tile, columns), lambda i, at: (i, 0)),
        ),
        out_shape=jax.ShapeDtypeStruct((size, columns), bf16),
        compiler_params=pltpu.CompilerParams(vmem_limit_bytes=48 * 1024 * 1024),
        cost_estimate=cost(2 * len(lefts) * tokens * size * columns, 12e6),
    )(place, *lefts, *rights)


def place_kernel(place_ref, shard_ref, *refs):
    refs[-1][...] = shard_ref[...].astype(f32)


def place_blocks(whole, shape, source, block, grid, place, from_block, to_block):
    in_specs = [pl.BlockSpec(block, from_block)]
    operands = [place, source]
    aliases = {}
    if whole is not None:
        in_specs.append(pl.BlockSpec(memory_space=pl.ANY))
        operands.append(whole)
        aliases = {2: 0}
    return pl.pallas_call(
        place_kernel,
        grid_spec=pltpu.PrefetchScalarGridSpec(
            num_scalar_prefetch=1,
            grid=grid,
            in_specs=in_specs,
            out_specs=pl.BlockSpec(block, to_block),
        ),
        out_shape=jax.ShapeDtypeStruct(shape, f32),
        input_output_aliases=aliases,
        compiler_params=pltpu.CompilerParams(vmem_limit_bytes=24 * 1024 * 1024),
        cost_estimate=cost(0, 6 * source.size),
    )(*operands)


def place_columns(halves, unit, place):
    whole = None
    rows = halves[0].shape[0] // 4
    for odd, half in enumerate(halves):
        whole = place_blocks(
            whole,
            (rows, CELL * unit),
            half,
            (rows, unit),
            (4,),
            place,
            lambda i, at: (i, 0),
            lambda i, at, odd=odd: (0, token_block(4 * odd + i, at)),
        )
    return whole


def place_rows(halves, place):
    whole = None
    rows, columns = halves[0].shape[0] // 4, halves[0].shape[1]
    for odd, half in enumerate(halves):
        whole = place_blocks(
            whole,
            (CELL * rows, columns),
            half,
            (rows, columns),
            (4,),
            place,
            lambda i, at: (i, 0),
            lambda i, at, odd=odd: (token_block(4 * odd + i, at), 0),
        )
    return whole


def place_heads_kernel(place_ref, even_ref, odd_ref, out_ref):
    query_width = HEADS * HEAD_DIM
    key_width = KV_HEADS * HEAD_DIM
    even = even_ref[...].astype(f32)
    odd = odd_ref[...].astype(f32)
    first = lax.rem(place_ref[2], 2) == 0
    low = jnp.where(first, even, odd)
    high = jnp.where(first, odd, even)
    twins = token_block(pl.program_id(0), place_ref) // 2

    def at(start, size):
        return pl.ds(pl.multiple_of(start + twins * size, 128), size)

    out_ref[:, at(0, 2 * GROUP_WIDTH)] = jnp.concatenate(
        [low[:, :GROUP_WIDTH], high[:, :GROUP_WIDTH]], axis=1
    )
    middle = GROUP_WIDTH + HEAD_DIM
    out_ref[:, at(query_width, 2 * HEAD_DIM)] = jnp.concatenate(
        [low[:, GROUP_WIDTH:middle], high[:, GROUP_WIDTH:middle]], axis=1
    )
    out_ref[:, at(query_width + key_width, 2 * HEAD_DIM)] = jnp.concatenate(
        [low[:, middle:], high[:, middle:]], axis=1
    )


def place_heads(halves, place):
    rows, columns = halves[0].shape[0] // 4, halves[0].shape[1]
    shape = (rows, CELL * columns)
    return pl.pallas_call(
        place_heads_kernel,
        grid_spec=pltpu.PrefetchScalarGridSpec(
            num_scalar_prefetch=1,
            grid=(4,),
            in_specs=[
                pl.BlockSpec((rows, columns), lambda i, at: (i, 0)),
                pl.BlockSpec((rows, columns), lambda i, at: (i % 2 * 2 + i // 2, 0)),
            ],
            out_specs=pl.BlockSpec(shape, lambda i, at: (0, 0)),
        ),
        out_shape=jax.ShapeDtypeStruct(shape, f32),
        compiler_params=pltpu.CompilerParams(vmem_limit_bytes=32 * 1024 * 1024),
        cost_estimate=cost(0, 6 * rows * CELL * columns),
    )(place, *halves)


def body(
    inputs,
    attention_gain,
    qkv_weight,
    query_gain,
    key_gain,
    out_weight,
    mlp_gain,
    gate_up_weight,
    down_weight,
    cotangent,
):
    rows, width = inputs.shape
    fsdp_count = lax.axis_size("fsdp")
    cell_count = lax.axis_size("ctx") // CELL
    pair = 2 if fsdp_count % 2 == 0 else 1
    pair_count = fsdp_count // pair
    fsdp_here = lax.axis_index("fsdp")
    ctx_here = lax.axis_index("ctx")
    head = ctx_here % CELL
    cell = ctx_here // CELL
    in_pair = fsdp_here % pair
    pair_here = fsdp_here // pair
    weight_rows = qkv_weight.shape[0]
    query_width = HEADS * HEAD_DIM
    key_width = KV_HEADS * HEAD_DIM
    hidden_width = gate_up_weight.shape[1] // 2
    unit = hidden_width // (fsdp_count * CELL)
    place = jnp.stack([fsdp_here, cell, head, in_pair]).astype(jnp.int32)

    def block(values, index, size, axis=0):
        return lax.dynamic_slice_in_dim(values, index * size, size, axis)

    def put(whole, part, index, axis=0):
        return lax.dynamic_update_slice_in_dim(whole, part, index * part.shape[axis], axis)

    def cell_sum(values):
        total = values.astype(f32)
        for step in range(1, cell_count):
            total = total + cell_send(values.astype(bf16), step).astype(f32)
        return total

    def cell_turn(values, split_axis, join_axis):
        groups = None
        if cell_count > 1:
            groups = [[c * CELL + i for i in range(CELL)] for c in range(cell_count)]
        return lax.all_to_all(
            values, "ctx", split_axis, join_axis, axis_index_groups=groups, tiled=True
        )

    blocks_here = cell * CELL + jnp.arange(CELL, dtype=jnp.int32)
    positions = (
        ((blocks_here * fsdp_count + fsdp_here) * rows)[:, None]
        + jnp.arange(rows, dtype=jnp.int32)[None, :]
    ).reshape(-1)
    cell_tokens = CELL * rows
    half_dim = HEAD_DIM // 2
    frequency = theta ** (-jnp.arange(half_dim, dtype=f32) * 2.0 / HEAD_DIM)

    def angle_table(here):
        turns = here.astype(f32)[:, None] * frequency[None, :]
        cosine = jnp.cos(turns)
        sine = jnp.sin(turns)
        return jnp.concatenate([cosine] * 4 + [-sine, sine] * 2, axis=1)

    gains = jnp.concatenate(
        [
            jnp.tile(query_gain, 2)[None, :],
            jnp.concatenate([key_gain, jnp.ones_like(key_gain)])[None, :],
            jnp.zeros((6, 2 * HEAD_DIM), f32),
        ],
        axis=0,
    )

    source = inputs.astype(f32)
    normed_attn_own = rms_scale(source, attention_gain).astype(bf16)
    def head_columns(start):
        both = lax.dynamic_slice_in_dim(
            qkv_weight, start + head // 2 * (2 * HEAD_DIM), 2 * HEAD_DIM, 1
        )
        return jnp.where(head % 2 == 0, both[:, :HEAD_DIM], both[:, HEAD_DIM:])

    qkv_own = jnp.concatenate(
        [
            block(qkv_weight, head, GROUP_WIDTH, 1),
            head_columns(query_width),
            head_columns(query_width + key_width),
        ],
        axis=1,
    )
    out_own = block(out_weight, head, width // CELL, 1)
    local_units = pair_count * unit
    pair_rows = pair * weight_rows

    def owner_columns(weight, owner):
        return jnp.concatenate(
            [
                lax.dynamic_slice_in_dim(
                    weight,
                    side * hidden_width + ((p * pair + owner) * CELL + head) * unit,
                    unit,
                    1,
                )
                for side in range(2)
                for p in range(pair_count)
            ],
            axis=1,
        )

    down_own = block(down_weight, head, unit)
    steps = Steps()
    sends = [functools.partial(fsdp_send, step=k) for k in range(fsdp_count)]

    class Buffer:
        def __init__(self, shape):
            self.value = blank(shape, bf16)

        def write(self, part, row, axis=0):
            self.value = lax.dynamic_update_slice_in_dim(self.value, part, row, axis)

    gate_up_pair = Buffer((pair_rows, 2 * local_units))
    gate_up_mine = Buffer((width, 2 * local_units))
    down_mine = Buffer((local_units, width))
    down_mine.write(down_own, pair_here * unit)
    pair_jobs, down_jobs, gate_up_jobs = [], [], []

    def part_of(values, n, count):
        size = values.shape[0] // count
        return lax.slice_in_dim(values, n * size, (n + 1) * size)

    for j in range(1, pair):
        for n in range(2):
            size = weight_rows // 2
            pair_jobs.append(
                (
                    lambda begin, n=n, j=j: pair_send(begin(part_of(owned[j], n, 2)), j, pair),
                    lambda got, n=n, j=j, size=size: gate_up_pair.write(
                        got, (in_pair - j) % pair * weight_rows + n * size
                    ),
                )
            )
    for step in range(1, pair_count):
        for n in range(4):
            size = unit // 4
            down_jobs.append(
                (
                    lambda begin, n=n, step=step: fsdp_send(
                        begin(part_of(down_own, n, 4)), step * pair
                    ),
                    lambda got, n=n, step=step, size=size: down_mine.write(
                        got, (pair_here - step) % pair_count * unit + n * size
                    ),
                )
            )
        for n in range(8):
            size = pair_rows // 8
            gate_up_jobs.append(
                (
                    lambda begin, n=n, step=step: fsdp_send(
                        begin(part_of(gate_up_pair.value, n, 8)), step * pair
                    ),
                    lambda got, n=n, step=step, size=size: gate_up_mine.write(
                        got, (pair_here - step) % pair_count * pair_rows + n * size
                    ),
                )
            )

    last = max(fsdp_count - 1, 3)
    got = steps.run(
        [(first_round, normed_attn_own), (angle_table, positions)]
        + [(send, qkv_own) for send in sends[1:2]]
    )
    angles = got[1]
    qkv_pieces = [qkv_own] + got[2:]
    two = rows_joined(normed_attn_own, got[0])
    got = steps.run(
        [
            (second_round, two),
            (
                lambda v: [owner_columns(v, (in_pair + j) % pair) for j in range(pair)],
                gate_up_weight,
            ),
        ]
        + [(send, qkv_own) for send in sends[2:last]]
    )
    owned = got[1]
    gate_up_pair.write(owned[0], in_pair * weight_rows)
    qkv_pieces += got[2:]
    mine = rows_joined(two, got[0])
    got = steps.run([(twin_send, mine)] + [(send, qkv_own) for send in sends[last:]])
    qkv_pieces += got[1:]
    normed_attn = [mine, got[0]]

    projected, outer_got, *out_got = steps.run(
        [
            (lambda v: project(place, *v, angles, gains, qkv_pieces, rows), normed_attn),
            (first_round, cotangent),
        ]
        + [(send, out_own) for send in sends[1::2]]
    )
    qkv_rows, query_low, kv_own = projected
    outer_two = rows_joined(cotangent, outer_got)
    kv_own = kv_own.reshape(CELL, 1, rows, 2 * HEAD_DIM)
    got = steps.run(
        [(send, kv_own) for send in sends[1:]]
        + [(second_round, outer_two)]
        + [(send, out_own) for send in sends[2::2]]
    )
    kv_pieces, got = [kv_own] + got[: fsdp_count - 1], got[fsdp_count - 1 :]
    outer_mine = rows_joined(outer_two, got[0])
    out_pieces = [out_own] + [None] * (fsdp_count - 1)
    out_pieces[1::2] = out_got
    out_pieces[2::2] = got[1:]
    kv_cells = blank((CELL, fsdp_count, rows, 2 * HEAD_DIM), bf16)
    out_columns = blank((width, width // CELL), bf16)
    for k in range(fsdp_count):
        kv_cells = put(kv_cells, kv_pieces[k], (fsdp_here - k) % fsdp_count, 1)
        out_columns = put(out_columns, out_pieces[k], (fsdp_here - k) % fsdp_count)
    chunk = fsdp_count * rows
    kv_all = kv_cells.reshape(CELL * chunk, 2 * HEAD_DIM)
    if cell_count > 1:
        kv_cells = kv_all
        kv_all = put(
            blank((cell_count * CELL * chunk, 2 * HEAD_DIM), bf16), kv_cells, cell
        )
        for step in range(1, cell_count):
            kv_all = put(kv_all, cell_send(kv_cells, step), (cell - step) % cell_count)

    steps.jobs = pair_jobs[:1] + down_jobs[:2]
    attended, out_rows, outer_other = steps.run(
        [
            (lambda v: attention(place, *v, rows, chunk), (query_low, kv_all)),
            (lambda v: cell_turn(v, 0, 1), out_columns),
            (twin_send, outer_mine),
        ],
        3,
    )
    *attended, log_total = attended
    outer_parts = [[outer_mine, outer_other]]
    steps.jobs = pair_jobs[1:] + down_jobs[2:] + gate_up_jobs
    terms = [dot(half, out_rows).astype(bf16) for half in attended]
    got = steps.run([(twin_send, terms[1])], 1)
    kept, sent = reduce_first(terms[0], got[0])
    got = steps.run(
        [(second_round, sent)]
        + [(lambda v, j=j: pair_send(v, -j, pair), cotangent) for j in range(1, pair)],
        2,
    )
    outer_next = got[1:]
    kept, sent = reduce_second(kept, got[0])
    got = steps.run([(first_round, sent)] + [(first_round, shard) for shard in outer_next], 1)
    outer_twos = [rows_joined(shard, g) for shard, g in zip(outer_next, got[1:])]
    hidden_mid = source + kept.astype(f32) + got[0].astype(f32)
    normed_own = rms_scale(hidden_mid, mlp_gain).astype(bf16)

    got = steps.run(
        [(first_round, normed_own)]
        + [(lambda v, j=j: pair_send(v, -j, pair), normed_own) for j in range(1, pair)]
        + [(second_round, v) for v in outer_twos],
        1,
    )
    two = rows_joined(normed_own, got[0])
    normed_next = got[1:pair]
    outer_mines = [rows_joined(v, g) for v, g in zip(outer_twos, got[pair:])]
    got = steps.run([(second_round, two)] + [(twin_send, v) for v in outer_mines], 2)
    mine = rows_joined(two, got[0])
    outer_parts += [[a, b] for a, b in zip(outer_mines, got[1:])]
    got = steps.run([(twin_send, mine)] + [(first_round, v) for v in normed_next], 1)
    normed_parts = [[mine, got[0]]]
    twos = [rows_joined(v, g) for v, g in zip(normed_next, got[1:])]
    if twos:
        got = steps.run([(second_round, v) for v in twos], 2)
        mines = [rows_joined(v, g) for v, g in zip(twos, got)]
        got = steps.run([(twin_send, v) for v in mines], 1)
        normed_parts += [[a, b] for a, b in zip(mines, got)]
    while steps.jobs:
        steps.run([(lambda v: v, normed_parts[-1][1])], 2)
    gate_up_mine.write(gate_up_pair.value, pair_here * pair_rows)
    gate_up_all, down_all = gate_up_mine.value, down_mine.value

    def feed_half(values):
        return feed(*values, gate_up_all, down_all)

    order = [(j, side) for j in reversed(range(pair)) for side in (1, 0)]
    results = {}
    waiting = []
    sums = {}

    def advance():
        return [(function, values) for function, values, _ in waiting]

    def settle(got):
        nonlocal waiting
        ongoing, waiting = waiting, []
        for (_, _, then), value in zip(ongoing, got):
            then(value)

    def reduce_start(j, mine, other):
        def ended(kept):
            def end(value):
                sums[j] = kept.astype(f32) + value.astype(f32)
                if j:
                    waiting.append(
                        (
                            lambda v: pair_send(v, j, pair),
                            sums[j].astype(bf16),
                            lambda value: sums.__setitem__(j, value.astype(f32)),
                        )
                    )

            return end

        def second(kept):
            def end(value):
                now, sent = reduce_second(kept, value)
                waiting.append((first_round, sent, ended(now)))

            return end

        def end(value):
            now, sent = reduce_first(mine(), value)
            waiting.append((second_round, sent, second(now)))

        waiting.append((twin_send, other, end))

    for j, side in order:
        ready = (normed_parts[j][side], outer_parts[j][side])
        result, *got = steps.run([(feed_half, ready)] + advance())
        results[j, side] = result
        settle(got)
        if side:
            reduce_start(j, lambda j=j: results[j, 0][2], result[2])
    keys = [(j, side) for j in range(pair) for side in range(2)]
    normed_flat = [normed_parts[j][side] for j, side in keys]
    outer_flat = [outer_parts[j][side] for j, side in keys]

    class PairTotal:
        def __init__(self, rows_of, operands, count=4):
            self.rows_of, self.operands, self.count = rows_of, operands, count
            self.pieces, self.got, self.left = None, [], count * (pair_count - 1)
            self.jobs = [
                (functools.partial(self.start, step, n), self.got.append)
                for step in range(1, pair_count)
                for n in range(count)
            ]

        def others(self):
            return (
                lambda v: [
                    self.rows_of(v, (pair_here + step) % pair_count) for step in range(1, pair_count)
                ],
                self.operands,
            )

        def own(self):
            return (lambda v: self.rows_of(v, pair_here), self.operands)

        def start(self, step, n, begin):
            if self.pieces is None:
                function, operands = self.others()
                self.pieces = function(operands)
            return fsdp_send(begin(part_of(self.pieces[step - 1], n, self.count)), step * pair)

        def complete(self):
            return len(self.got) == self.left

        def total(self, mine):
            steps.drain(self.complete)
            rows_here = [part_of(mine, n, self.count).astype(f32) for n in range(self.count)]
            for k, value in enumerate(self.got):
                rows_here[k % self.count] += value.astype(f32)
            return cell_sum(rows_joined(*rows_here)).astype(bf16)

    def side_total(side):
        return PairTotal(
            lambda v, p: weight_grad(*v, p, pair_rows, side, local_units),
            (normed_flat, [results[k][1] for k in keys]),
        )

    gate, up = side_total(0), side_total(1)
    down = PairTotal(
        lambda v, p: weight_grad(*v, p, unit, 0, width),
        ([results[k][0] for k in keys], outer_flat),
    )

    def shares_sent(total):
        return [
            pair_send(block(total, (in_pair + j) % pair, weight_rows), j, pair)
            for j in range(1, pair)
        ]

    def shares(total, got):
        return jnp.concatenate([block(total, in_pair, weight_rows)] + got, axis=1)

    branch_terms = [tuple(results[j, side][3] for side in range(2)) for j in range(pair)]
    branch_twins = []
    steps.jobs = gate.jobs + up.jobs + down.jobs
    gate_mine = None
    while waiting:
        parts = advance()
        count = len(parts)
        extra = []
        if len(branch_twins) < pair:
            extra.append((twin_send, branch_terms[pair - 1 - len(branch_twins)][1]))
        if gate.pieces is not None and gate_mine is None:
            extra.append(gate.own())
        got = steps.run(parts + extra, 1)
        settle(got[:count])
        got = got[count:]
        if len(branch_twins) < pair:
            branch_twins.append(got.pop(0))
        if got:
            gate_mine = got[0]
    normed_grad = sum(sums[j] for j in range(pair))
    mid_part, mlp_gain_grad = jax.vjp(rms_scale, hidden_mid, mlp_gain)[1](normed_grad)
    hidden_grad = cotangent.astype(f32) + mid_part
    branch_own = hidden_grad.astype(bf16)
    got = steps.run([(first_round, branch_own), up.others()], 1)
    up.pieces = got[1]
    two = rows_joined(branch_own, got[0])
    got = steps.run([(second_round, two), up.own()], 1)
    up_mine = got[1]
    mine = rows_joined(two, got[0])
    if gate_mine is None:
        gate_mine = gate.own()[0](gate.operands)
    gate_total = gate.total(gate_mine)
    branch_twins = branch_twins[::-1]
    branch_kept, branch_sent = map(
        list,
        zip(*[reduce_first(terms[0], value) for terms, value in zip(branch_terms, branch_twins)]),
    )
    got = steps.run(
        [
            (twin_send, mine),
            (second_round, branch_sent[-1]),
            (shares_sent, gate_total),
            down.others(),
        ],
        1,
    )
    branch_grad = [mine, got[0]]
    branch_kept[-1], branch_sent[-1] = reduce_second(branch_kept[-1], got[1])
    gate_share = shares(gate_total, got[2])
    down.pieces = got[3]

    def attention_half(other, kv_grad=None):
        return lambda v: attention_grad(
            place, query_low, v, attended[other], log_total, out_rows, kv_all, rows, chunk, other, kv_grad
        )

    (query_grad_mine, kv_grad), gate_got, *got = steps.run(
        [(attention_half(0), branch_grad[0]), (first_round, gate_share)]
        + [(second_round, sent) for sent in branch_sent[:-1]],
        2,
    )
    gate_two = rows_joined(gate_share, gate_got)
    for j, value in enumerate(got):
        branch_kept[j], branch_sent[j] = reduce_second(branch_kept[j], value)
    (query_grad_other, kv_grad), gate_got = steps.run(
        [(attention_half(1, kv_grad), branch_grad[1]), (second_round, gate_two)], 2
    )
    gate_half = rows_joined(gate_two, gate_got)
    query_grad = (query_grad_mine, query_grad_other)
    kv_grad = kv_grad.astype(bf16)
    if cell_count > 1:
        kv_grad_cell = block(kv_grad, cell, CELL * chunk).astype(f32)
        for step in range(1, cell_count):
            piece = block(kv_grad, (cell + step) % cell_count, CELL * chunk)
            kv_grad_cell = kv_grad_cell + cell_send(piece, step).astype(f32)
        kv_grad = kv_grad_cell.astype(bf16)
    kv_grad = kv_grad.reshape(CELL, fsdp_count, rows, 2 * HEAD_DIM)

    def kv_piece(k):
        return block(kv_grad, (fsdp_here + k) % fsdp_count, 1, 1)

    def fsdp_piece(values, k):
        return block(values, (fsdp_here + k) % fsdp_count, weight_rows)

    up_total = up.total(up_mine)
    got = steps.run(
        [(sends[k], kv_piece(k)) for k in range(1, fsdp_count)]
        + [(first_round, sent) for sent in branch_sent]
        + [
            (shares_sent, up_total),
            (
                lambda v: sum(dot(half, branch, TN) for half, branch in zip(*v)).astype(bf16),
                (attended, branch_grad),
            ),
        ]
    )
    kv_total = kv_piece(0).astype(f32)
    for value in got[: fsdp_count - 1]:
        kv_total = kv_total + value.astype(f32)
    kv_total = kv_total.reshape(cell_tokens, 2 * HEAD_DIM)
    branch_sums = [
        kept.astype(f32) + value.astype(f32)
        for kept, value in zip(branch_kept, got[fsdp_count - 1 :])
    ]
    outputs = hidden_mid + branch_sums[0]
    up_got, out_partial = got[-2:]
    up_share = shares(up_total, up_got)

    projected, gate_got, up_got, *branch_got = steps.run(
        [
            (
                lambda v: project_grad(
                    place, *normed_attn, angles, gains, qkv_rows, query_grad, v, qkv_pieces, rows
                ),
                kv_total,
            ),
            (twin_send, gate_half),
            (first_round, up_share),
        ]
        + [
            (lambda v, j=j: pair_send(v, j, pair), value.astype(bf16))
            for j, value in enumerate(branch_sums[1:], 1)
        ],
        1,
    )
    *qkv_grad, attn_mine, attn_other, head_gain_grad, attention_gain_grad = projected
    for value in branch_got:
        outputs = outputs + value.astype(f32)
    outputs = outputs.astype(bf16)
    gate_halves = (gate_half, gate_got)
    up_two = rows_joined(up_share, up_got)

    def gather_place(side, odd, half, whole):
        return place_blocks(
            whole,
            gate_up_weight.shape,
            half,
            (weight_rows, unit),
            (4, pair * pair_count),
            place,
            lambda i, g, at: (i, g),
            lambda i, g, at: (
                0,
                side * (hidden_width // unit)
                + ((g % pair_count) * pair + (at[3] - g // pair_count + pair) % pair) * CELL
                + token_block(4 * odd + i, at),
            ),
        )

    got = steps.run(
        [
            (twin_send, attn_other),
            (second_round, up_two),
            (down.own()),
            (lambda v: gather_place(0, 0, v, None), gate_halves[0]),
            (
                lambda v: sum(dot(half, grad, TN) for half, grad in zip(*v)).astype(bf16),
                (normed_attn, qkv_grad),
            ),
        ],
        2,
    )
    kept, sent = reduce_first(attn_mine, got[0])
    up_half = rows_joined(up_two, got[1])
    down_own_rows, grad_gate_up, qkv_partial = got[2:]
    gains_here = jnp.concatenate(
        [
            attention_gain_grad[0] / attention_gain,
            mlp_gain_grad,
            head_gain_grad[0],
            head_gain_grad[1],
        ]
    ).reshape(-1, 2 * HEAD_DIM)
    got = steps.run(
        [
            (second_round, sent),
            (lambda v: cell_turn(v, 1, 0), out_partial),
            (twin_send, up_half),
            (lambda v: gather_place(0, 1, *v), (gate_halves[1], grad_gate_up)),
        ],
        1,
    )
    kept, sent = reduce_second(kept, got[0])
    out_partial = got[1]
    up_halves = (up_half, got[2])
    grad_gate_up = got[3]
    down_share = down.total(down_own_rows)
    got = steps.run(
        [
            (first_round, sent),
            (first_round, down_share),
            (lambda v: gather_place(1, 0, *v), (up_halves[0], grad_gate_up)),
        ]
        + [(sends[k], fsdp_piece(out_partial, k)) for k in range(1, fsdp_count)]
    )
    attn_normed_grad = kept.astype(f32) + got[0].astype(f32)
    down_two = rows_joined(down_share, got[1])
    grad_gate_up = got[2]
    out_total = fsdp_piece(out_partial, 0).astype(f32)
    for value in got[3:]:
        out_total = out_total + value.astype(f32)
    out_share = cell_sum(out_total).astype(bf16)
    got = steps.run(
        [
            (second_round, down_two),
            (first_round, out_share),
            (lambda v: gather_place(1, 1, *v), (up_halves[1], grad_gate_up)),
        ]
        + [(sends[k], fsdp_piece(qkv_partial, k)) for k in range(1, fsdp_count)]
    )
    down_half = rows_joined(down_two, got[0])
    out_two = rows_joined(out_share, got[1])
    grad_gate_up = got[2]
    qkv_total = fsdp_piece(qkv_partial, 0).astype(f32)
    for value in got[3:]:
        qkv_total = qkv_total + value.astype(f32)
    qkv_share = cell_sum(qkv_total).astype(bf16)
    got = steps.run(
        [
            (twin_send, down_half),
            (second_round, out_two),
            (first_round, qkv_share),
            (sum_everywhere, gains_here),
            (
                lambda v: jax.vjp(lambda u: rms_scale(u, attention_gain), source)[1](v)[0],
                attn_normed_grad,
            ),
        ]
    )
    grad_down_halves = (down_half, got[0])
    out_half = rows_joined(out_two, got[1])
    qkv_two = rows_joined(qkv_share, got[2])
    gain_sums = got[3].reshape(-1)
    grad_inputs = (hidden_grad + got[4]).astype(bf16)
    got = steps.run(
        [
            (twin_send, out_half),
            (second_round, qkv_two),
            (lambda v: place_rows(v, place), grad_down_halves),
        ]
    )
    out_halves = (out_half, got[0])
    qkv_half = rows_joined(qkv_two, got[1])
    grad_down = got[2]
    got = steps.run(
        [
            (twin_send, qkv_half),
            (lambda v: place_columns(v, width // CELL, place), out_halves),
        ]
    )
    grad_out = got[1]
    grad_qkv = place_heads([qkv_half, got[0]], place)
    attention_gain_sum, mlp_gain_sum = gain_sums[:width], gain_sums[width : 2 * width]
    head_sums = gain_sums[2 * width :].reshape(4, HEAD_DIM)

    gain_sums = (
        attention_gain_sum,
        head_sums[0] + head_sums[1],
        head_sums[2],
        mlp_gain_sum,
    )

    return (
        outputs,
        grad_inputs,
        gain_sums[0],
        grad_qkv,
        gain_sums[1],
        gain_sums[2],
        grad_out,
        gain_sums[3],
        grad_gate_up,
        grad_down,
    )


def solution(mesh):
    return jax.shard_map(
        body,
        mesh=mesh,
        in_specs=(
            P(("ctx", "fsdp"), None),
            P(),
            P("fsdp", None),
            P(),
            P(),
            P("fsdp", None),
            P(),
            P("fsdp", None),
            P("fsdp", None),
            P(("ctx", "fsdp"), None),
        ),
        out_specs=(
            P(("ctx", "fsdp"), None),
            P(("ctx", "fsdp"), None),
            P(),
            P("fsdp", None),
            P(),
            P(),
            P("fsdp", None),
            P(),
            P("fsdp", None),
            P("fsdp", None),
        ),
        check_vma=False,
    )
```

```python
import functools

import jax
import jax.numpy as jnp
from jax import lax
from jax.experimental import pallas as pl
from jax.experimental.pallas import tpu as pltpu
from jax.sharding import PartitionSpec as P

HEADS = 32
KV_HEADS = 8
HEAD_DIM = 64
GROUP = HEADS // KV_HEADS
GROUP_WIDTH = GROUP * HEAD_DIM

epsilon = 1e-05
theta = 1000000.0
score_scale = HEAD_DIM ** (-0.5)

f32 = jnp.float32
bf16 = jnp.bfloat16

CELL = KV_HEADS

NN = (((1,), (0,)), ((), ()))
NT = (((1,), (1,)), ((), ()))
TN = (((0,), (0,)), ((), ()))


def dot(left, right, dims=NN):
    return lax.dot_general(left, right, dims, preferred_element_type=f32)


def rms_scale(values, gain):
    return values * lax.rsqrt(jnp.mean(values * values, axis=-1, keepdims=True) + epsilon) * gain


def xor_send(values, distance):
    count = lax.axis_size("ctx")
    return lax.ppermute(values, "ctx", [(i, i ^ distance) for i in range(count)])


def cell_send(values, step):
    count = lax.axis_size("ctx")
    return lax.ppermute(values, "ctx", [(i, (i + step * CELL) % count) for i in range(count)])


def fsdp_send(values, step):
    count = lax.axis_size("fsdp")
    return lax.ppermute(values, "fsdp", [(i, (i + step) % count) for i in range(count)])


def pair_send(values, step, pair):
    count = lax.axis_size("fsdp")
    return lax.ppermute(
        values, "fsdp", [(i, i // pair * pair + (i % pair + step) % pair) for i in range(count)]
    )


def fsdp_relay(shard):
    count = lax.axis_size("fsdp")
    return [shard] + [fsdp_send(shard, step) for step in range(1, count)]


def fsdp_collect(piece_for):
    count = lax.axis_size("fsdp")
    total = piece_for(0).astype(f32)
    for step in range(1, count):
        total = total + fsdp_send(piece_for(step), step).astype(f32)
    return total


def round_send(values, odd_round):
    count = lax.axis_size("ctx")
    pairs = []
    for i in range(count):
        pairs.append((i, i ^ (2 if i % 2 == odd_round else 4)))
    return lax.ppermute(values, "ctx", pairs)


def add_low(left, right):
    return (left.astype(f32) + right.astype(f32)).astype(bf16)


def after(values, event):
    return lax.optimization_barrier((values, event))[0]


class Steps:
    def __init__(self):
        self.event = None
        self.jobs = []

    def begin(self, values):
        return values if self.event is None else after(values, self.event)

    def run(self, parts, spare=0):
        jobs, self.jobs = self.jobs[:spare], self.jobs[spare:]
        results = [function(self.begin(values)) for function, values in parts]
        results += [start(self.begin) for start, _ in jobs]
        results = lax.optimization_barrier(results)
        for (_, finish), value in zip(jobs, results[len(parts) :]):
            finish(value)
        self.event = results[0]
        return results[: len(parts)]

    def drain(self, done):
        while self.jobs and not done():
            self.run([(lambda v: v, self.event)], 2)


def first_round(values):
    return round_send(values, 0)


def second_round(values):
    return round_send(values, 1)


def twin_send(values):
    return xor_send(values, 1)


def join_kernel(place_ref, *refs):
    for n, ref in enumerate(refs[:-1]):

        @pl.when(pl.program_id(0) == n)
        def _(ref=ref):
            refs[-1][...] = ref[...]


def join(parts, places=None):
    shape, dtype = parts[0].shape, parts[0].dtype
    if places is None:
        places = list(range(len(parts)))
    size = parts[0].size * 2
    return pl.pallas_call(
        join_kernel,
        grid_spec=pltpu.PrefetchScalarGridSpec(
            num_scalar_prefetch=1,
            grid=(len(parts),),
            in_specs=[pl.BlockSpec(shape, lambda i, at: (0, 0))] * len(parts),
            out_specs=pl.BlockSpec(shape, lambda i, at: (at[i], 0)),
        ),
        out_shape=jax.ShapeDtypeStruct((len(parts) * shape[0], shape[1]), dtype),
        compiler_params=pltpu.CompilerParams(
            vmem_limit_bytes=(2 * len(parts) + 2) * size + 4 * 1024 * 1024
        ),
        cost_estimate=cost(0, 2 * size * len(parts)),
    )(jnp.stack([jnp.asarray(p, jnp.int32) for p in places]), *parts)


def rows_joined(*parts):
    return join(parts)


def add_kernel(left_ref, right_ref, first_ref, second_ref):
    total = (left_ref[...].astype(f32) + right_ref[...].astype(f32)).astype(bf16)

    @pl.when(pl.program_id(0) == 0)
    def _():
        first_ref[...] = total

    @pl.when(pl.program_id(0) == 1)
    def _():
        second_ref[...] = total


def add_halves(left, right):
    rows, columns = left.shape
    half = jax.ShapeDtypeStruct((rows // 2, columns), bf16)
    in_spec = pl.BlockSpec((rows // 2, columns), lambda i: (i, 0))
    out_spec = pl.BlockSpec((rows // 2, columns), lambda i: (0, 0))
    return pl.pallas_call(
        add_kernel,
        grid=(2,),
        in_specs=[in_spec] * 2,
        out_specs=[out_spec] * 2,
        out_shape=[half, half],
        compiler_params=pltpu.CompilerParams(vmem_limit_bytes=20 * 1024 * 1024),
        cost_estimate=cost(left.size, 6 * left.size),
    )(left, right)


def reduce_first(mine, from_twin):
    return add_halves(mine, from_twin)


def reduce_second(kept, received):
    return add_halves(kept, received)


class SumEverywhere:
    def __init__(self, values):
        self.total = values
        self.rounds = []
        for axis in ("ctx", "fsdp"):
            count = lax.axis_size(axis)
            if count & (count - 1):
                self.rounds.append(functools.partial(self.whole, axis))
                continue
            distance = 1
            while distance < count:
                self.rounds.append(functools.partial(self.exchange, axis, count, distance))
                distance *= 2

    def exchange(self, axis, count, distance, values):
        return lax.ppermute(values, axis, [(i, i ^ distance) for i in range(count)])

    def whole(self, axis, values):
        return lax.psum(values, axis) - values

    def part(self):
        return (self.rounds.pop(0), self.total)

    def add(self, got):
        self.total = self.total + got

    def finish(self):
        while self.rounds:
            function, values = self.part()
            self.add(function(values))
        return self.total


def blank(shape, dtype):
    return pl.pallas_call(
        lambda ref: None,
        out_specs=pl.BlockSpec(memory_space=pl.ANY),
        out_shape=jax.ShapeDtypeStruct(shape, dtype),
        cost_estimate=pl.CostEstimate(flops=0, bytes_accessed=0, transcendentals=0),
    )()


def vmem(mebibytes, keys=0):
    return pltpu.CompilerParams(vmem_limit_bytes=mebibytes * 1024 * 1024 + keys * 2560)


def cost(flops, moved, transcendentals=0):
    return pl.CostEstimate(
        flops=int(flops), bytes_accessed=int(moved), transcendentals=int(transcendentals)
    )


def own(i, place):
    slot = i % 4
    other = i // 4
    swapped = (place[2] + other) % 2
    return slot // 2 * (4 - 2 * swapped) + slot % 2 * (2 + 2 * swapped) + other


def token_block(i, place):
    return jnp.bitwise_xor(own(i, place), place[2])


def even_block(i):
    return jnp.minimum(i, 3)


def odd_block(i):
    return jnp.maximum(i - 4, 0)


def swap_halves(values):
    lane = lax.broadcasted_iota(jnp.int32, values.shape, 1) % HEAD_DIM
    return jnp.where(
        lane < HEAD_DIM // 2,
        pltpu.roll(values, values.shape[1] - HEAD_DIM // 2, 1),
        pltpu.roll(values, HEAD_DIM // 2, 1),
    )


def head_mean(values):
    first = lax.broadcasted_iota(jnp.int32, values.shape, 1) < HEAD_DIM
    low = jnp.sum(jnp.where(first, values, 0.0), axis=1, keepdims=True)
    high = jnp.sum(jnp.where(first, 0.0, values), axis=1, keepdims=True)
    return jnp.where(first, low, high) * (1.0 / HEAD_DIM)


def project_kernel(fsdp_count, place_ref, even_ref, odd_ref, angle_ref, gain_ref, *refs):
    weight_refs, (rows_ref, q_ref, kv_ref) = refs[:fsdp_count], refs[fsdp_count:]
    depth = weight_refs[0].shape[0]

    def project(left_ref):
        total = None
        for step in range(fsdp_count):
            owner = lax.rem(place_ref[0] - step + fsdp_count, fsdp_count)
            left = left_ref[:, pl.ds(pl.multiple_of(owner * depth, depth), depth)]
            term = dot(left, weight_refs[step][...])
            total = term if total is None else total + term
        rows_ref[...] = total

    @pl.when(pl.program_id(0) < 4)
    def _():
        project(even_ref)

    @pl.when(pl.program_id(0) >= 4)
    def _():
        project(odd_ref)

    cosine = angle_ref[:, : 2 * HEAD_DIM]
    sine = angle_ref[:, 2 * HEAD_DIM :]
    wide = 2 * HEAD_DIM
    for group in range(GROUP_WIDTH // wide + 1):
        values = rows_ref[:, group * wide : (group + 1) * wide]
        last = group == GROUP_WIDTH // wide
        normed = values * lax.rsqrt(head_mean(values * values) + epsilon)
        normed = normed * gain_ref[int(last) : int(last) + 1, :]
        turned = normed * cosine + swap_halves(normed) * sine
        if last:
            lane = lax.broadcasted_iota(jnp.int32, values.shape, 1)
            kv_ref[...] = jnp.where(lane < HEAD_DIM, turned, values).astype(bf16)
        else:
            q_ref[:, group * wide : (group + 1) * wide] = turned.astype(bf16)


def project(place, even, odd, angles, gains, weights, rows):
    count = CELL
    fsdp_count = len(weights)
    width = even.shape[1]
    columns = weights[0].shape[1]
    return pl.pallas_call(
        functools.partial(project_kernel, fsdp_count),
        grid_spec=pltpu.PrefetchScalarGridSpec(
            num_scalar_prefetch=1,
            grid=(count,),
            in_specs=[
                pl.BlockSpec((rows, width), lambda i, place: (even_block(i), 0)),
                pl.BlockSpec((rows, width), lambda i, place: (odd_block(i), 0)),
                pl.BlockSpec((rows, 4 * HEAD_DIM), lambda i, place: (token_block(i, place), 0)),
                pl.BlockSpec((8, 2 * HEAD_DIM), lambda i, place: (0, 0)),
            ]
            + [pl.BlockSpec(w.shape, lambda i, place: (0, 0)) for w in weights],
            out_specs=[
                pl.BlockSpec((rows, columns), lambda i, place: (token_block(i, place), 0)),
                pl.BlockSpec((rows, GROUP_WIDTH), lambda i, place: (token_block(i, place), 0)),
                pl.BlockSpec((rows, 2 * HEAD_DIM), lambda i, place: (token_block(i, place), 0)),
            ],
        ),
        out_shape=[
            jax.ShapeDtypeStruct((count * rows, columns), f32),
            jax.ShapeDtypeStruct((count * rows, GROUP_WIDTH), bf16),
            jax.ShapeDtypeStruct((count * rows, 2 * HEAD_DIM), bf16),
        ],
        compiler_params=vmem(20),
        cost_estimate=cost(2 * count * rows * width * columns, 8e6),
    )(place, even, odd, angles, gains, *weights)


def project_grad_kernel(
    fsdp_count,
    place_ref,
    even_ref,
    odd_ref,
    angle_ref,
    gain_ref,
    rows_ref,
    q_even_ref,
    q_odd_ref,
    kv_ref,
    *refs,
):
    weight_refs = refs[:fsdp_count]
    (grad_even_ref, grad_odd_ref, part_even_ref, part_odd_ref, head_gain_ref, gain_grad_ref) = refs[
        fsdp_count:
    ]
    depth = weight_refs[0].shape[0]
    step_here = pl.program_id(0)

    @pl.when(step_here == 0)
    def _():
        head_gain_ref[...] = jnp.zeros_like(head_gain_ref)
        gain_grad_ref[...] = jnp.zeros_like(gain_grad_ref)

    cosine = angle_ref[:, : 2 * HEAD_DIM]
    sine = angle_ref[:, 2 * HEAD_DIM :]
    wide = 2 * HEAD_DIM
    pieces = []
    for group in range(GROUP_WIDTH // wide + 1):
        last = group == GROUP_WIDTH // wide
        values = rows_ref[:, group * wide : (group + 1) * wide]
        at = pl.ds(group * wide, wide)
        if last:
            grad = kv_ref[...]
        else:
            grad = jnp.where(step_here < 4, q_even_ref[:, at], q_odd_ref[:, at])
        scale = lax.rsqrt(head_mean(values * values) + epsilon)
        gain = gain_ref[int(last) : int(last) + 1, :]
        unturned = grad * cosine + swap_halves(grad * sine)
        head_gain_ref[int(last) : int(last) + 1, :] += jnp.sum(
            unturned * values * scale, axis=0, keepdims=True
        )
        scaled = unturned * gain
        piece = scale * scaled - values * (scale * scale * scale) * head_mean(scaled * values)
        if last:
            lane = lax.broadcasted_iota(jnp.int32, values.shape, 1)
            piece = jnp.where(lane < HEAD_DIM, piece, grad)
        pieces.append(piece.astype(bf16))
    low = jnp.concatenate(pieces, axis=1)

    def finish(normed_ref, grad_out_ref, part_ref):
        grad_out_ref[...] = low
        for step in range(fsdp_count):
            owner = lax.rem(place_ref[0] - step + fsdp_count, fsdp_count)
            at = pl.ds(pl.multiple_of(owner * depth, depth), depth)
            part = dot(low, weight_refs[step][...], NT)
            part_ref[:, at] = part.astype(bf16)
            gain_grad_ref[0:1, at] += jnp.sum(
                part * normed_ref[:, at].astype(f32), axis=0, keepdims=True
            )

    @pl.when(step_here < 4)
    def _():
        finish(even_ref, grad_even_ref, part_even_ref)

    @pl.when(step_here >= 4)
    def _():
        finish(odd_ref, grad_odd_ref, part_odd_ref)


def project_grad(place, even, odd, angles, gains, qkv_rows, query_grad, kv_grad, weights, rows):
    count = CELL
    fsdp_count = len(weights)
    width = even.shape[1]
    columns = weights[0].shape[1]

    def by_token(size):
        return pl.BlockSpec((rows, size), lambda i, place: (token_block(i, place), 0))

    def halves(size):
        return [
            pl.BlockSpec((rows, size), lambda i, place: (even_block(i), 0)),
            pl.BlockSpec((rows, size), lambda i, place: (odd_block(i), 0)),
        ]

    return pl.pallas_call(
        functools.partial(project_grad_kernel, fsdp_count),
        grid_spec=pltpu.PrefetchScalarGridSpec(
            num_scalar_prefetch=1,
            grid=(count,),
            in_specs=halves(width)
            + [
                by_token(4 * HEAD_DIM),
                pl.BlockSpec((8, 2 * HEAD_DIM), lambda i, place: (0, 0)),
                by_token(columns),
                *halves(GROUP_WIDTH),
                by_token(2 * HEAD_DIM),
            ]
            + [pl.BlockSpec(w.shape, lambda i, place: (0, 0)) for w in weights],
            out_specs=halves(columns)
            + halves(width)
            + [
                pl.BlockSpec((8, 2 * HEAD_DIM), lambda i, place: (0, 0)),
                pl.BlockSpec((8, width), lambda i, place: (0, 0)),
            ],
        ),
        out_shape=[
            jax.ShapeDtypeStruct((4 * rows, columns), bf16),
            jax.ShapeDtypeStruct((4 * rows, columns), bf16),
            jax.ShapeDtypeStruct((4 * rows, width), bf16),
            jax.ShapeDtypeStruct((4 * rows, width), bf16),
            jax.ShapeDtypeStruct((8, 2 * HEAD_DIM), f32),
            jax.ShapeDtypeStruct((8, width), f32),
        ],
        compiler_params=vmem(48),
        cost_estimate=cost(2 * count * rows * width * columns, 12e6),
    )(place, even, odd, angles, gains, qkv_rows, *query_grad, kv_grad, *weights)


def stack_heads(block):
    return jnp.concatenate(
        [block[:, i * HEAD_DIM : (i + 1) * HEAD_DIM] for i in range(GROUP)], axis=0
    )


def unstack_heads(turned, rows):
    return jnp.concatenate([turned[:, i * rows : (i + 1) * rows].T for i in range(GROUP)], axis=1)


def fill_turned(place_ref, kv_ref, turned_ref, chunk):
    @pl.when(pl.program_id(0) == 0)
    def _():
        def turn(n, _):
            start = pl.multiple_of(n * chunk, chunk)
            turned_ref[:, pl.ds(start, chunk)] = kv_ref[pl.ds(start, chunk), :].T
            return 0

        lax.fori_loop(0, (place_ref[1] + 1) * CELL, turn, 0)


def visible_keys(place_ref, chunk, rows):
    key_row = lax.broadcasted_iota(jnp.int32, (chunk, GROUP * rows), 0)
    row_at = lax.broadcasted_iota(jnp.int32, (chunk, GROUP * rows), 1) % rows
    count = chunk // rows
    owner = (place_ref[0] - key_row // rows + count) % count
    return owner * rows + key_row % rows <= row_at + place_ref[0] * rows


def attention_kernel(
    chunk, place_ref, q_ref, kv_ref, even_ref, odd_ref, log_ref, turned_ref
):
    rows = q_ref.shape[0]
    fill_turned(place_ref, kv_ref, turned_ref, chunk)
    queries = stack_heads(q_ref[...].astype(f32) * score_scale).astype(bf16)
    queries = jnp.concatenate([queries, jnp.zeros_like(queries)], axis=1)

    def step(n, running, masked):
        total, summed = running
        start = pl.multiple_of(n * chunk, chunk)
        weights = jnp.exp(dot(kv_ref[pl.ds(start, chunk), :], queries, NT))
        if masked:
            weights = jnp.where(visible_keys(place_ref, chunk, rows), weights, 0.0)
        return (
            total + jnp.sum(weights, axis=0, keepdims=True),
            summed + dot(turned_ref[:, pl.ds(start, chunk)], weights.astype(bf16)),
        )

    last = place_ref[1] * CELL + token_block(pl.program_id(0), place_ref)
    running = (
        jnp.zeros((1, GROUP * rows), f32),
        jnp.zeros((2 * HEAD_DIM, GROUP * rows), f32),
    )
    running = lax.fori_loop(0, last, lambda n, r: step(n, r, False), running)
    total, summed = step(last, running, True)
    result = unstack_heads(summed[HEAD_DIM:] / total, rows).astype(bf16)

    @pl.when(pl.program_id(0) < 4)
    def _():
        even_ref[...] = result

    @pl.when(pl.program_id(0) >= 4)
    def _():
        odd_ref[...] = result

    log_ref[...] = jnp.log(total)[None]


def attention(place, queries, keys_values, rows, chunk):
    count = queries.shape[0] // rows
    keys = keys_values.shape[0]
    half = jax.ShapeDtypeStruct((4 * rows, GROUP_WIDTH), bf16)
    return pl.pallas_call(
        functools.partial(attention_kernel, chunk),
        grid_spec=pltpu.PrefetchScalarGridSpec(
            num_scalar_prefetch=1,
            grid=(count,),
            in_specs=[
                pl.BlockSpec((rows, GROUP_WIDTH), lambda i, place: (token_block(i, place), 0)),
                pl.BlockSpec((keys, 2 * HEAD_DIM), lambda i, place: (0, 0)),
            ],
            out_specs=[
                pl.BlockSpec((rows, GROUP_WIDTH), lambda i, place: (even_block(i), 0)),
                pl.BlockSpec((rows, GROUP_WIDTH), lambda i, place: (odd_block(i), 0)),
                pl.BlockSpec((1, 1, GROUP * rows), lambda i, place: (i, 0, 0)),
            ],
            scratch_shapes=[pltpu.VMEM((2 * HEAD_DIM, keys), bf16)],
        ),
        out_shape=[half, half, jax.ShapeDtypeStruct((count, 1, GROUP * rows), f32)],
        compiler_params=vmem(12, keys),
        cost_estimate=cost(16e9, 8e6, 1e7),
    )(place, queries, keys_values)


def attention_grad_kernel(
    chunk,
    other,
    place_ref,
    q_ref,
    branch_ref,
    out_ref,
    log_ref,
    weight_ref,
    kv_ref,
    *refs,
):
    q_grad_ref, kv_grad_ref, turned_ref = refs[-3:]
    rows = q_ref.shape[0]
    fill_turned(place_ref, kv_ref, turned_ref, chunk)

    @pl.when(pl.program_id(0) == 0)
    def _():
        kv_grad_ref[...] = refs[0][...] if other else jnp.zeros_like(kv_grad_ref)

    queries = stack_heads(q_ref[...].astype(f32) * score_scale).astype(bf16)
    queries = jnp.concatenate([queries, jnp.zeros_like(queries)], axis=1)
    out_grad = dot(branch_ref[...], weight_ref[...], NT).astype(bf16)
    grads = stack_heads(out_grad)
    attended = stack_heads(out_ref[...]).astype(f32)
    row_delta = jnp.sum((grads.astype(f32) * attended).T, axis=0, keepdims=True)
    grads = jnp.concatenate([jnp.zeros_like(grads), grads], axis=1)
    log_total = log_ref[0]

    def step(n, summed, masked):
        start = pl.multiple_of(n * chunk, chunk)
        block = kv_ref[pl.ds(start, chunk), :]
        weights = jnp.exp(dot(block, queries, NT) - log_total)
        if masked:
            weights = jnp.where(visible_keys(place_ref, chunk, rows), weights, 0.0)
        score_grad = (weights * (dot(block, grads, NT) - row_delta)).astype(bf16)
        kv_grad_ref[pl.ds(start, chunk), :] += dot(score_grad, queries) + dot(
            weights.astype(bf16), grads
        )
        return summed + dot(turned_ref[:, pl.ds(start, chunk)], score_grad)

    last = place_ref[1] * CELL + token_block(pl.program_id(0) + 4 * other, place_ref)
    summed = jnp.zeros((2 * HEAD_DIM, GROUP * rows), f32)
    summed = lax.fori_loop(0, last, lambda n, r: step(n, r, False), summed)
    summed = step(last, summed, True)
    q_grad_ref[...] = unstack_heads(summed[:HEAD_DIM] * score_scale, rows)


def attention_grad(
    place, queries, branch, attended, log_total, weight, keys_values, rows, chunk, other, kv_grad=None
):
    keys = keys_values.shape[0]
    width = weight.shape[1]
    whole_spec = pl.BlockSpec((keys, 2 * HEAD_DIM), lambda i, place: (0, 0))
    added = [] if kv_grad is None else [kv_grad]
    return pl.pallas_call(
        functools.partial(attention_grad_kernel, chunk, other),
        grid_spec=pltpu.PrefetchScalarGridSpec(
            num_scalar_prefetch=1,
            grid=(4,),
            in_specs=[
                pl.BlockSpec(
                    (rows, GROUP_WIDTH), lambda i, place: (token_block(i + 4 * other, place), 0)
                ),
                pl.BlockSpec((rows, width), lambda i, place: (i, 0)),
                pl.BlockSpec((rows, GROUP_WIDTH), lambda i, place: (i, 0)),
                pl.BlockSpec((1, 1, GROUP * rows), lambda i, place: (i + 4 * other, 0, 0)),
                pl.BlockSpec(weight.shape, lambda i, place: (0, 0)),
                whole_spec,
            ]
            + [whole_spec] * len(added),
            out_specs=[
                pl.BlockSpec((rows, GROUP_WIDTH), lambda i, place: (i, 0)),
                whole_spec,
            ],
            scratch_shapes=[pltpu.VMEM((2 * HEAD_DIM, keys), bf16)],
        ),
        out_shape=[
            jax.ShapeDtypeStruct((4 * rows, GROUP_WIDTH), f32),
            jax.ShapeDtypeStruct(keys_values.shape, f32),
        ],
        compiler_params=vmem(18, keys),
        cost_estimate=cost(18e9, 12e6, 5e6),
    )(place, queries, branch, attended, log_total, weight, keys_values, *added)


def feed_kernel(
    normed_ref, outer_ref, weight_ref, down_ref, active_ref, gate_grad_ref, part_ref, branch_ref
):
    units = active_ref.shape[1]
    both = dot(normed_ref[...], weight_ref[...])
    gate = both[:, :units]
    up = both[:, units:]
    act_grad = dot(outer_ref[...], down_ref[...], NT)
    logistic = 1.0 / (1.0 + jnp.exp(-gate))
    silu = gate * logistic
    active_ref[...] = (silu * up).astype(bf16)
    gate_part = act_grad * up * (logistic * (1.0 + gate * (1.0 - logistic)))
    gate_grad_ref[:, :units] = gate_part.astype(bf16)
    gate_grad_ref[:, units:] = (act_grad * silu).astype(bf16)
    part_ref[...] = dot(gate_grad_ref[...], weight_ref[...], NT).astype(bf16)
    branch_ref[...] = dot(active_ref[...], down_ref[...]).astype(bf16)


def feed(normed, outer, weight, down):
    tokens, width = normed.shape
    columns = weight.shape[1]
    rows = 256 if tokens % 256 == 0 else tokens

    def by_row(size):
        return pl.BlockSpec((rows, size), lambda i: (i, 0))

    def low(size):
        return jax.ShapeDtypeStruct((tokens, size), bf16)

    return pl.pallas_call(
        feed_kernel,
        grid=(tokens // rows,),
        in_specs=[
            by_row(width),
            by_row(width),
            pl.BlockSpec(weight.shape, lambda i: (0, 0)),
            pl.BlockSpec(down.shape, lambda i: (0, 0)),
        ],
        out_specs=[by_row(columns // 2), by_row(columns), by_row(width), by_row(width)],
        out_shape=[low(columns // 2), low(columns), low(width), low(width)],
        compiler_params=vmem(36),
        cost_estimate=cost(6 * tokens * width * columns, 16e6, tokens * columns),
    )(normed, outer, weight, down)


def weight_grad_kernel(count, place_ref, *refs):
    total = None
    for left_ref, right_ref in zip(refs[:count], refs[count : 2 * count]):
        term = dot(left_ref[...], right_ref[...], TN)
        total = term if total is None else total + term
    for n, ref in enumerate(refs[2 * count :]):

        @pl.when(pl.program_id(0) == n)
        def _(ref=ref):
            ref[...] = total.astype(bf16)


def weight_grad(lefts, rights, first, size, column, columns, count):
    tokens = lefts[0].shape[0]
    tile = size // count
    place = jnp.stack([first * count]).astype(jnp.int32)
    if tile % 128:
        tile, place = size, jnp.stack([first]).astype(jnp.int32)
    parts = size // tile
    made = pl.pallas_call(
        functools.partial(weight_grad_kernel, len(lefts)),
        grid_spec=pltpu.PrefetchScalarGridSpec(
            num_scalar_prefetch=1,
            grid=(parts,),
            in_specs=[pl.BlockSpec((tokens, tile), lambda i, at: (0, at[0] + i))] * len(lefts)
            + [pl.BlockSpec((tokens, columns), lambda i, at: (0, column))] * len(rights),
            out_specs=[pl.BlockSpec((tile, columns), lambda i, at: (0, 0))] * parts,
        ),
        out_shape=[jax.ShapeDtypeStruct((tile, columns), bf16)] * parts,
        compiler_params=vmem(36),
        cost_estimate=cost(2 * len(lefts) * tokens * size * columns, 12e6),
    )(place, *lefts, *rights)
    if parts == count:
        return list(made)
    return [lax.slice_in_dim(made[0], n * size // count, (n + 1) * size // count) for n in range(count)]


def place_kernel(place_ref, shard_ref, *refs):
    refs[-1][...] = shard_ref[...].astype(f32)


def place_blocks(whole, shape, source, block, grid, place, from_block, to_block):
    in_specs = [pl.BlockSpec(block, from_block)]
    operands = [place, source]
    aliases = {}
    if whole is not None:
        in_specs.append(pl.BlockSpec(memory_space=pl.ANY))
        operands.append(whole)
        aliases = {2: 0}
    return pl.pallas_call(
        place_kernel,
        grid_spec=pltpu.PrefetchScalarGridSpec(
            num_scalar_prefetch=1,
            grid=grid,
            in_specs=in_specs,
            out_specs=pl.BlockSpec(block, to_block),
        ),
        out_shape=jax.ShapeDtypeStruct(shape, f32),
        input_output_aliases=aliases,
        compiler_params=vmem(16),
        cost_estimate=cost(0, 6 * source.size),
    )(*operands)


def place_units_kernel(block_at, unit, columns, place_ref, source_ref, *refs):
    out_ref, wide_ref, sems = refs[-3:]
    rows = wide_ref.shape[1]
    copies = []
    for n in range(wide_ref.shape[0]):
        slot, column = n // columns, n % columns
        wide_ref[n] = source_ref[
            slot * rows : (slot + 1) * rows, column * unit : (column + 1) * unit
        ].astype(f32)
        start = pl.multiple_of(block_at(slot, column, place_ref) * unit, unit)
        copies.append(
            pltpu.make_async_copy(wide_ref.at[n], out_ref.at[:, pl.ds(start, unit)], sems.at[n])
        )
        copies[-1].start()
    for copy in copies:
        copy.wait()


def place_units(whole, shape, source, rows, unit, place, block_at):
    slots, columns = source.shape[0] // rows, source.shape[1] // unit
    count = slots * columns
    in_specs = [pl.BlockSpec(source.shape, lambda i, at: (0, 0))]
    operands = [place, source]
    aliases = {}
    if whole is not None:
        in_specs.append(pl.BlockSpec(memory_space=pl.ANY))
        operands.append(whole)
        aliases = {2: 0}
    return pl.pallas_call(
        functools.partial(place_units_kernel, block_at, unit, columns),
        grid_spec=pltpu.PrefetchScalarGridSpec(
            num_scalar_prefetch=1,
            grid=(1,),
            in_specs=in_specs,
            out_specs=pl.BlockSpec(memory_space=pl.ANY),
            scratch_shapes=[
                pltpu.VMEM((count, rows, unit), f32),
                pltpu.SemaphoreType.DMA((count,)),
            ],
        ),
        out_shape=jax.ShapeDtypeStruct(shape, f32),
        input_output_aliases=aliases,
        compiler_params=vmem(16),
        cost_estimate=cost(0, 6 * source.size),
    )(*operands)


def place_columns(halves, unit, place):
    whole = None
    rows = halves[0].shape[0] // 4
    for odd, half in enumerate(halves):
        whole = place_blocks(
            whole,
            (rows, CELL * unit),
            half,
            (rows, unit),
            (4,),
            place,
            lambda i, at: (i, 0),
            lambda i, at, odd=odd: (0, token_block(4 * odd + i, at)),
        )
    return whole


def place_rows(quarters, place):
    whole = None
    rows, columns = quarters[0].shape[0] // 2, quarters[0].shape[1]
    for n, quarter in enumerate(quarters):
        whole = place_blocks(
            whole,
            (CELL * rows, columns),
            quarter,
            (rows, columns),
            (2,),
            place,
            lambda i, at: (i, 0),
            lambda i, at, n=n: (token_block(2 * n + i, at), 0),
        )
    return whole


def place_heads_kernel(place_ref, even_ref, odd_ref, out_ref):
    query_width = HEADS * HEAD_DIM
    key_width = KV_HEADS * HEAD_DIM
    even = even_ref[...].astype(f32)
    odd = odd_ref[...].astype(f32)
    first = lax.rem(place_ref[2], 2) == 0
    low = jnp.where(first, even, odd)
    high = jnp.where(first, odd, even)
    twins = token_block(pl.program_id(0), place_ref) // 2

    def at(start, size):
        return pl.ds(pl.multiple_of(start + twins * size, 128), size)

    out_ref[:, at(0, 2 * GROUP_WIDTH)] = jnp.concatenate(
        [low[:, :GROUP_WIDTH], high[:, :GROUP_WIDTH]], axis=1
    )
    middle = GROUP_WIDTH + HEAD_DIM
    out_ref[:, at(query_width, 2 * HEAD_DIM)] = jnp.concatenate(
        [low[:, GROUP_WIDTH:middle], high[:, GROUP_WIDTH:middle]], axis=1
    )
    out_ref[:, at(query_width + key_width, 2 * HEAD_DIM)] = jnp.concatenate(
        [low[:, middle:], high[:, middle:]], axis=1
    )


def place_heads(halves, place):
    rows, columns = halves[0].shape[0] // 4, halves[0].shape[1]
    shape = (rows, CELL * columns)
    return pl.pallas_call(
        place_heads_kernel,
        grid_spec=pltpu.PrefetchScalarGridSpec(
            num_scalar_prefetch=1,
            grid=(4,),
            in_specs=[
                pl.BlockSpec((rows, columns), lambda i, at: (i, 0)),
                pl.BlockSpec((rows, columns), lambda i, at: (i % 2 * 2 + i // 2, 0)),
            ],
            out_specs=pl.BlockSpec(shape, lambda i, at: (0, 0)),
        ),
        out_shape=jax.ShapeDtypeStruct(shape, f32),
        compiler_params=vmem(28),
        cost_estimate=cost(0, 6 * rows * CELL * columns),
    )(place, *halves)


def body(
    inputs,
    attention_gain,
    qkv_weight,
    query_gain,
    key_gain,
    out_weight,
    mlp_gain,
    gate_up_weight,
    down_weight,
    cotangent,
):
    rows, width = inputs.shape
    fsdp_count = lax.axis_size("fsdp")
    cell_count = lax.axis_size("ctx") // CELL
    pair = 2 if fsdp_count % 2 == 0 else 1
    pair_count = fsdp_count // pair
    fsdp_here = lax.axis_index("fsdp")
    ctx_here = lax.axis_index("ctx")
    head = ctx_here % CELL
    cell = ctx_here // CELL
    in_pair = fsdp_here % pair
    pair_here = fsdp_here // pair
    weight_rows = qkv_weight.shape[0]
    query_width = HEADS * HEAD_DIM
    key_width = KV_HEADS * HEAD_DIM
    hidden_width = gate_up_weight.shape[1] // 2
    unit = hidden_width // (fsdp_count * CELL)
    place = jnp.stack([fsdp_here, cell, head, in_pair]).astype(jnp.int32)

    def block(values, index, size, axis=0):
        return lax.dynamic_slice_in_dim(values, index * size, size, axis)

    def put(whole, part, index, axis=0):
        return lax.dynamic_update_slice_in_dim(whole, part, index * part.shape[axis], axis)

    def cell_sum(values):
        total = values.astype(f32)
        for step in range(1, cell_count):
            total = total + cell_send(values.astype(bf16), step).astype(f32)
        return total

    def cell_turn(values, split_axis, join_axis):
        groups = None
        if cell_count > 1:
            groups = [[c * CELL + i for i in range(CELL)] for c in range(cell_count)]
        return lax.all_to_all(
            values, "ctx", split_axis, join_axis, axis_index_groups=groups, tiled=True
        )

    blocks_here = cell * CELL + jnp.arange(CELL, dtype=jnp.int32)
    positions = (
        ((blocks_here * fsdp_count + fsdp_here) * rows)[:, None]
        + jnp.arange(rows, dtype=jnp.int32)[None, :]
    ).reshape(-1)
    cell_tokens = CELL * rows
    half_dim = HEAD_DIM // 2
    frequency = theta ** (-jnp.arange(half_dim, dtype=f32) * 2.0 / HEAD_DIM)

    def angle_table(here):
        turns = here.astype(f32)[:, None] * frequency[None, :]
        cosine = jnp.cos(turns)
        sine = jnp.sin(turns)
        return jnp.concatenate([cosine] * 4 + [-sine, sine] * 2, axis=1)

    gains = jnp.concatenate(
        [
            jnp.tile(query_gain, 2)[None, :],
            jnp.concatenate([key_gain, jnp.ones_like(key_gain)])[None, :],
            jnp.zeros((6, 2 * HEAD_DIM), f32),
        ],
        axis=0,
    )

    source = inputs.astype(f32)
    normed_attn_own = rms_scale(source, attention_gain).astype(bf16)
    def head_columns(start):
        both = lax.dynamic_slice_in_dim(
            qkv_weight, start + head // 2 * (2 * HEAD_DIM), 2 * HEAD_DIM, 1
        )
        return jnp.where(head % 2 == 0, both[:, :HEAD_DIM], both[:, HEAD_DIM:])

    qkv_own = jnp.concatenate(
        [
            block(qkv_weight, head, GROUP_WIDTH, 1),
            head_columns(query_width),
            head_columns(query_width + key_width),
        ],
        axis=1,
    )
    out_own = block(out_weight, head, width // CELL, 1)
    local_units = pair_count * unit
    pair_rows = pair * weight_rows

    def owner_columns(weight, owner):
        return jnp.concatenate(
            [
                lax.dynamic_slice_in_dim(
                    weight,
                    side * hidden_width + ((p * pair + owner) * CELL + head) * unit,
                    unit,
                    1,
                )
                for side in range(2)
                for p in range(pair_count)
            ],
            axis=1,
        )

    steps = Steps()
    sends = [functools.partial(fsdp_send, step=k) for k in range(fsdp_count)]

    pair_jobs, down_jobs, own_jobs, mate_jobs = [], [], [], []
    gate_up_parts, down_parts = [], []

    def half_columns(weight, owner, n):
        size = weight_rows // 2
        return owner_columns(lax.slice_in_dim(weight, n * size, (n + 1) * size), owner)

    def cross_job(read, step, row):
        return (
            lambda begin: fsdp_send(begin(read()), step * pair),
            lambda got: gate_up_parts.append((got, (fsdp_here - step * pair) % fsdp_count, row)),
        )

    mates = {}

    def mate_job(j, n):
        def finish(got):
            mates[j, n] = got
            gate_up_parts.append((got, pair_here * pair + (in_pair - j) % pair, n))

        return (lambda begin: pair_send(begin(owned[j, n]), j, pair), finish)

    def mate_cross_job(j, n, step):
        def finish(got):
            layer = (pair_here - step) % pair_count * pair + (in_pair - j) % pair
            gate_up_parts.append((got, layer, n))

        return (lambda begin: fsdp_send(begin(mates[j, n]), step * pair), finish)

    def down_job(step, n):
        return (
            lambda begin: fsdp_send(begin(down_pieces[n]), step * pair),
            lambda got: down_parts.append((got, (pair_here - step) % pair_count, n)),
        )

    for n in range(2):
        for j in range(1, pair):
            pair_jobs.append(mate_job(j, n))
        for step in range(1, pair_count):
            own_jobs.append(cross_job(lambda n=n: owned[0, n], step, n))
            for j in range(1, pair):
                mate_jobs.append(mate_cross_job(j, n, step))
    for n in range(4):
        for step in range(1, pair_count):
            down_jobs.append(down_job(step, n))

    last = max(fsdp_count - 1, 3)
    got = steps.run(
        [(first_round, normed_attn_own), (angle_table, positions)]
        + [(send, qkv_own) for send in sends[1:2]]
    )
    angles = got[1]
    qkv_pieces = [qkv_own] + got[2:]
    two = rows_joined(normed_attn_own, got[0])
    got = steps.run(
        [
            (second_round, two),
            (
                lambda v: (
                    {
                        (j, n): half_columns(v[0], (in_pair + j) % pair, n)
                        for j in range(pair)
                        for n in range(2)
                    },
                    [
                        lax.dynamic_slice_in_dim(
                            v[1], head * unit + n * (unit // 4), unit // 4
                        )
                        for n in range(4)
                    ],
                ),
                (gate_up_weight, down_weight),
            ),
        ]
        + [(send, qkv_own) for send in sends[2:last]]
    )
    owned, down_pieces = got[1]
    for n in range(2):
        gate_up_parts.append((owned[0, n], fsdp_here, n))
    for n in range(4):
        down_parts.append((down_pieces[n], pair_here, n))
    qkv_pieces += got[2:]
    mine = rows_joined(two, got[0])
    got = steps.run([(twin_send, mine)] + [(send, qkv_own) for send in sends[last:]])
    qkv_pieces += got[1:]
    normed_attn = [mine, got[0]]

    queue = [pair_jobs, pair_jobs, own_jobs, down_jobs, own_jobs, down_jobs, down_jobs]
    for jobs in queue + [mate_jobs, down_jobs, mate_jobs]:
        if jobs:
            steps.jobs.append(jobs.pop(0))
    steps.jobs += pair_jobs + down_jobs + own_jobs + mate_jobs

    projected, outer_got, *out_got = steps.run(
        [
            (lambda v: project(place, *v, angles, gains, qkv_pieces, rows), normed_attn),
            (first_round, cotangent),
        ]
        + [(send, out_own) for send in sends[1:]],
        1,
    )
    qkv_rows, query_low, kv_own = projected
    outer_two = rows_joined(cotangent, outer_got)
    kv_own = kv_own.reshape(CELL, 1, rows, 2 * HEAD_DIM)
    out_columns = join([out_own] + out_got, [(fsdp_here - k) % fsdp_count for k in range(fsdp_count)])

    def send_then_turn(split_axis, join_axis):
        def act(v):
            got = sends[1](v[0])
            return got, cell_turn(after(v[1], got), split_axis, join_axis)

        return act

    (kv_next, out_rows), *got = steps.run(
        [(send_then_turn(0, 1), (kv_own, out_columns))]
        + [(send, kv_own) for send in sends[2:]]
        + [(second_round, outer_two)],
        1,
    )
    kv_pieces = [kv_own, kv_next] + got[:-1]
    outer_mine = rows_joined(outer_two, got[-1])
    kv_cells = jnp.concatenate(kv_pieces, axis=1)
    chunk = fsdp_count * rows
    kv_all = kv_cells.reshape(CELL * chunk, 2 * HEAD_DIM)
    if cell_count > 1:
        kv_cells = kv_all
        kv_all = put(
            blank((cell_count * CELL * chunk, 2 * HEAD_DIM), bf16), kv_cells, cell
        )
        for step in range(1, cell_count):
            kv_all = put(kv_all, cell_send(kv_cells, step), (cell - step) % cell_count)

    attended, outer_other = steps.run(
        [
            (lambda v: attention(place, *v, rows, chunk), (query_low, kv_all)),
            (twin_send, outer_mine),
        ],
        1,
    )
    *attended, log_total = attended
    outer_parts = [[outer_mine, outer_other]]
    terms = [dot(half, out_rows).astype(bf16) for half in attended]
    got = steps.run([(twin_send, terms[1])], 1)
    kept, sent = reduce_first(terms[0], got[0])
    got = steps.run(
        [(second_round, sent)]
        + [(lambda v, j=j: pair_send(v, -j, pair), cotangent) for j in range(1, pair)],
        1,
    )
    outer_next = got[1:]
    kept, sent = reduce_second(kept, got[0])
    got = steps.run([(first_round, sent)] + [(first_round, shard) for shard in outer_next], 1)
    outer_twos = [rows_joined(shard, g) for shard, g in zip(outer_next, got[1:])]
    hidden_mid = source + kept.astype(f32) + got[0].astype(f32)
    normed_own = rms_scale(hidden_mid, mlp_gain).astype(bf16)

    got = steps.run(
        [(first_round, normed_own)]
        + [(lambda v, j=j: pair_send(v, -j, pair), normed_own) for j in range(1, pair)]
        + [(second_round, v) for v in outer_twos],
        1,
    )
    two = rows_joined(normed_own, got[0])
    normed_next = got[1:pair]
    outer_mines = [rows_joined(v, g) for v, g in zip(outer_twos, got[pair:])]
    got = steps.run(
        [(second_round, two)]
        + [(first_round, v) for v in normed_next]
        + [(twin_send, v) for v in outer_mines],
        1,
    )
    mine = rows_joined(two, got[0])
    twos = [rows_joined(v, g) for v, g in zip(normed_next, got[1:])]
    outer_parts += [[a, b] for a, b in zip(outer_mines, got[1 + len(twos) :])]
    got = steps.run([(twin_send, mine)] + [(second_round, v) for v in twos], 1)
    normed_parts = [[mine, got[0]]]
    mines = [rows_joined(v, g) for v, g in zip(twos, got[1:])]
    if mines:
        got = steps.run([(twin_send, v) for v in mines], 1)
        normed_parts += [[a, b] for a, b in zip(mines, got)]
    steps.drain(lambda: False)
    gate_up_all = join(
        [part for part, _, _ in gate_up_parts], [layer * 2 + n for _, layer, n in gate_up_parts]
    )
    down_all = join([part for part, _, _ in down_parts], [p * 4 + n for _, p, n in down_parts])

    def feed_half(values):
        return feed(*values, gate_up_all, down_all)

    order = [(j, side) for j in reversed(range(pair)) for side in (1, 0)]
    results = {}
    waiting = []
    sums = {}

    def advance():
        return [(function, values) for function, values, _ in waiting]

    def settle(got):
        nonlocal waiting
        ongoing, waiting = waiting, []
        for (_, _, then), value in zip(ongoing, got):
            then(value)

    def reduce_start(j, mine, other):
        def ended(kept):
            def end(value):
                sums[j] = kept.astype(f32) + value.astype(f32)
                if j:
                    waiting.append(
                        (
                            lambda v: pair_send(v, j, pair),
                            sums[j].astype(bf16),
                            lambda value: sums.__setitem__(j, value.astype(f32)),
                        )
                    )

            return end

        def second(kept):
            def end(value):
                now, sent = reduce_second(kept, value)
                waiting.append((first_round, sent, ended(now)))

            return end

        def end(value):
            now, sent = reduce_first(mine(), value)
            waiting.append((second_round, sent, second(now)))

        waiting.append((twin_send, other, end))

    for j, side in order:
        ready = (normed_parts[j][side], outer_parts[j][side])
        result, *got = steps.run([(feed_half, ready)] + advance())
        results[j, side] = result
        settle(got)
        if side:
            reduce_start(j, lambda j=j: results[j, 0][2], result[2])
    keys = [(j, side) for j in range(pair) for side in range(2)]
    normed_flat = [normed_parts[j][side] for j, side in keys]
    outer_flat = [outer_parts[j][side] for j, side in keys]

    class PairTotal:
        def __init__(self, rows_of, operands, count=4):
            self.rows_of, self.operands, self.count = rows_of, operands, count
            self.pieces, self.got, self.left = None, [], count * (pair_count - 1)
            self.jobs = [
                (functools.partial(self.start, step, n), self.got.append)
                for step in range(1, pair_count)
                for n in range(count)
            ]

        def others(self):
            return (
                lambda v: [
                    self.rows_of(v, (pair_here + step) % pair_count) for step in range(1, pair_count)
                ],
                self.operands,
            )

        def own(self):
            return (lambda v: self.rows_of(v, pair_here), self.operands)

        def start(self, step, n, begin):
            if self.pieces is None:
                function, operands = self.others()
                self.pieces = function(operands)
            return fsdp_send(begin(self.pieces[step - 1][n]), step * pair)

        def complete(self):
            return len(self.got) == self.left

        def total(self, mine):
            steps.drain(self.complete)
            rows_here = [part.astype(f32) for part in mine]
            for k, value in enumerate(self.got):
                rows_here[k % self.count] += value.astype(f32)
            return join([cell_sum(part).astype(bf16) for part in rows_here])

    def side_total(side):
        return PairTotal(
            lambda v, p: weight_grad(*v, p, pair_rows, side, local_units, 4),
            (normed_flat, [results[k][1] for k in keys]),
        )

    gate, up = side_total(0), side_total(1)
    down = PairTotal(
        lambda v, p: weight_grad(*v, p, unit, 0, width, 4),
        ([results[k][0] for k in keys], outer_flat),
    )

    def shares_sent(total):
        return [
            pair_send(block(total, (in_pair + j) % pair, weight_rows), j, pair)
            for j in range(1, pair)
        ]

    def shares(total, got):
        return jnp.concatenate([block(total, in_pair, weight_rows)] + got, axis=1)

    branch_terms = [tuple(results[j, side][3] for side in range(2)) for j in range(pair)]
    branch_twins = []
    steps.jobs = gate.jobs + up.jobs + down.jobs
    kernels = [gate.others(), gate.own()]
    made = []
    while waiting or len(branch_twins) < pair:
        parts = advance()
        count = len(parts)
        extra = []
        if len(branch_twins) < pair:
            extra.append((twin_send, branch_terms[pair - 1 - len(branch_twins)][1]))
        if kernels:
            extra.append(kernels.pop(0))
        got = steps.run(parts + extra, 1 if made else 0)
        settle(got[:count])
        got = got[count:]
        if len(branch_twins) < pair:
            branch_twins.append(got.pop(0))
        if got:
            made.append(got[0])
            gate.pieces = made[0]
    normed_grad = sum(sums[j] for j in range(pair))
    mid_part, mlp_gain_grad = jax.vjp(rms_scale, hidden_mid, mlp_gain)[1](normed_grad)
    hidden_grad = cotangent.astype(f32) + mid_part
    branch_own = hidden_grad.astype(bf16)
    branch_twins = branch_twins[::-1]
    got = steps.run(
        [
            (first_round, branch_own),
            up.others(),
            (
                lambda v: [reduce_first(mine, value) for mine, value in v],
                [(terms[0], value) for terms, value in zip(branch_terms, branch_twins)],
            ),
        ]
        + kernels,
        1,
    )
    made += got[3:]
    gate_mine = made[1]
    up.pieces = got[1]
    branch_kept, branch_sent = map(list, zip(*got[2]))
    two = rows_joined(branch_own, got[0])
    got = steps.run([(second_round, two), up.own()], 1)
    up_mine = got[1]
    mine = rows_joined(two, got[0])
    got = steps.run([(twin_send, mine), (second_round, branch_sent[-1]), down.others()], 1)
    branch_grad = [mine, got[0]]
    branch_kept[-1], branch_sent[-1] = reduce_second(branch_kept[-1], got[1])
    down.pieces = got[2]
    gate_total = gate.total(gate_mine)

    def attention_half(other, kv_grad=None):
        return lambda v: attention_grad(
            place, query_low, v, attended[other], log_total, out_rows, kv_all, rows, chunk, other, kv_grad
        )

    (query_grad_mine, kv_grad), gate_got, *got = steps.run(
        [
            (attention_half(0), branch_grad[0]),
            (shares_sent, gate_total),
            (
                lambda v: sum(dot(half, branch, TN) for half, branch in zip(*v)).astype(bf16),
                (attended, branch_grad),
            ),
        ]
        + [(second_round, sent) for sent in branch_sent[:-1]],
        2,
    )
    out_partial, *got = got
    gate_share = shares(gate_total, gate_got)
    for j, value in enumerate(got):
        branch_kept[j], branch_sent[j] = reduce_second(branch_kept[j], value)
    (query_grad_other, kv_grad), gate_got, *branch_got = steps.run(
        [(attention_half(1, kv_grad), branch_grad[1]), (first_round, gate_share)]
        + [(first_round, sent) for sent in branch_sent],
        2,
    )
    gate_two = rows_joined(gate_share, gate_got)
    branch_sums = [
        kept.astype(f32) + value.astype(f32) for kept, value in zip(branch_kept, branch_got)
    ]
    outputs = hidden_mid + branch_sums[0]
    query_grad = (query_grad_mine, query_grad_other)
    kv_grad = kv_grad.astype(bf16)
    if cell_count > 1:
        kv_grad_cell = block(kv_grad, cell, CELL * chunk).astype(f32)
        for step in range(1, cell_count):
            piece = block(kv_grad, (cell + step) % cell_count, CELL * chunk)
            kv_grad_cell = kv_grad_cell + cell_send(piece, step).astype(f32)
        kv_grad = kv_grad_cell.astype(bf16)
    kv_grad = kv_grad.reshape(CELL, fsdp_count, rows, 2 * HEAD_DIM)

    def kv_piece(k):
        at = -k % fsdp_count
        return lax.slice_in_dim(kv_grad, at, at + 1, axis=1)

    def fsdp_piece(values, k):
        return block(values, (fsdp_here + k) % fsdp_count, weight_rows)

    up_total = up.total(up_mine)

    def send_then_share(v):
        got = sends[1](v[0])
        return got, shares_sent(after(v[1], got))

    (kv_next, up_got), *got = steps.run(
        [(send_then_share, (kv_piece(1), up_total))]
        + [(sends[k], kv_piece(k)) for k in range(2, fsdp_count)]
        + [(second_round, gate_two)]
    )
    kv_total = kv_piece(0).astype(f32) + kv_next.astype(f32)
    for value in got[:-1]:
        kv_total = kv_total + value.astype(f32)
    kv_total = kv_total.reshape(cell_tokens, 2 * HEAD_DIM)
    gate_got = got[-1]
    up_share = shares(up_total, up_got)

    projected, gate_two_twin, up_got, out_partial, *branch_got = steps.run(
        [
            (
                lambda v: project_grad(
                    place, *normed_attn, angles, gains, qkv_rows, query_grad, v, qkv_pieces, rows
                ),
                kv_total,
            ),
            (twin_send, gate_two),
            (first_round, up_share),
            (lambda v: cell_turn(v, 1, 0), out_partial),
        ]
        + [
            (lambda v, j=j: pair_send(v, j, pair), value.astype(bf16))
            for j, value in enumerate(branch_sums[1:], 1)
        ],
        2,
    )
    *qkv_grad, attn_mine, attn_other, head_gain_grad, attention_gain_grad = projected
    up_two = rows_joined(up_share, up_got)
    gains_here = SumEverywhere(jnp.concatenate(
        [
            attention_gain_grad[0] / attention_gain,
            mlp_gain_grad,
            head_gain_grad[0],
            head_gain_grad[1],
        ]
    ).reshape(-1, 2 * HEAD_DIM))

    def gather_place(side, slot, part, whole):
        return place_units(
            whole,
            gate_up_weight.shape,
            part,
            weight_rows,
            unit,
            place,
            lambda i, g, at: (
                side * (hidden_width // unit)
                + ((g % pair_count) * pair + (at[3] - g // pair_count + pair) % pair) * CELL
                + token_block(slot + i, at)
            ),
        )

    def placing(side, parts):
        def place_all(v):
            whole, arrays = v
            for (slot, _), array in zip(parts, arrays):
                whole = gather_place(side, slot, array, whole)
            return whole

        return place_all, (grad_gate_up, [part for _, part in parts])

    def fsdp_sum(values, got):
        total = fsdp_piece(values, 0).astype(f32)
        for value in got:
            total = total + value.astype(f32)
        return cell_sum(total).astype(bf16)

    def sent_pieces(values, distances):
        return [(sends[k], fsdp_piece(values, k)) for k in distances]

    odd_steps, even_steps = range(1, fsdp_count, 2), range(2, fsdp_count, 2)
    grad_gate_up = None
    got = steps.run(
        [
            (twin_send, attn_other),
            (second_round, up_two),
            (
                lambda v: sum(dot(half, grad, TN) for half, grad in zip(*v)).astype(bf16),
                (normed_attn, qkv_grad),
            ),
            down.own(),
            (lambda v: gather_place(0, 0, v, None), gate_two),
            gains_here.part(),
        ],
        2,
    )
    kept, sent = reduce_first(attn_mine, got[0])
    up_got = got[1]
    qkv_partial, down_own_rows, grad_gate_up, gain_got = got[2:]
    gains_here.add(gain_got)
    down_share = down.total(down_own_rows)
    got = steps.run(
        [
            (second_round, sent),
            (first_round, down_share),
            (twin_send, gate_got),
            placing(0, [(4, gate_two_twin), (2, gate_got)]),
        ]
        + sent_pieces(qkv_partial, odd_steps)
    )
    kept, sent = reduce_second(kept, got[0])
    down_two = rows_joined(down_share, got[1])
    gate_got_twin = got[2]
    grad_gate_up = got[3]
    qkv_got = got[4:]
    got = steps.run(
        [
            (first_round, sent),
            (second_round, down_two),
            placing(0, [(6, gate_got_twin)]),
        ]
        + sent_pieces(qkv_partial, even_steps)
        + sent_pieces(out_partial, odd_steps)
    )
    attn_normed_grad = kept.astype(f32) + got[0].astype(f32)
    down_got = got[1]
    grad_gate_up = got[2]
    qkv_share = fsdp_sum(qkv_partial, qkv_got + got[3 : 3 + len(even_steps)])
    out_got = got[3 + len(even_steps) :]
    got = steps.run(
        [
            (first_round, qkv_share),
            (twin_send, up_two),
            (twin_send, up_got),
            placing(1, [(0, up_two), (2, up_got)]),
            gains_here.part(),
        ]
        + sent_pieces(out_partial, even_steps)
    )
    qkv_two = rows_joined(qkv_share, got[0])
    up_two_twin, up_got_twin, grad_gate_up = got[1:4]
    gains_here.add(got[4])
    out_share = fsdp_sum(out_partial, out_got + got[5:])
    got = steps.run(
        [
            (second_round, qkv_two),
            (first_round, out_share),
            (twin_send, down_two),
            (twin_send, down_got),
            placing(1, [(4, up_two_twin), (6, up_got_twin)]),
            (
                lambda v: (
                    v[1] + jax.vjp(lambda u: rms_scale(u, attention_gain), source)[1](v[0])[0]
                ).astype(bf16),
                (attn_normed_grad, hidden_grad),
            ),
            gains_here.part(),
            (
                lambda v: sum([g.astype(f32) for g in v[1:]], v[0]).astype(bf16),
                [outputs] + branch_got,
            ),
        ]
    )
    qkv_half = rows_joined(qkv_two, got[0])
    out_two = rows_joined(out_share, got[1])
    down_two_twin, down_got_twin, grad_gate_up, grad_inputs, gain_got, outputs = got[2:]
    gains_here.add(gain_got)
    got = steps.run(
        [
            gains_here.part(),
            (second_round, out_two),
            (twin_send, qkv_half),
            (
                lambda v: place_rows(v, place),
                [down_two, down_got, down_two_twin, down_got_twin],
            ),
        ]
    )
    gains_here.add(got[0])
    got = got[1:]
    out_half = rows_joined(out_two, got[0])
    grad_down = got[2]
    got = steps.run(
        [
            gains_here.part(),
            (twin_send, out_half),
            (lambda v: place_heads(v, place), (qkv_half, got[1])),
        ]
    )
    gains_here.add(got[0])
    gain_sums = gains_here.finish().reshape(-1)
    got = got[1:]
    grad_qkv = got[1]
    grad_out = place_columns((out_half, got[0]), width // CELL, place)
    attention_gain_sum, mlp_gain_sum = gain_sums[:width], gain_sums[width : 2 * width]
    head_sums = gain_sums[2 * width :].reshape(4, HEAD_DIM)

    gain_sums = (
        attention_gain_sum,
        head_sums[0] + head_sums[1],
        head_sums[2],
        mlp_gain_sum,
    )

    return (
        outputs,
        grad_inputs,
        gain_sums[0],
        grad_qkv,
        gain_sums[1],
        gain_sums[2],
        grad_out,
        gain_sums[3],
        grad_gate_up,
        grad_down,
    )


def solution(mesh):
    return jax.shard_map(
        body,
        mesh=mesh,
        in_specs=(
            P(("ctx", "fsdp"), None),
            P(),
            P("fsdp", None),
            P(),
            P(),
            P("fsdp", None),
            P(),
            P("fsdp", None),
            P("fsdp", None),
            P(("ctx", "fsdp"), None),
        ),
        out_specs=(
            P(("ctx", "fsdp"), None),
            P(("ctx", "fsdp"), None),
            P(),
            P("fsdp", None),
            P(),
            P(),
            P("fsdp", None),
            P(),
            P("fsdp", None),
            P("fsdp", None),
        ),
        check_vma=False,
    )
```

```python
import functools

import jax
import jax.numpy as jnp
from jax import lax
from jax.experimental import pallas as pl
from jax.experimental.pallas import tpu as pltpu
from jax.sharding import PartitionSpec as P

HEADS = 32
KV_HEADS = 8
HEAD_DIM = 64
GROUP = HEADS // KV_HEADS
GROUP_WIDTH = GROUP * HEAD_DIM

epsilon = 1e-05
theta = 1000000.0
score_scale = HEAD_DIM ** (-0.5)

f32 = jnp.float32
bf16 = jnp.bfloat16

CELL = KV_HEADS

NN = (((1,), (0,)), ((), ()))
NT = (((1,), (1,)), ((), ()))
TN = (((0,), (0,)), ((), ()))


def dot(left, right, dims=NN):
    return lax.dot_general(left, right, dims, preferred_element_type=f32)


def rms_scale(values, gain):
    return values * lax.rsqrt(jnp.mean(values * values, axis=-1, keepdims=True) + epsilon) * gain


def xor_send(values, distance):
    count = lax.axis_size("ctx")
    return lax.ppermute(values, "ctx", [(i, i ^ distance) for i in range(count)])


def cell_send(values, step):
    count = lax.axis_size("ctx")
    return lax.ppermute(values, "ctx", [(i, (i + step * CELL) % count) for i in range(count)])


def fsdp_send(values, step):
    count = lax.axis_size("fsdp")
    return lax.ppermute(values, "fsdp", [(i, (i + step) % count) for i in range(count)])


def pair_send(values, step, pair):
    count = lax.axis_size("fsdp")
    return lax.ppermute(
        values, "fsdp", [(i, i // pair * pair + (i % pair + step) % pair) for i in range(count)]
    )


def fsdp_relay(shard):
    count = lax.axis_size("fsdp")
    return [shard] + [fsdp_send(shard, step) for step in range(1, count)]


def fsdp_collect(piece_for):
    count = lax.axis_size("fsdp")
    total = piece_for(0).astype(f32)
    for step in range(1, count):
        total = total + fsdp_send(piece_for(step), step).astype(f32)
    return total


def round_send(values, odd_round):
    count = lax.axis_size("ctx")
    pairs = []
    for i in range(count):
        pairs.append((i, i ^ (2 if i % 2 == odd_round else 4)))
    return lax.ppermute(values, "ctx", pairs)


def add_low(left, right):
    return (left.astype(f32) + right.astype(f32)).astype(bf16)


def after(values, event):
    return lax.optimization_barrier((values, event))[0]


class Steps:
    def __init__(self):
        self.event = None
        self.jobs = []

    def begin(self, values):
        return values if self.event is None else after(values, self.event)

    def run(self, parts, spare=0):
        jobs, self.jobs = self.jobs[:spare], self.jobs[spare:]
        early = [start(self.begin) for start, _ in jobs]
        results = [function(self.begin(values)) for function, values in parts]
        early, results = lax.optimization_barrier((early, results))
        for (_, finish), value in zip(jobs, early):
            finish(value)
        self.event = results[0]
        return results

    def drain(self, done):
        while self.jobs and not done():
            self.run([(lambda v: v, self.event)], 2)


def first_round(values):
    return round_send(values, 0)


def second_round(values):
    return round_send(values, 1)


def twin_send(values):
    return xor_send(values, 1)


def join_kernel(place_ref, *refs):
    for n, ref in enumerate(refs[:-1]):

        @pl.when(pl.program_id(0) == n)
        def _(ref=ref):
            refs[-1][...] = ref[...]


def join(parts, places=None):
    shape, dtype = parts[0].shape, parts[0].dtype
    if places is None:
        places = list(range(len(parts)))
    size = parts[0].size * 2
    return pl.pallas_call(
        join_kernel,
        grid_spec=pltpu.PrefetchScalarGridSpec(
            num_scalar_prefetch=1,
            grid=(len(parts),),
            in_specs=[pl.BlockSpec(shape, lambda i, at: (0, 0))] * len(parts),
            out_specs=pl.BlockSpec(shape, lambda i, at: (at[i], 0)),
        ),
        out_shape=jax.ShapeDtypeStruct((len(parts) * shape[0], shape[1]), dtype),
        compiler_params=pltpu.CompilerParams(
            vmem_limit_bytes=(2 * len(parts) + 2) * size + 4 * 1024 * 1024
        ),
        cost_estimate=cost(0, 2 * size * len(parts)),
    )(jnp.stack([jnp.asarray(p, jnp.int32) for p in places]), *parts)


def rows_joined(*parts):
    return join(parts)


def add_kernel(left_ref, right_ref, first_ref, second_ref):
    total = (left_ref[...].astype(f32) + right_ref[...].astype(f32)).astype(bf16)

    @pl.when(pl.program_id(0) == 0)
    def _():
        first_ref[...] = total

    @pl.when(pl.program_id(0) == 1)
    def _():
        second_ref[...] = total


def add_halves(left, right):
    rows, columns = left.shape
    half = jax.ShapeDtypeStruct((rows // 2, columns), bf16)
    in_spec = pl.BlockSpec((rows // 2, columns), lambda i: (i, 0))
    out_spec = pl.BlockSpec((rows // 2, columns), lambda i: (0, 0))
    return pl.pallas_call(
        add_kernel,
        grid=(2,),
        in_specs=[in_spec] * 2,
        out_specs=[out_spec] * 2,
        out_shape=[half, half],
        compiler_params=pltpu.CompilerParams(vmem_limit_bytes=20 * 1024 * 1024),
        cost_estimate=cost(left.size, 6 * left.size),
    )(left, right)


def reduce_first(mine, from_twin):
    return add_halves(mine, from_twin)


def reduce_second(kept, received):
    return add_halves(kept, received)


class SumEverywhere:
    def __init__(self, values):
        self.total = values
        self.rounds = []
        for axis in ("ctx", "fsdp"):
            count = lax.axis_size(axis)
            if count & (count - 1):
                self.rounds.append(functools.partial(self.whole, axis))
                continue
            distance = 1
            while distance < count:
                self.rounds.append(functools.partial(self.exchange, axis, count, distance))
                distance *= 2

    def exchange(self, axis, count, distance, values):
        return lax.ppermute(values, axis, [(i, i ^ distance) for i in range(count)])

    def whole(self, axis, values):
        return lax.psum(values, axis) - values

    def part(self):
        return (self.rounds.pop(0), self.total)

    def add(self, got):
        self.total = self.total + got

    def finish(self):
        while self.rounds:
            function, values = self.part()
            self.add(function(values))
        return self.total


def blank(shape, dtype):
    return pl.pallas_call(
        lambda ref: None,
        out_specs=pl.BlockSpec(memory_space=pl.ANY),
        out_shape=jax.ShapeDtypeStruct(shape, dtype),
        cost_estimate=pl.CostEstimate(flops=0, bytes_accessed=0, transcendentals=0),
    )()


def vmem(mebibytes, keys=0):
    return pltpu.CompilerParams(vmem_limit_bytes=mebibytes * 1024 * 1024 + keys * 2560)


def cost(flops, moved, transcendentals=0):
    return pl.CostEstimate(
        flops=int(flops), bytes_accessed=int(moved), transcendentals=int(transcendentals)
    )


def own(i, place):
    slot = i % 4
    other = i // 4
    swapped = (place[2] + other) % 2
    return slot // 2 * (4 - 2 * swapped) + slot % 2 * (2 + 2 * swapped) + other


def token_block(i, place):
    return jnp.bitwise_xor(own(i, place), place[2])


def even_block(i):
    return jnp.minimum(i, 3)


def odd_block(i):
    return jnp.maximum(i - 4, 0)


def swap_halves(values):
    lane = lax.broadcasted_iota(jnp.int32, values.shape, 1) % HEAD_DIM
    return jnp.where(
        lane < HEAD_DIM // 2,
        pltpu.roll(values, values.shape[1] - HEAD_DIM // 2, 1),
        pltpu.roll(values, HEAD_DIM // 2, 1),
    )


def head_mean(values):
    first = lax.broadcasted_iota(jnp.int32, values.shape, 1) < HEAD_DIM
    low = jnp.sum(jnp.where(first, values, 0.0), axis=1, keepdims=True)
    high = jnp.sum(jnp.where(first, 0.0, values), axis=1, keepdims=True)
    return jnp.where(first, low, high) * (1.0 / HEAD_DIM)


def project_kernel(fsdp_count, place_ref, even_ref, odd_ref, angle_ref, gain_ref, *refs):
    weight_refs, (rows_ref, q_ref, kv_ref) = refs[:fsdp_count], refs[fsdp_count:]
    depth = weight_refs[0].shape[0]

    def project(left_ref):
        total = None
        for step in range(fsdp_count):
            owner = lax.rem(place_ref[0] - step + fsdp_count, fsdp_count)
            left = left_ref[:, pl.ds(pl.multiple_of(owner * depth, depth), depth)]
            term = dot(left, weight_refs[step][...])
            total = term if total is None else total + term
        rows_ref[...] = total

    @pl.when(pl.program_id(0) < 4)
    def _():
        project(even_ref)

    @pl.when(pl.program_id(0) >= 4)
    def _():
        project(odd_ref)

    cosine = angle_ref[:, : 2 * HEAD_DIM]
    sine = angle_ref[:, 2 * HEAD_DIM :]
    wide = 2 * HEAD_DIM
    for group in range(GROUP_WIDTH // wide + 1):
        values = rows_ref[:, group * wide : (group + 1) * wide]
        last = group == GROUP_WIDTH // wide
        normed = values * lax.rsqrt(head_mean(values * values) + epsilon)
        normed = normed * gain_ref[int(last) : int(last) + 1, :]
        turned = normed * cosine + swap_halves(normed) * sine
        if last:
            lane = lax.broadcasted_iota(jnp.int32, values.shape, 1)
            kv_ref[...] = jnp.where(lane < HEAD_DIM, turned, values).astype(bf16)
        else:
            q_ref[:, group * wide : (group + 1) * wide] = turned.astype(bf16)


def project(place, even, odd, angles, gains, weights, rows):
    count = CELL
    fsdp_count = len(weights)
    width = even.shape[1]
    columns = weights[0].shape[1]
    return pl.pallas_call(
        functools.partial(project_kernel, fsdp_count),
        grid_spec=pltpu.PrefetchScalarGridSpec(
            num_scalar_prefetch=1,
            grid=(count,),
            in_specs=[
                pl.BlockSpec((rows, width), lambda i, place: (even_block(i), 0)),
                pl.BlockSpec((rows, width), lambda i, place: (odd_block(i), 0)),
                pl.BlockSpec((rows, 4 * HEAD_DIM), lambda i, place: (token_block(i, place), 0)),
                pl.BlockSpec((8, 2 * HEAD_DIM), lambda i, place: (0, 0)),
            ]
            + [pl.BlockSpec(w.shape, lambda i, place: (0, 0)) for w in weights],
            out_specs=[
                pl.BlockSpec((rows, columns), lambda i, place: (token_block(i, place), 0)),
                pl.BlockSpec((rows, GROUP_WIDTH), lambda i, place: (token_block(i, place), 0)),
                pl.BlockSpec((rows, 2 * HEAD_DIM), lambda i, place: (token_block(i, place), 0)),
            ],
        ),
        out_shape=[
            jax.ShapeDtypeStruct((count * rows, columns), f32),
            jax.ShapeDtypeStruct((count * rows, GROUP_WIDTH), bf16),
            jax.ShapeDtypeStruct((count * rows, 2 * HEAD_DIM), bf16),
        ],
        compiler_params=vmem(20),
        cost_estimate=cost(2 * count * rows * width * columns, 8e6),
    )(place, even, odd, angles, gains, *weights)


def project_grad_kernel(
    fsdp_count,
    place_ref,
    even_ref,
    odd_ref,
    angle_ref,
    gain_ref,
    rows_ref,
    q_even_ref,
    q_odd_ref,
    kv_ref,
    *refs,
):
    weight_refs = refs[:fsdp_count]
    (grad_even_ref, grad_odd_ref, part_even_ref, part_odd_ref, head_gain_ref, gain_grad_ref) = refs[
        fsdp_count:
    ]
    depth = weight_refs[0].shape[0]
    step_here = pl.program_id(0)

    @pl.when(step_here == 0)
    def _():
        head_gain_ref[...] = jnp.zeros_like(head_gain_ref)
        gain_grad_ref[...] = jnp.zeros_like(gain_grad_ref)

    cosine = angle_ref[:, : 2 * HEAD_DIM]
    sine = angle_ref[:, 2 * HEAD_DIM :]
    wide = 2 * HEAD_DIM
    pieces = []
    for group in range(GROUP_WIDTH // wide + 1):
        last = group == GROUP_WIDTH // wide
        values = rows_ref[:, group * wide : (group + 1) * wide]
        at = pl.ds(group * wide, wide)
        if last:
            grad = kv_ref[...]
        else:
            grad = jnp.where(step_here < 4, q_even_ref[:, at], q_odd_ref[:, at])
        scale = lax.rsqrt(head_mean(values * values) + epsilon)
        gain = gain_ref[int(last) : int(last) + 1, :]
        unturned = grad * cosine + swap_halves(grad * sine)
        head_gain_ref[int(last) : int(last) + 1, :] += jnp.sum(
            unturned * values * scale, axis=0, keepdims=True
        )
        scaled = unturned * gain
        piece = scale * scaled - values * (scale * scale * scale) * head_mean(scaled * values)
        if last:
            lane = lax.broadcasted_iota(jnp.int32, values.shape, 1)
            piece = jnp.where(lane < HEAD_DIM, piece, grad)
        pieces.append(piece.astype(bf16))
    low = jnp.concatenate(pieces, axis=1)

    def finish(normed_ref, grad_out_ref, part_ref):
        grad_out_ref[...] = low
        for step in range(fsdp_count):
            owner = lax.rem(place_ref[0] - step + fsdp_count, fsdp_count)
            at = pl.ds(pl.multiple_of(owner * depth, depth), depth)
            part = dot(low, weight_refs[step][...], NT)
            part_ref[:, at] = part.astype(bf16)
            gain_grad_ref[0:1, at] += jnp.sum(
                part * normed_ref[:, at].astype(f32), axis=0, keepdims=True
            )

    @pl.when(step_here < 4)
    def _():
        finish(even_ref, grad_even_ref, part_even_ref)

    @pl.when(step_here >= 4)
    def _():
        finish(odd_ref, grad_odd_ref, part_odd_ref)


def project_grad(place, even, odd, angles, gains, qkv_rows, query_grad, kv_grad, weights, rows):
    count = CELL
    fsdp_count = len(weights)
    width = even.shape[1]
    columns = weights[0].shape[1]

    def by_token(size):
        return pl.BlockSpec((rows, size), lambda i, place: (token_block(i, place), 0))

    def halves(size):
        return [
            pl.BlockSpec((rows, size), lambda i, place: (even_block(i), 0)),
            pl.BlockSpec((rows, size), lambda i, place: (odd_block(i), 0)),
        ]

    return pl.pallas_call(
        functools.partial(project_grad_kernel, fsdp_count),
        grid_spec=pltpu.PrefetchScalarGridSpec(
            num_scalar_prefetch=1,
            grid=(count,),
            in_specs=halves(width)
            + [
                by_token(4 * HEAD_DIM),
                pl.BlockSpec((8, 2 * HEAD_DIM), lambda i, place: (0, 0)),
                by_token(columns),
                *halves(GROUP_WIDTH),
                by_token(2 * HEAD_DIM),
            ]
            + [pl.BlockSpec(w.shape, lambda i, place: (0, 0)) for w in weights],
            out_specs=halves(columns)
            + halves(width)
            + [
                pl.BlockSpec((8, 2 * HEAD_DIM), lambda i, place: (0, 0)),
                pl.BlockSpec((8, width), lambda i, place: (0, 0)),
            ],
        ),
        out_shape=[
            jax.ShapeDtypeStruct((4 * rows, columns), bf16),
            jax.ShapeDtypeStruct((4 * rows, columns), bf16),
            jax.ShapeDtypeStruct((4 * rows, width), bf16),
            jax.ShapeDtypeStruct((4 * rows, width), bf16),
            jax.ShapeDtypeStruct((8, 2 * HEAD_DIM), f32),
            jax.ShapeDtypeStruct((8, width), f32),
        ],
        compiler_params=vmem(48),
        cost_estimate=cost(2 * count * rows * width * columns, 12e6),
    )(place, even, odd, angles, gains, qkv_rows, *query_grad, kv_grad, *weights)


def stack_heads(block):
    return jnp.concatenate(
        [block[:, i * HEAD_DIM : (i + 1) * HEAD_DIM] for i in range(GROUP)], axis=0
    )


def unstack_heads(turned, rows):
    return jnp.concatenate([turned[:, i * rows : (i + 1) * rows].T for i in range(GROUP)], axis=1)


def fill_turned(place_ref, kv_ref, turned_ref, chunk):
    @pl.when(pl.program_id(0) == 0)
    def _():
        def turn(n, _):
            start = pl.multiple_of(n * chunk, chunk)
            turned_ref[:, pl.ds(start, chunk)] = kv_ref[pl.ds(start, chunk), :].T
            return 0

        lax.fori_loop(0, (place_ref[1] + 1) * CELL, turn, 0)


def visible_keys(place_ref, chunk, rows):
    key_row = lax.broadcasted_iota(jnp.int32, (chunk, GROUP * rows), 0)
    row_at = lax.broadcasted_iota(jnp.int32, (chunk, GROUP * rows), 1) % rows
    count = chunk // rows
    owner = (place_ref[0] - key_row // rows + count) % count
    return owner * rows + key_row % rows <= row_at + place_ref[0] * rows


def attention_kernel(
    chunk, place_ref, q_ref, kv_ref, even_ref, odd_ref, log_ref, turned_ref
):
    rows = q_ref.shape[0]
    fill_turned(place_ref, kv_ref, turned_ref, chunk)
    queries = stack_heads(q_ref[...].astype(f32) * score_scale).astype(bf16)
    queries = jnp.concatenate([queries, jnp.zeros_like(queries)], axis=1)

    def step(n, running, masked):
        total, summed = running
        start = pl.multiple_of(n * chunk, chunk)
        weights = jnp.exp(dot(kv_ref[pl.ds(start, chunk), :], queries, NT))
        if masked:
            weights = jnp.where(visible_keys(place_ref, chunk, rows), weights, 0.0)
        return (
            total + jnp.sum(weights, axis=0, keepdims=True),
            summed + dot(turned_ref[:, pl.ds(start, chunk)], weights.astype(bf16)),
        )

    last = place_ref[1] * CELL + token_block(pl.program_id(0), place_ref)
    running = (
        jnp.zeros((1, GROUP * rows), f32),
        jnp.zeros((2 * HEAD_DIM, GROUP * rows), f32),
    )
    running = lax.fori_loop(0, last, lambda n, r: step(n, r, False), running)
    total, summed = step(last, running, True)
    result = unstack_heads(summed[HEAD_DIM:] / total, rows).astype(bf16)

    @pl.when(pl.program_id(0) < 4)
    def _():
        even_ref[...] = result

    @pl.when(pl.program_id(0) >= 4)
    def _():
        odd_ref[...] = result

    log_ref[...] = jnp.log(total)[None]


def attention(place, queries, keys_values, rows, chunk):
    count = queries.shape[0] // rows
    keys = keys_values.shape[0]
    half = jax.ShapeDtypeStruct((4 * rows, GROUP_WIDTH), bf16)
    return pl.pallas_call(
        functools.partial(attention_kernel, chunk),
        grid_spec=pltpu.PrefetchScalarGridSpec(
            num_scalar_prefetch=1,
            grid=(count,),
            in_specs=[
                pl.BlockSpec((rows, GROUP_WIDTH), lambda i, place: (token_block(i, place), 0)),
                pl.BlockSpec((keys, 2 * HEAD_DIM), lambda i, place: (0, 0)),
            ],
            out_specs=[
                pl.BlockSpec((rows, GROUP_WIDTH), lambda i, place: (even_block(i), 0)),
                pl.BlockSpec((rows, GROUP_WIDTH), lambda i, place: (odd_block(i), 0)),
                pl.BlockSpec((1, 1, GROUP * rows), lambda i, place: (i, 0, 0)),
            ],
            scratch_shapes=[pltpu.VMEM((2 * HEAD_DIM, keys), bf16)],
        ),
        out_shape=[half, half, jax.ShapeDtypeStruct((count, 1, GROUP * rows), f32)],
        compiler_params=vmem(12, keys),
        cost_estimate=cost(16e9, 8e6, 1e7),
    )(place, queries, keys_values)


def attention_grad_kernel(
    chunk,
    other,
    place_ref,
    q_ref,
    branch_ref,
    out_ref,
    log_ref,
    weight_ref,
    kv_ref,
    *refs,
):
    q_grad_ref, kv_grad_ref, turned_ref = refs[-3:]
    rows = q_ref.shape[0]
    fill_turned(place_ref, kv_ref, turned_ref, chunk)

    @pl.when(pl.program_id(0) == 0)
    def _():
        kv_grad_ref[...] = refs[0][...] if other else jnp.zeros_like(kv_grad_ref)

    queries = stack_heads(q_ref[...].astype(f32) * score_scale).astype(bf16)
    queries = jnp.concatenate([queries, jnp.zeros_like(queries)], axis=1)
    out_grad = dot(branch_ref[...], weight_ref[...], NT).astype(bf16)
    grads = stack_heads(out_grad)
    attended = stack_heads(out_ref[...]).astype(f32)
    row_delta = jnp.sum((grads.astype(f32) * attended).T, axis=0, keepdims=True)
    grads = jnp.concatenate([jnp.zeros_like(grads), grads], axis=1)
    log_total = log_ref[0]

    def step(n, summed, masked):
        start = pl.multiple_of(n * chunk, chunk)
        block = kv_ref[pl.ds(start, chunk), :]
        weights = jnp.exp(dot(block, queries, NT) - log_total)
        if masked:
            weights = jnp.where(visible_keys(place_ref, chunk, rows), weights, 0.0)
        score_grad = (weights * (dot(block, grads, NT) - row_delta)).astype(bf16)
        kv_grad_ref[pl.ds(start, chunk), :] += dot(score_grad, queries) + dot(
            weights.astype(bf16), grads
        )
        return summed + dot(turned_ref[:, pl.ds(start, chunk)], score_grad)

    last = place_ref[1] * CELL + token_block(pl.program_id(0) + 4 * other, place_ref)
    summed = jnp.zeros((2 * HEAD_DIM, GROUP * rows), f32)
    summed = lax.fori_loop(0, last, lambda n, r: step(n, r, False), summed)
    summed = step(last, summed, True)
    q_grad_ref[...] = unstack_heads(summed[:HEAD_DIM] * score_scale, rows)


def attention_grad(
    place, queries, branch, attended, log_total, weight, keys_values, rows, chunk, other, kv_grad=None
):
    keys = keys_values.shape[0]
    width = weight.shape[1]
    whole_spec = pl.BlockSpec((keys, 2 * HEAD_DIM), lambda i, place: (0, 0))
    added = [] if kv_grad is None else [kv_grad]
    return pl.pallas_call(
        functools.partial(attention_grad_kernel, chunk, other),
        grid_spec=pltpu.PrefetchScalarGridSpec(
            num_scalar_prefetch=1,
            grid=(4,),
            in_specs=[
                pl.BlockSpec(
                    (rows, GROUP_WIDTH), lambda i, place: (token_block(i + 4 * other, place), 0)
                ),
                pl.BlockSpec((rows, width), lambda i, place: (i, 0)),
                pl.BlockSpec((rows, GROUP_WIDTH), lambda i, place: (i, 0)),
                pl.BlockSpec((1, 1, GROUP * rows), lambda i, place: (i + 4 * other, 0, 0)),
                pl.BlockSpec(weight.shape, lambda i, place: (0, 0)),
                whole_spec,
            ]
            + [whole_spec] * len(added),
            out_specs=[
                pl.BlockSpec((rows, GROUP_WIDTH), lambda i, place: (i, 0)),
                whole_spec,
            ],
            scratch_shapes=[pltpu.VMEM((2 * HEAD_DIM, keys), bf16)],
        ),
        out_shape=[
            jax.ShapeDtypeStruct((4 * rows, GROUP_WIDTH), f32),
            jax.ShapeDtypeStruct(keys_values.shape, f32),
        ],
        compiler_params=vmem(18, keys),
        cost_estimate=cost(18e9, 12e6, 5e6),
    )(place, queries, branch, attended, log_total, weight, keys_values, *added)


def feed_kernel(
    normed_ref, outer_ref, weight_ref, down_ref, active_ref, gate_grad_ref, part_ref, branch_ref
):
    units = active_ref.shape[1]
    both = dot(normed_ref[...], weight_ref[...])
    gate = both[:, :units]
    up = both[:, units:]
    act_grad = dot(outer_ref[...], down_ref[...], NT)
    logistic = 1.0 / (1.0 + jnp.exp(-gate))
    silu = gate * logistic
    active_ref[...] = (silu * up).astype(bf16)
    gate_part = act_grad * up * (logistic * (1.0 + gate * (1.0 - logistic)))
    gate_grad_ref[:, :units] = gate_part.astype(bf16)
    gate_grad_ref[:, units:] = (act_grad * silu).astype(bf16)
    part_ref[...] = dot(gate_grad_ref[...], weight_ref[...], NT).astype(bf16)
    branch_ref[...] = dot(active_ref[...], down_ref[...]).astype(bf16)


def feed(normed, outer, weight, down):
    tokens, width = normed.shape
    columns = weight.shape[1]
    rows = 256 if tokens % 256 == 0 else tokens

    def by_row(size):
        return pl.BlockSpec((rows, size), lambda i: (i, 0))

    def low(size):
        return jax.ShapeDtypeStruct((tokens, size), bf16)

    return pl.pallas_call(
        feed_kernel,
        grid=(tokens // rows,),
        in_specs=[
            by_row(width),
            by_row(width),
            pl.BlockSpec(weight.shape, lambda i: (0, 0)),
            pl.BlockSpec(down.shape, lambda i: (0, 0)),
        ],
        out_specs=[by_row(columns // 2), by_row(columns), by_row(width), by_row(width)],
        out_shape=[low(columns // 2), low(columns), low(width), low(width)],
        compiler_params=vmem(36),
        cost_estimate=cost(6 * tokens * width * columns, 16e6, tokens * columns),
    )(normed, outer, weight, down)


def weight_grad_kernel(count, place_ref, *refs):
    total = None
    for left_ref, right_ref in zip(refs[:count], refs[count : 2 * count]):
        term = dot(left_ref[...], right_ref[...], TN)
        total = term if total is None else total + term
    for n, ref in enumerate(refs[2 * count :]):

        @pl.when(pl.program_id(0) == n)
        def _(ref=ref):
            ref[...] = total.astype(bf16)


def weight_grad(lefts, rights, first, size, column, columns, count):
    tokens = lefts[0].shape[0]
    tile = size // count
    place = jnp.stack([first * count]).astype(jnp.int32)
    if tile % 128:
        tile, place = size, jnp.stack([first]).astype(jnp.int32)
    parts = size // tile
    made = pl.pallas_call(
        functools.partial(weight_grad_kernel, len(lefts)),
        grid_spec=pltpu.PrefetchScalarGridSpec(
            num_scalar_prefetch=1,
            grid=(parts,),
            in_specs=[pl.BlockSpec((tokens, tile), lambda i, at: (0, at[0] + i))] * len(lefts)
            + [pl.BlockSpec((tokens, columns), lambda i, at: (0, column))] * len(rights),
            out_specs=[pl.BlockSpec((tile, columns), lambda i, at: (0, 0))] * parts,
        ),
        out_shape=[jax.ShapeDtypeStruct((tile, columns), bf16)] * parts,
        compiler_params=vmem(36),
        cost_estimate=cost(2 * len(lefts) * tokens * size * columns, 12e6),
    )(place, *lefts, *rights)
    if parts == count:
        return list(made)
    return [lax.slice_in_dim(made[0], n * size // count, (n + 1) * size // count) for n in range(count)]


def norm_grad_kernel(hidden_ref, outer_ref, gain_ref, *refs):
    terms, (low_ref, grad_ref, gain_grad_ref) = refs[:-3], refs[-3:]
    normed_grad = terms[0][...]
    for term in terms[1:]:
        normed_grad = normed_grad + term[...]
    hidden = hidden_ref[...]
    scale = lax.rsqrt(jnp.mean(hidden * hidden, axis=1, keepdims=True) + epsilon)
    scaled = normed_grad * gain_ref[...]
    along = jnp.mean(scaled * hidden, axis=1, keepdims=True)
    grad = outer_ref[...].astype(f32) + scale * scaled - hidden * (scale * scale * scale * along)
    grad_ref[...] = grad
    low_ref[...] = grad.astype(bf16)

    @pl.when(pl.program_id(0) == 0)
    def _():
        gain_grad_ref[...] = jnp.zeros_like(gain_grad_ref)

    gain_grad_ref[0:1, :] += jnp.sum(normed_grad * hidden * scale, axis=0, keepdims=True)


def norm_grad(hidden, outer, gain, terms):
    tokens, width = hidden.shape
    rows = tokens // 4
    by_row = pl.BlockSpec((rows, width), lambda i: (i, 0))
    return pl.pallas_call(
        norm_grad_kernel,
        grid=(4,),
        in_specs=[by_row, by_row, pl.BlockSpec((1, width), lambda i: (0, 0))] + [by_row] * len(terms),
        out_specs=[by_row, by_row, pl.BlockSpec((8, width), lambda i: (0, 0))],
        out_shape=[
            jax.ShapeDtypeStruct((tokens, width), bf16),
            jax.ShapeDtypeStruct((tokens, width), f32),
            jax.ShapeDtypeStruct((8, width), f32),
        ],
        compiler_params=vmem(16),
        cost_estimate=cost(20 * tokens * width, 5e6),
    )(hidden, outer, gain[None, :], *terms)


def place_units_kernel(block_at, unit, columns, place_ref, source_ref, *refs):
    out_ref, wide_ref, sems = refs[-3:]
    rows = wide_ref.shape[1]
    copies = []
    for n in range(wide_ref.shape[0]):
        slot, column = n // columns, n % columns
        wide_ref[n] = source_ref[
            slot * rows : (slot + 1) * rows, column * unit : (column + 1) * unit
        ].astype(f32)
        start = pl.multiple_of(block_at(slot, column, place_ref) * unit, unit)
        copies.append(
            pltpu.make_async_copy(wide_ref.at[n], out_ref.at[:, pl.ds(start, unit)], sems.at[n])
        )
        copies[-1].start()
    for copy in copies:
        copy.wait()


def place_units(whole, shape, source, rows, unit, place, block_at):
    slots, columns = source.shape[0] // rows, source.shape[1] // unit
    count = slots * columns
    in_specs = [pl.BlockSpec(source.shape, lambda i, at: (0, 0))]
    operands = [place, source]
    aliases = {}
    if whole is not None:
        in_specs.append(pl.BlockSpec(memory_space=pl.ANY))
        operands.append(whole)
        aliases = {2: 0}
    return pl.pallas_call(
        functools.partial(place_units_kernel, block_at, unit, columns),
        grid_spec=pltpu.PrefetchScalarGridSpec(
            num_scalar_prefetch=1,
            grid=(1,),
            in_specs=in_specs,
            out_specs=pl.BlockSpec(memory_space=pl.ANY),
            scratch_shapes=[
                pltpu.VMEM((count, rows, unit), f32),
                pltpu.SemaphoreType.DMA((count,)),
            ],
        ),
        out_shape=jax.ShapeDtypeStruct(shape, f32),
        input_output_aliases=aliases,
        compiler_params=vmem(16),
        cost_estimate=cost(0, 6 * source.size),
    )(*operands)


def place_columns(halves, unit, place):
    whole = None
    rows = halves[0].shape[0] // 4
    for odd, half in enumerate(halves):
        whole = place_units(
            whole,
            (rows, CELL * unit),
            half,
            rows,
            unit,
            place,
            lambda slot, column, at, odd=odd: token_block(4 * odd + slot, at),
        )
    return whole


def place_rows_kernel(slot, place_ref, source_ref, *refs):
    out_ref, wide_ref, sems = refs[-3:]
    rows = wide_ref.shape[1]
    copies = []
    for n in range(wide_ref.shape[0]):
        wide_ref[n] = source_ref[n * rows : (n + 1) * rows].astype(f32)
        start = pl.multiple_of(token_block(slot + n, place_ref) * rows, rows)
        copies.append(
            pltpu.make_async_copy(wide_ref.at[n], out_ref.at[pl.ds(start, rows)], sems.at[n])
        )
        copies[-1].start()
    for copy in copies:
        copy.wait()


def place_rows(quarters, place):
    whole = None
    rows, columns = quarters[0].shape[0] // 2, quarters[0].shape[1]
    for n, quarter in enumerate(quarters):
        extra = [] if whole is None else [whole]
        whole = pl.pallas_call(
            functools.partial(place_rows_kernel, 2 * n),
            grid_spec=pltpu.PrefetchScalarGridSpec(
                num_scalar_prefetch=1,
                grid=(1,),
                in_specs=[pl.BlockSpec(quarter.shape, lambda i, at: (0, 0))]
                + [pl.BlockSpec(memory_space=pl.ANY)] * len(extra),
                out_specs=pl.BlockSpec(memory_space=pl.ANY),
                scratch_shapes=[
                    pltpu.VMEM((2, rows, columns), f32),
                    pltpu.SemaphoreType.DMA((2,)),
                ],
            ),
            out_shape=jax.ShapeDtypeStruct((CELL * rows, columns), f32),
            input_output_aliases={2: 0} if extra else {},
            compiler_params=vmem(16),
            cost_estimate=cost(0, 6 * quarter.size),
        )(place, quarter, *extra)
    return whole


def place_heads_kernel(place_ref, even_ref, odd_ref, out_ref):
    query_width = HEADS * HEAD_DIM
    key_width = KV_HEADS * HEAD_DIM
    even = even_ref[...].astype(f32)
    odd = odd_ref[...].astype(f32)
    first = lax.rem(place_ref[2], 2) == 0
    low = jnp.where(first, even, odd)
    high = jnp.where(first, odd, even)
    twins = token_block(pl.program_id(0), place_ref) // 2

    def at(start, size):
        return pl.ds(pl.multiple_of(start + twins * size, 128), size)

    out_ref[:, at(0, 2 * GROUP_WIDTH)] = jnp.concatenate(
        [low[:, :GROUP_WIDTH], high[:, :GROUP_WIDTH]], axis=1
    )
    middle = GROUP_WIDTH + HEAD_DIM
    out_ref[:, at(query_width, 2 * HEAD_DIM)] = jnp.concatenate(
        [low[:, GROUP_WIDTH:middle], high[:, GROUP_WIDTH:middle]], axis=1
    )
    out_ref[:, at(query_width + key_width, 2 * HEAD_DIM)] = jnp.concatenate(
        [low[:, middle:], high[:, middle:]], axis=1
    )


def place_heads(halves, place):
    rows, columns = halves[0].shape[0] // 4, halves[0].shape[1]
    shape = (rows, CELL * columns)
    return pl.pallas_call(
        place_heads_kernel,
        grid_spec=pltpu.PrefetchScalarGridSpec(
            num_scalar_prefetch=1,
            grid=(4,),
            in_specs=[
                pl.BlockSpec((rows, columns), lambda i, at: (i, 0)),
                pl.BlockSpec((rows, columns), lambda i, at: (i % 2 * 2 + i // 2, 0)),
            ],
            out_specs=pl.BlockSpec(shape, lambda i, at: (0, 0)),
        ),
        out_shape=jax.ShapeDtypeStruct(shape, f32),
        compiler_params=vmem(28),
        cost_estimate=cost(0, 6 * rows * CELL * columns),
    )(place, *halves)


def body(
    inputs,
    attention_gain,
    qkv_weight,
    query_gain,
    key_gain,
    out_weight,
    mlp_gain,
    gate_up_weight,
    down_weight,
    cotangent,
):
    rows, width = inputs.shape
    fsdp_count = lax.axis_size("fsdp")
    cell_count = lax.axis_size("ctx") // CELL
    pair = 2 if fsdp_count % 2 == 0 else 1
    pair_count = fsdp_count // pair
    fsdp_here = lax.axis_index("fsdp")
    ctx_here = lax.axis_index("ctx")
    head = ctx_here % CELL
    cell = ctx_here // CELL
    in_pair = fsdp_here % pair
    pair_here = fsdp_here // pair
    weight_rows = qkv_weight.shape[0]
    query_width = HEADS * HEAD_DIM
    key_width = KV_HEADS * HEAD_DIM
    hidden_width = gate_up_weight.shape[1] // 2
    unit = hidden_width // (fsdp_count * CELL)
    place = jnp.stack([fsdp_here, cell, head, in_pair]).astype(jnp.int32)

    def block(values, index, size, axis=0):
        return lax.dynamic_slice_in_dim(values, index * size, size, axis)

    def put(whole, part, index, axis=0):
        return lax.dynamic_update_slice_in_dim(whole, part, index * part.shape[axis], axis)

    def cell_sum(values):
        total = values.astype(f32)
        for step in range(1, cell_count):
            total = total + cell_send(values.astype(bf16), step).astype(f32)
        return total

    def cell_turn(values, split_axis, join_axis):
        groups = None
        if cell_count > 1:
            groups = [[c * CELL + i for i in range(CELL)] for c in range(cell_count)]
        return lax.all_to_all(
            values, "ctx", split_axis, join_axis, axis_index_groups=groups, tiled=True
        )

    blocks_here = cell * CELL + jnp.arange(CELL, dtype=jnp.int32)
    positions = (
        ((blocks_here * fsdp_count + fsdp_here) * rows)[:, None]
        + jnp.arange(rows, dtype=jnp.int32)[None, :]
    ).reshape(-1)
    cell_tokens = CELL * rows
    half_dim = HEAD_DIM // 2
    frequency = theta ** (-jnp.arange(half_dim, dtype=f32) * 2.0 / HEAD_DIM)

    def angle_table(here):
        turns = here.astype(f32)[:, None] * frequency[None, :]
        cosine = jnp.cos(turns)
        sine = jnp.sin(turns)
        return jnp.concatenate([cosine] * 4 + [-sine, sine] * 2, axis=1)

    gains = jnp.concatenate(
        [
            jnp.tile(query_gain, 2)[None, :],
            jnp.concatenate([key_gain, jnp.ones_like(key_gain)])[None, :],
            jnp.zeros((6, 2 * HEAD_DIM), f32),
        ],
        axis=0,
    )

    source = inputs.astype(f32)
    normed_attn_own = rms_scale(source, attention_gain).astype(bf16)
    def head_columns(start):
        both = lax.dynamic_slice_in_dim(
            qkv_weight, start + head // 2 * (2 * HEAD_DIM), 2 * HEAD_DIM, 1
        )
        return jnp.where(head % 2 == 0, both[:, :HEAD_DIM], both[:, HEAD_DIM:])

    qkv_own = jnp.concatenate(
        [
            block(qkv_weight, head, GROUP_WIDTH, 1),
            head_columns(query_width),
            head_columns(query_width + key_width),
        ],
        axis=1,
    )
    out_own = block(out_weight, head, width // CELL, 1)
    local_units = pair_count * unit
    pair_rows = pair * weight_rows

    def owner_columns(weight, owner):
        return jnp.concatenate(
            [
                lax.dynamic_slice_in_dim(
                    weight,
                    side * hidden_width + ((p * pair + owner) * CELL + head) * unit,
                    unit,
                    1,
                )
                for side in range(2)
                for p in range(pair_count)
            ],
            axis=1,
        )

    steps = Steps()
    sends = [functools.partial(fsdp_send, step=k) for k in range(fsdp_count)]

    pair_jobs, down_jobs, own_jobs, mate_jobs = [], [], [], []
    gate_up_parts, down_parts = [], []

    def half_columns(weight, owner, n):
        size = weight_rows // 2
        return owner_columns(lax.slice_in_dim(weight, n * size, (n + 1) * size), owner)

    def cross_job(read, step, row):
        return (
            lambda begin: fsdp_send(begin(read()), step * pair),
            lambda got: gate_up_parts.append((got, (fsdp_here - step * pair) % fsdp_count, row)),
        )

    mates = {}

    def mate_job(j, n):
        def finish(got):
            mates[j, n] = got
            gate_up_parts.append((got, pair_here * pair + (in_pair - j) % pair, n))

        return (lambda begin: pair_send(begin(owned[j, n]), j, pair), finish)

    def mate_cross_job(j, n, step):
        def finish(got):
            layer = (pair_here - step) % pair_count * pair + (in_pair - j) % pair
            gate_up_parts.append((got, layer, n))

        return (lambda begin: fsdp_send(begin(mates[j, n]), step * pair), finish)

    def down_job(step, n):
        return (
            lambda begin: fsdp_send(begin(down_pieces[n]), step * pair),
            lambda got: down_parts.append((got, (pair_here - step) % pair_count, n)),
        )

    for n in range(2):
        for j in range(1, pair):
            pair_jobs.append(mate_job(j, n))
        for step in range(1, pair_count):
            own_jobs.append(cross_job(lambda n=n: owned[0, n], step, n))
            for j in range(1, pair):
                mate_jobs.append(mate_cross_job(j, n, step))
    for n in range(4):
        for step in range(1, pair_count):
            down_jobs.append(down_job(step, n))

    last = max(fsdp_count - 1, 3)
    got = steps.run(
        [(first_round, normed_attn_own), (angle_table, positions)]
        + [(send, qkv_own) for send in sends[1:2]]
    )
    angles = got[1]
    qkv_pieces = [qkv_own] + got[2:]
    two = rows_joined(normed_attn_own, got[0])
    got = steps.run(
        [
            (second_round, two),
            (
                lambda v: (
                    {
                        (j, n): half_columns(v[0], (in_pair + j) % pair, n)
                        for j in range(pair)
                        for n in range(2)
                    },
                    [
                        lax.dynamic_slice_in_dim(
                            v[1], head * unit + n * (unit // 4), unit // 4
                        )
                        for n in range(4)
                    ],
                ),
                (gate_up_weight, down_weight),
            ),
        ]
        + [(send, qkv_own) for send in sends[2:last]]
    )
    owned, down_pieces = got[1]
    for n in range(2):
        gate_up_parts.append((owned[0, n], fsdp_here, n))
    for n in range(4):
        down_parts.append((down_pieces[n], pair_here, n))
    qkv_pieces += got[2:]
    mine = rows_joined(two, got[0])
    got = steps.run([(twin_send, mine)] + [(send, qkv_own) for send in sends[last:]])
    qkv_pieces += got[1:]
    normed_attn = [mine, got[0]]

    queue = [pair_jobs, pair_jobs, own_jobs, down_jobs, own_jobs, down_jobs, down_jobs]
    for jobs in queue + [mate_jobs, down_jobs, mate_jobs]:
        if jobs:
            steps.jobs.append(jobs.pop(0))
    steps.jobs += pair_jobs + down_jobs + own_jobs + mate_jobs

    projected, outer_got, *out_got = steps.run(
        [
            (lambda v: project(place, *v, angles, gains, qkv_pieces, rows), normed_attn),
            (first_round, cotangent),
        ]
        + [(send, out_own) for send in sends[1:]],
        1,
    )
    qkv_rows, query_low, kv_own = projected
    outer_two = rows_joined(cotangent, outer_got)
    kv_own = kv_own.reshape(CELL, 1, rows, 2 * HEAD_DIM)
    out_columns = join([out_own] + out_got, [(fsdp_here - k) % fsdp_count for k in range(fsdp_count)])

    def send_then_turn(split_axis, join_axis):
        def act(v):
            got = sends[1](v[0])
            return got, cell_turn(after(v[1], got), split_axis, join_axis)

        return act

    (kv_next, out_rows), *got = steps.run(
        [(send_then_turn(0, 1), (kv_own, out_columns))]
        + [(send, kv_own) for send in sends[2:]]
        + [(second_round, outer_two)],
        1,
    )
    kv_pieces = [kv_own, kv_next] + got[:-1]
    outer_mine = rows_joined(outer_two, got[-1])
    kv_cells = jnp.concatenate(kv_pieces, axis=1)
    chunk = fsdp_count * rows
    kv_all = kv_cells.reshape(CELL * chunk, 2 * HEAD_DIM)
    if cell_count > 1:
        kv_cells = kv_all
        kv_all = put(
            blank((cell_count * CELL * chunk, 2 * HEAD_DIM), bf16), kv_cells, cell
        )
        for step in range(1, cell_count):
            kv_all = put(kv_all, cell_send(kv_cells, step), (cell - step) % cell_count)

    attended, outer_other, *outer_next = steps.run(
        [
            (lambda v: attention(place, *v, rows, chunk), (query_low, kv_all)),
            (twin_send, outer_mine),
        ]
        + [(lambda v, j=j: pair_send(v, -j, pair), cotangent) for j in range(1, pair)],
        1,
    )
    *attended, log_total = attended
    outer_parts = [[outer_mine, outer_other]]
    terms = [dot(half, out_rows).astype(bf16) for half in attended]
    got = steps.run([(twin_send, terms[1])] + [(first_round, shard) for shard in outer_next], 1)
    outer_twos = [rows_joined(shard, g) for shard, g in zip(outer_next, got[1:])]
    kept, sent = reduce_first(terms[0], got[0])
    got = steps.run([(second_round, sent)] + [(second_round, v) for v in outer_twos], 1)
    outer_mines = [rows_joined(v, g) for v, g in zip(outer_twos, got[1:])]
    kept, sent = reduce_second(kept, got[0])
    got = steps.run([(first_round, sent)] + [(twin_send, v) for v in outer_mines], 1)
    outer_parts += [[a, b] for a, b in zip(outer_mines, got[1:])]
    hidden_mid = source + kept.astype(f32) + got[0].astype(f32)
    normed_own = rms_scale(hidden_mid, mlp_gain).astype(bf16)

    got = steps.run(
        [(first_round, normed_own)]
        + [(lambda v, j=j: pair_send(v, -j, pair), normed_own) for j in range(1, pair)],
        1,
    )
    two = rows_joined(normed_own, got[0])
    normed_next = got[1:]
    got = steps.run([(second_round, two)] + [(first_round, v) for v in normed_next], 1)
    mine = rows_joined(two, got[0])
    twos = [rows_joined(v, g) for v, g in zip(normed_next, got[1:])]
    got = steps.run([(twin_send, mine)] + [(second_round, v) for v in twos], 1)
    normed_parts = [[mine, got[0]]]
    mines = [rows_joined(v, g) for v, g in zip(twos, got[1:])]
    if mines:
        got = steps.run([(twin_send, v) for v in mines], 1)
        normed_parts += [[a, b] for a, b in zip(mines, got)]
    steps.drain(lambda: False)
    gate_up_all = join(
        [part for part, _, _ in gate_up_parts], [layer * 2 + n for _, layer, n in gate_up_parts]
    )
    down_all = join([part for part, _, _ in down_parts], [p * 4 + n for _, p, n in down_parts])

    def feed_half(values):
        return feed(*values, gate_up_all, down_all)

    order = [(j, side) for j in reversed(range(pair)) for side in (1, 0)]
    results = {}
    waiting = []
    sums = {}

    def advance():
        return [(function, values) for function, values, _ in waiting]

    def settle(got):
        nonlocal waiting
        ongoing, waiting = waiting, []
        for (_, _, then), value in zip(ongoing, got):
            then(value)

    def reduce_start(j, mine, other):
        def ended(kept):
            def end(value):
                sums[j] = kept.astype(f32) + value.astype(f32)
                if j:
                    waiting.append(
                        (
                            lambda v: pair_send(v, j, pair),
                            sums[j].astype(bf16),
                            lambda value: sums.__setitem__(j, value.astype(f32)),
                        )
                    )

            return end

        def second(kept):
            def end(value):
                now, sent = reduce_second(kept, value)
                waiting.append((first_round, sent, ended(now)))

            return end

        def end(value):
            now, sent = reduce_first(mine(), value)
            waiting.append((second_round, sent, second(now)))

        waiting.append((twin_send, other, end))

    for j, side in order:
        ready = (normed_parts[j][side], outer_parts[j][side])
        result, *got = steps.run([(feed_half, ready)] + advance())
        results[j, side] = result
        settle(got)
        if side:
            reduce_start(j, lambda j=j: results[j, 0][2], result[2])
    keys = [(j, side) for j in range(pair) for side in range(2)]
    normed_flat = [normed_parts[j][side] for j, side in keys]
    outer_flat = [outer_parts[j][side] for j, side in keys]

    class PairTotal:
        def __init__(self, rows_of, operands, count):
            self.rows_of, self.operands, self.count = rows_of, operands, count
            self.pieces, self.got, self.left = None, [], count * (pair_count - 1)
            self.jobs = [
                (functools.partial(self.start, step, n), self.got.append)
                for step in range(1, pair_count)
                for n in range(count)
            ]

        def others(self):
            return (
                lambda v: [
                    self.rows_of(v, (pair_here + step) % pair_count) for step in range(1, pair_count)
                ],
                self.operands,
            )

        def own(self):
            return (lambda v: self.rows_of(v, pair_here), self.operands)

        def start(self, step, n, begin):
            if self.pieces is None:
                function, operands = self.others()
                self.pieces = function(operands)
            return fsdp_send(begin(self.pieces[step - 1][n]), step * pair)

        def complete(self):
            return len(self.got) == self.left

        def total(self, mine):
            steps.drain(self.complete)
            rows_here = [part.astype(f32) for part in mine]
            for k, value in enumerate(self.got):
                rows_here[k % self.count] += value.astype(f32)
            return join([cell_sum(part).astype(bf16) for part in rows_here])

    def side_total(side, count):
        return PairTotal(
            lambda v, p: weight_grad(*v, p, pair_rows, side, local_units, count),
            (normed_flat, [results[k][1] for k in keys]),
            count,
        )

    gate, up = side_total(0, 4), side_total(1, 2)
    down = PairTotal(
        lambda v, p: weight_grad(*v, p, unit, 0, width, 2),
        ([results[k][0] for k in keys], outer_flat),
        2,
    )

    def shares_sent(total):
        return [
            pair_send(block(total, (in_pair + j) % pair, weight_rows), j, pair)
            for j in range(1, pair)
        ]

    def shares(total, got):
        return jnp.concatenate([block(total, in_pair, weight_rows)] + got, axis=1)

    branch_terms = [tuple(results[j, side][3] for side in range(2)) for j in range(pair)]
    branch_twins = []
    steps.jobs = gate.jobs + up.jobs + down.jobs
    kernels = [gate.others(), gate.own()]
    made = []
    while waiting or len(branch_twins) < pair:
        parts = advance()
        count = len(parts)
        extra = []
        if len(branch_twins) < pair:
            extra.append((twin_send, branch_terms[pair - 1 - len(branch_twins)][1]))
        if kernels:
            extra.append(kernels.pop(0))
        got = steps.run(parts + extra, 1 if made else 0)
        settle(got[:count])
        got = got[count:]
        if len(branch_twins) < pair:
            branch_twins.append(got.pop(0))
        if got:
            made.append(got[0])
            gate.pieces = made[0]
    branch_own, hidden_grad, mlp_gain_grad = norm_grad(
        hidden_mid, cotangent, mlp_gain, [sums[j] for j in range(pair)]
    )
    mlp_gain_grad = mlp_gain_grad[0]
    branch_twins = branch_twins[::-1]
    got = steps.run(
        [
            (first_round, branch_own),
            up.others(),
            (
                lambda v: [reduce_first(mine, value) for mine, value in v],
                [(terms[0], value) for terms, value in zip(branch_terms, branch_twins)],
            ),
        ]
        + kernels,
        1,
    )
    made += got[3:]
    gate_mine = made[1]
    up.pieces = got[1]
    branch_kept, branch_sent = map(list, zip(*got[2]))
    two = rows_joined(branch_own, got[0])
    got = steps.run([(second_round, two), up.own()], 1)
    up_mine = got[1]
    mine = rows_joined(two, got[0])
    got = steps.run([(twin_send, mine), (second_round, branch_sent[-1]), down.others()], 1)
    branch_grad = [mine, got[0]]
    branch_kept[-1], branch_sent[-1] = reduce_second(branch_kept[-1], got[1])
    down.pieces = got[2]
    gate_total = gate.total(gate_mine)

    def attention_half(other, kv_grad=None):
        return lambda v: attention_grad(
            place, query_low, v, attended[other], log_total, out_rows, kv_all, rows, chunk, other, kv_grad
        )

    (query_grad_mine, kv_grad), gate_got, *got = steps.run(
        [
            (attention_half(0), branch_grad[0]),
            (shares_sent, gate_total),
        ]
        + [(second_round, sent) for sent in branch_sent[:-1]],
        1,
    )
    gate_share = shares(gate_total, gate_got)
    for j, value in enumerate(got):
        branch_kept[j], branch_sent[j] = reduce_second(branch_kept[j], value)
    (query_grad_other, kv_grad), gate_got, *branch_got = steps.run(
        [(attention_half(1, kv_grad), branch_grad[1]), (first_round, gate_share)]
        + [(first_round, sent) for sent in branch_sent],
        1,
    )
    gate_two = rows_joined(gate_share, gate_got)
    branch_sums = [
        kept.astype(f32) + value.astype(f32) for kept, value in zip(branch_kept, branch_got)
    ]
    outputs = hidden_mid + branch_sums[0]
    query_grad = (query_grad_mine, query_grad_other)
    kv_grad = kv_grad.astype(bf16)
    if cell_count > 1:
        kv_grad_cell = block(kv_grad, cell, CELL * chunk).astype(f32)
        for step in range(1, cell_count):
            piece = block(kv_grad, (cell + step) % cell_count, CELL * chunk)
            kv_grad_cell = kv_grad_cell + cell_send(piece, step).astype(f32)
        kv_grad = kv_grad_cell.astype(bf16)
    kv_grad = kv_grad.reshape(CELL, fsdp_count, rows, 2 * HEAD_DIM)

    def kv_piece(k):
        at = -k % fsdp_count
        return lax.slice_in_dim(kv_grad, at, at + 1, axis=1)

    def fsdp_piece(values, k):
        return block(values, (fsdp_here + k) % fsdp_count, weight_rows)

    up_total = up.total(up_mine)

    def send_then_share(v):
        got = sends[1](v[0])
        return got, shares_sent(after(v[1], got))

    (kv_next, up_got), *got = steps.run(
        [(send_then_share, (kv_piece(1), up_total))]
        + [(sends[k], kv_piece(k)) for k in range(2, fsdp_count)]
        + [
            (second_round, gate_two),
            (
                lambda v: sum(dot(half, branch, TN) for half, branch in zip(*v)).astype(bf16),
                (attended, branch_grad),
            ),
        ]
    )
    out_partial = got.pop()
    kv_total = kv_piece(0).astype(f32) + kv_next.astype(f32)
    for value in got[:-1]:
        kv_total = kv_total + value.astype(f32)
    kv_total = kv_total.reshape(cell_tokens, 2 * HEAD_DIM)
    gate_got = got[-1]
    up_share = shares(up_total, up_got)

    projected, gate_two_twin, up_got, out_partial, *branch_got = steps.run(
        [
            (
                lambda v: project_grad(
                    place, *normed_attn, angles, gains, qkv_rows, query_grad, v, qkv_pieces, rows
                ),
                kv_total,
            ),
            (twin_send, gate_two),
            (first_round, up_share),
            (lambda v: cell_turn(v, 1, 0), out_partial),
        ]
        + [
            (lambda v, j=j: pair_send(v, j, pair), value.astype(bf16))
            for j, value in enumerate(branch_sums[1:], 1)
        ],
        1,
    )
    *qkv_grad, attn_mine, attn_other, head_gain_grad, attention_gain_grad = projected
    up_two = rows_joined(up_share, up_got)
    gains_here = SumEverywhere(jnp.concatenate(
        [
            attention_gain_grad[0] / attention_gain,
            mlp_gain_grad,
            head_gain_grad[0],
            head_gain_grad[1],
        ]
    ).reshape(-1, 2 * HEAD_DIM))

    def gather_place(side, slot, part, whole):
        return place_units(
            whole,
            gate_up_weight.shape,
            part,
            weight_rows,
            unit,
            place,
            lambda i, g, at: (
                side * (hidden_width // unit)
                + ((g % pair_count) * pair + (at[3] - g // pair_count + pair) % pair) * CELL
                + token_block(slot + i, at)
            ),
        )

    def placing(side, parts):
        def place_all(v):
            whole, arrays = v
            for (slot, _), array in zip(parts, arrays):
                whole = gather_place(side, slot, array, whole)
            return whole

        return place_all, (grad_gate_up, [part for _, part in parts])

    def fsdp_sum(values, got):
        total = fsdp_piece(values, 0).astype(f32)
        for value in got:
            total = total + value.astype(f32)
        return cell_sum(total).astype(bf16)

    def sent_pieces(values, distances):
        return [(sends[k], fsdp_piece(values, k)) for k in distances]

    odd_steps, even_steps = range(1, fsdp_count, 2), range(2, fsdp_count, 2)
    grad_gate_up = None
    got = steps.run(
        [
            (twin_send, attn_other),
            (second_round, up_two),
            (
                lambda v: sum(dot(half, grad, TN) for half, grad in zip(*v)).astype(bf16),
                (normed_attn, qkv_grad),
            ),
            down.own(),
            (lambda v: gather_place(0, 0, v, None), gate_two),
            gains_here.part(),
        ],
        1,
    )
    kept, sent = reduce_first(attn_mine, got[0])
    up_got = got[1]
    qkv_partial, down_own_rows, grad_gate_up, gain_got = got[2:]
    gains_here.add(gain_got)
    down_share = down.total(down_own_rows)
    got = steps.run(
        [
            (second_round, sent),
            (first_round, down_share),
            (twin_send, gate_got),
            placing(0, [(4, gate_two_twin), (2, gate_got)]),
        ]
        + sent_pieces(qkv_partial, odd_steps)
    )
    kept, sent = reduce_second(kept, got[0])
    down_two = rows_joined(down_share, got[1])
    gate_got_twin = got[2]
    grad_gate_up = got[3]
    qkv_got = got[4:]
    got = steps.run(
        [
            (first_round, sent),
            (second_round, down_two),
            placing(0, [(6, gate_got_twin)]),
        ]
        + sent_pieces(qkv_partial, even_steps)
        + sent_pieces(out_partial, odd_steps)
    )
    attn_normed_grad = kept.astype(f32) + got[0].astype(f32)
    down_got = got[1]
    grad_gate_up = got[2]
    qkv_share = fsdp_sum(qkv_partial, qkv_got + got[3 : 3 + len(even_steps)])
    out_got = got[3 + len(even_steps) :]
    got = steps.run(
        [
            (first_round, qkv_share),
            (twin_send, up_two),
            (twin_send, up_got),
            placing(1, [(0, up_two), (2, up_got)]),
            gains_here.part(),
        ]
        + sent_pieces(out_partial, even_steps)
    )
    qkv_two = rows_joined(qkv_share, got[0])
    up_two_twin, up_got_twin, grad_gate_up = got[1:4]
    gains_here.add(got[4])
    out_share = fsdp_sum(out_partial, out_got + got[5:])
    got = steps.run(
        [
            (second_round, qkv_two),
            (first_round, out_share),
            (twin_send, down_two),
            (twin_send, down_got),
            placing(1, [(4, up_two_twin), (6, up_got_twin)]),
            (
                lambda v: (
                    v[1] + jax.vjp(lambda u: rms_scale(u, attention_gain), source)[1](v[0])[0]
                ).astype(bf16),
                (attn_normed_grad, hidden_grad),
            ),
            gains_here.part(),
            (
                lambda v: sum([g.astype(f32) for g in v[1:]], v[0]).astype(bf16),
                [outputs] + branch_got,
            ),
        ]
    )
    qkv_half = rows_joined(qkv_two, got[0])
    out_two = rows_joined(out_share, got[1])
    down_two_twin, down_got_twin, grad_gate_up, grad_inputs, gain_got, outputs = got[2:]
    gains_here.add(gain_got)
    got = steps.run(
        [
            gains_here.part(),
            (second_round, out_two),
            (twin_send, qkv_half),
            (
                lambda v: place_rows(v, place),
                [down_two, down_got, down_two_twin, down_got_twin],
            ),
        ]
    )
    gains_here.add(got[0])
    got = got[1:]
    out_half = rows_joined(out_two, got[0])
    grad_down = got[2]
    got = steps.run(
        [
            gains_here.part(),
            (twin_send, out_half),
            (lambda v: place_heads(v, place), (qkv_half, got[1])),
        ]
    )
    gains_here.add(got[0])
    gain_sums = gains_here.finish().reshape(-1)
    got = got[1:]
    grad_qkv = got[1]
    grad_out = place_columns((out_half, got[0]), width // CELL, place)
    attention_gain_sum, mlp_gain_sum = gain_sums[:width], gain_sums[width : 2 * width]
    head_sums = gain_sums[2 * width :].reshape(4, HEAD_DIM)

    gain_sums = (
        attention_gain_sum,
        head_sums[0] + head_sums[1],
        head_sums[2],
        mlp_gain_sum,
    )

    return (
        outputs,
        grad_inputs,
        gain_sums[0],
        grad_qkv,
        gain_sums[1],
        gain_sums[2],
        grad_out,
        gain_sums[3],
        grad_gate_up,
        grad_down,
    )


def solution(mesh):
    return jax.shard_map(
        body,
        mesh=mesh,
        in_specs=(
            P(("ctx", "fsdp"), None),
            P(),
            P("fsdp", None),
            P(),
            P(),
            P("fsdp", None),
            P(),
            P("fsdp", None),
            P("fsdp", None),
            P(("ctx", "fsdp"), None),
        ),
        out_specs=(
            P(("ctx", "fsdp"), None),
            P(("ctx", "fsdp"), None),
            P(),
            P("fsdp", None),
            P(),
            P(),
            P("fsdp", None),
            P(),
            P("fsdp", None),
            P("fsdp", None),
        ),
        check_vma=False,
    )
```

```python
import functools

import jax
import jax.numpy as jnp
from jax import lax
from jax.experimental import pallas as pl
from jax.experimental.pallas import tpu as pltpu
from jax.sharding import PartitionSpec as P

HEADS = 32
KV_HEADS = 8
HEAD_DIM = 64
GROUP = HEADS // KV_HEADS
GROUP_WIDTH = GROUP * HEAD_DIM

epsilon = 1e-05
theta = 1000000.0
score_scale = HEAD_DIM ** (-0.5)

f32 = jnp.float32
bf16 = jnp.bfloat16

CELL = KV_HEADS

NN = (((1,), (0,)), ((), ()))
NT = (((1,), (1,)), ((), ()))
TN = (((0,), (0,)), ((), ()))


def dot(left, right, dims=NN):
    return lax.dot_general(left, right, dims, preferred_element_type=f32)


def rms_scale(values, gain):
    return values * lax.rsqrt(jnp.mean(values * values, axis=-1, keepdims=True) + epsilon) * gain


def xor_send(values, distance):
    count = lax.axis_size("ctx")
    return lax.ppermute(values, "ctx", [(i, i ^ distance) for i in range(count)])


def cell_send(values, step):
    count = lax.axis_size("ctx")
    return lax.ppermute(values, "ctx", [(i, (i + step * CELL) % count) for i in range(count)])


def fsdp_send(values, step):
    count = lax.axis_size("fsdp")
    return lax.ppermute(values, "fsdp", [(i, (i + step) % count) for i in range(count)])


def pair_send(values, step, pair):
    count = lax.axis_size("fsdp")
    return lax.ppermute(
        values, "fsdp", [(i, i // pair * pair + (i % pair + step) % pair) for i in range(count)]
    )


def fsdp_relay(shard):
    count = lax.axis_size("fsdp")
    return [shard] + [fsdp_send(shard, step) for step in range(1, count)]


def fsdp_collect(piece_for):
    count = lax.axis_size("fsdp")
    total = piece_for(0).astype(f32)
    for step in range(1, count):
        total = total + fsdp_send(piece_for(step), step).astype(f32)
    return total


def round_send(values, odd_round):
    count = lax.axis_size("ctx")
    pairs = []
    for i in range(count):
        pairs.append((i, i ^ (2 if i % 2 == odd_round else 4)))
    return lax.ppermute(values, "ctx", pairs)


def add_low(left, right):
    return (left.astype(f32) + right.astype(f32)).astype(bf16)


def after(values, event):
    return lax.optimization_barrier((values, event))[0]


class Steps:
    def __init__(self):
        self.event = None
        self.jobs = []

    def begin(self, values):
        return values if self.event is None else after(values, self.event)

    def run(self, parts, spare=0):
        jobs, self.jobs = self.jobs[:spare], self.jobs[spare:]
        early = [start(self.begin) for start, _ in jobs]
        results = [function(self.begin(values)) for function, values in parts]
        early, results = lax.optimization_barrier((early, results))
        for (_, finish), value in zip(jobs, early):
            finish(value)
        self.event = results[0]
        return results

    def drain(self, done):
        while self.jobs and not done():
            self.run([(lambda v: v, self.event)], 2)


def first_round(values):
    return round_send(values, 0)


def second_round(values):
    return round_send(values, 1)


def twin_send(values):
    return xor_send(values, 1)


def join_kernel(place_ref, *refs):
    for n, ref in enumerate(refs[:-1]):

        @pl.when(pl.program_id(0) == n)
        def _(ref=ref):
            refs[-1][...] = ref[...]


def join(parts, places=None):
    shape, dtype = parts[0].shape, parts[0].dtype
    if places is None:
        places = list(range(len(parts)))
    size = parts[0].size * 2
    return pl.pallas_call(
        join_kernel,
        grid_spec=pltpu.PrefetchScalarGridSpec(
            num_scalar_prefetch=1,
            grid=(len(parts),),
            in_specs=[pl.BlockSpec(shape, lambda i, at: (0, 0))] * len(parts),
            out_specs=pl.BlockSpec(shape, lambda i, at: (at[i], 0)),
        ),
        out_shape=jax.ShapeDtypeStruct((len(parts) * shape[0], shape[1]), dtype),
        compiler_params=pltpu.CompilerParams(
            vmem_limit_bytes=(2 * len(parts) + 2) * size + 4 * 1024 * 1024
        ),
        cost_estimate=cost(0, 2 * size * len(parts)),
    )(jnp.stack([jnp.asarray(p, jnp.int32) for p in places]), *parts)


def rows_joined(*parts):
    return join(parts)


def add_kernel(left_ref, right_ref, first_ref, second_ref):
    total = (left_ref[...].astype(f32) + right_ref[...].astype(f32)).astype(bf16)

    @pl.when(pl.program_id(0) == 0)
    def _():
        first_ref[...] = total

    @pl.when(pl.program_id(0) == 1)
    def _():
        second_ref[...] = total


def add_halves(left, right):
    rows, columns = left.shape
    half = jax.ShapeDtypeStruct((rows // 2, columns), bf16)
    in_spec = pl.BlockSpec((rows // 2, columns), lambda i: (i, 0))
    out_spec = pl.BlockSpec((rows // 2, columns), lambda i: (0, 0))
    return pl.pallas_call(
        add_kernel,
        grid=(2,),
        in_specs=[in_spec] * 2,
        out_specs=[out_spec] * 2,
        out_shape=[half, half],
        compiler_params=pltpu.CompilerParams(vmem_limit_bytes=20 * 1024 * 1024),
        cost_estimate=cost(left.size, 6 * left.size),
    )(left, right)


def reduce_first(mine, from_twin):
    return add_halves(mine, from_twin)


def reduce_second(kept, received):
    return add_halves(kept, received)


class SumEverywhere:
    def __init__(self, values):
        self.total = values
        self.rounds = []
        for axis in ("ctx", "fsdp"):
            count = lax.axis_size(axis)
            if count & (count - 1):
                self.rounds.append(functools.partial(self.whole, axis))
                continue
            distance = 1
            while distance < count:
                self.rounds.append(functools.partial(self.exchange, axis, count, distance))
                distance *= 2

    def exchange(self, axis, count, distance, values):
        return lax.ppermute(values, axis, [(i, i ^ distance) for i in range(count)])

    def whole(self, axis, values):
        return lax.psum(values, axis) - values

    def part(self):
        return (self.rounds.pop(0), self.total)

    def add(self, got):
        self.total = self.total + got

    def finish(self):
        while self.rounds:
            function, values = self.part()
            self.add(function(values))
        return self.total


def blank(shape, dtype):
    return pl.pallas_call(
        lambda ref: None,
        out_specs=pl.BlockSpec(memory_space=pl.ANY),
        out_shape=jax.ShapeDtypeStruct(shape, dtype),
        cost_estimate=pl.CostEstimate(flops=0, bytes_accessed=0, transcendentals=0),
    )()


def vmem(mebibytes, keys=0):
    return pltpu.CompilerParams(vmem_limit_bytes=mebibytes * 1024 * 1024 + keys * 2560)


def cost(flops, moved, transcendentals=0):
    return pl.CostEstimate(
        flops=int(flops), bytes_accessed=int(moved), transcendentals=int(transcendentals)
    )


def own(i, place):
    slot = i % 4
    other = i // 4
    swapped = (place[2] + other) % 2
    return slot // 2 * (4 - 2 * swapped) + slot % 2 * (2 + 2 * swapped) + other


def token_block(i, place):
    return jnp.bitwise_xor(own(i, place), place[2])


def even_block(i):
    return jnp.minimum(i, 3)


def odd_block(i):
    return jnp.maximum(i - 4, 0)


def swap_halves(values):
    lane = lax.broadcasted_iota(jnp.int32, values.shape, 1) % HEAD_DIM
    return jnp.where(
        lane < HEAD_DIM // 2,
        pltpu.roll(values, values.shape[1] - HEAD_DIM // 2, 1),
        pltpu.roll(values, HEAD_DIM // 2, 1),
    )


def head_mean(values):
    first = lax.broadcasted_iota(jnp.int32, values.shape, 1) < HEAD_DIM
    low = jnp.sum(jnp.where(first, values, 0.0), axis=1, keepdims=True)
    high = jnp.sum(jnp.where(first, 0.0, values), axis=1, keepdims=True)
    return jnp.where(first, low, high) * (1.0 / HEAD_DIM)


def project_kernel(fsdp_count, place_ref, even_ref, odd_ref, angle_ref, gain_ref, *refs):
    weight_refs, (rows_ref, q_ref, kv_ref) = refs[:fsdp_count], refs[fsdp_count:]
    depth = weight_refs[0].shape[0]

    def project(left_ref):
        total = None
        for step in range(fsdp_count):
            owner = lax.rem(place_ref[0] - step + fsdp_count, fsdp_count)
            left = left_ref[:, pl.ds(pl.multiple_of(owner * depth, depth), depth)]
            term = dot(left, weight_refs[step][...])
            total = term if total is None else total + term
        rows_ref[...] = total

    @pl.when(pl.program_id(0) < 4)
    def _():
        project(even_ref)

    @pl.when(pl.program_id(0) >= 4)
    def _():
        project(odd_ref)

    cosine = angle_ref[:, : 2 * HEAD_DIM]
    sine = angle_ref[:, 2 * HEAD_DIM :]
    wide = 2 * HEAD_DIM
    for group in range(GROUP_WIDTH // wide + 1):
        values = rows_ref[:, group * wide : (group + 1) * wide]
        last = group == GROUP_WIDTH // wide
        normed = values * lax.rsqrt(head_mean(values * values) + epsilon)
        normed = normed * gain_ref[int(last) : int(last) + 1, :]
        turned = normed * cosine + swap_halves(normed) * sine
        if last:
            lane = lax.broadcasted_iota(jnp.int32, values.shape, 1)
            kv_ref[...] = jnp.where(lane < HEAD_DIM, turned, values).astype(bf16)
        else:
            q_ref[:, group * wide : (group + 1) * wide] = turned.astype(bf16)


def project(place, even, odd, angles, gains, weights, rows):
    count = CELL
    fsdp_count = len(weights)
    width = even.shape[1]
    columns = weights[0].shape[1]
    return pl.pallas_call(
        functools.partial(project_kernel, fsdp_count),
        grid_spec=pltpu.PrefetchScalarGridSpec(
            num_scalar_prefetch=1,
            grid=(count,),
            in_specs=[
                pl.BlockSpec((rows, width), lambda i, place: (even_block(i), 0)),
                pl.BlockSpec((rows, width), lambda i, place: (odd_block(i), 0)),
                pl.BlockSpec((rows, 4 * HEAD_DIM), lambda i, place: (token_block(i, place), 0)),
                pl.BlockSpec((8, 2 * HEAD_DIM), lambda i, place: (0, 0)),
            ]
            + [pl.BlockSpec(w.shape, lambda i, place: (0, 0)) for w in weights],
            out_specs=[
                pl.BlockSpec((rows, columns), lambda i, place: (token_block(i, place), 0)),
                pl.BlockSpec((rows, GROUP_WIDTH), lambda i, place: (token_block(i, place), 0)),
                pl.BlockSpec((rows, 2 * HEAD_DIM), lambda i, place: (token_block(i, place), 0)),
            ],
        ),
        out_shape=[
            jax.ShapeDtypeStruct((count * rows, columns), f32),
            jax.ShapeDtypeStruct((count * rows, GROUP_WIDTH), bf16),
            jax.ShapeDtypeStruct((count * rows, 2 * HEAD_DIM), bf16),
        ],
        compiler_params=vmem(20),
        cost_estimate=cost(2 * count * rows * width * columns, 8e6),
    )(place, even, odd, angles, gains, *weights)


def project_grad_kernel(
    fsdp_count,
    place_ref,
    even_ref,
    odd_ref,
    angle_ref,
    gain_ref,
    rows_ref,
    q_even_ref,
    q_odd_ref,
    kv_ref,
    *refs,
):
    weight_refs = refs[:fsdp_count]
    (grad_even_ref, grad_odd_ref, part_even_ref, part_odd_ref, head_gain_ref, gain_grad_ref) = refs[
        fsdp_count:
    ]
    depth = weight_refs[0].shape[0]
    step_here = pl.program_id(0)

    @pl.when(step_here == 0)
    def _():
        head_gain_ref[...] = jnp.zeros_like(head_gain_ref)
        gain_grad_ref[...] = jnp.zeros_like(gain_grad_ref)

    cosine = angle_ref[:, : 2 * HEAD_DIM]
    sine = angle_ref[:, 2 * HEAD_DIM :]
    wide = 2 * HEAD_DIM
    pieces = []
    for group in range(GROUP_WIDTH // wide + 1):
        last = group == GROUP_WIDTH // wide
        values = rows_ref[:, group * wide : (group + 1) * wide]
        at = pl.ds(group * wide, wide)
        if last:
            grad = kv_ref[...]
        else:
            grad = jnp.where(step_here < 4, q_even_ref[:, at], q_odd_ref[:, at])
        scale = lax.rsqrt(head_mean(values * values) + epsilon)
        gain = gain_ref[int(last) : int(last) + 1, :]
        unturned = grad * cosine + swap_halves(grad * sine)
        head_gain_ref[int(last) : int(last) + 1, :] += jnp.sum(
            unturned * values * scale, axis=0, keepdims=True
        )
        scaled = unturned * gain
        piece = scale * scaled - values * (scale * scale * scale) * head_mean(scaled * values)
        if last:
            lane = lax.broadcasted_iota(jnp.int32, values.shape, 1)
            piece = jnp.where(lane < HEAD_DIM, piece, grad)
        pieces.append(piece.astype(bf16))
    low = jnp.concatenate(pieces, axis=1)

    def finish(normed_ref, grad_out_ref, part_ref):
        grad_out_ref[...] = low
        for step in range(fsdp_count):
            owner = lax.rem(place_ref[0] - step + fsdp_count, fsdp_count)
            at = pl.ds(pl.multiple_of(owner * depth, depth), depth)
            part = dot(low, weight_refs[step][...], NT)
            part_ref[:, at] = part.astype(bf16)
            gain_grad_ref[0:1, at] += jnp.sum(
                part * normed_ref[:, at].astype(f32), axis=0, keepdims=True
            )

    @pl.when(step_here < 4)
    def _():
        finish(even_ref, grad_even_ref, part_even_ref)

    @pl.when(step_here >= 4)
    def _():
        finish(odd_ref, grad_odd_ref, part_odd_ref)


def project_grad(place, even, odd, angles, gains, qkv_rows, query_grad, kv_grad, weights, rows):
    count = CELL
    fsdp_count = len(weights)
    width = even.shape[1]
    columns = weights[0].shape[1]

    def by_token(size):
        return pl.BlockSpec((rows, size), lambda i, place: (token_block(i, place), 0))

    def halves(size):
        return [
            pl.BlockSpec((rows, size), lambda i, place: (even_block(i), 0)),
            pl.BlockSpec((rows, size), lambda i, place: (odd_block(i), 0)),
        ]

    return pl.pallas_call(
        functools.partial(project_grad_kernel, fsdp_count),
        grid_spec=pltpu.PrefetchScalarGridSpec(
            num_scalar_prefetch=1,
            grid=(count,),
            in_specs=halves(width)
            + [
                by_token(4 * HEAD_DIM),
                pl.BlockSpec((8, 2 * HEAD_DIM), lambda i, place: (0, 0)),
                by_token(columns),
                *halves(GROUP_WIDTH),
                by_token(2 * HEAD_DIM),
            ]
            + [pl.BlockSpec(w.shape, lambda i, place: (0, 0)) for w in weights],
            out_specs=halves(columns)
            + halves(width)
            + [
                pl.BlockSpec((8, 2 * HEAD_DIM), lambda i, place: (0, 0)),
                pl.BlockSpec((8, width), lambda i, place: (0, 0)),
            ],
        ),
        out_shape=[
            jax.ShapeDtypeStruct((4 * rows, columns), bf16),
            jax.ShapeDtypeStruct((4 * rows, columns), bf16),
            jax.ShapeDtypeStruct((4 * rows, width), bf16),
            jax.ShapeDtypeStruct((4 * rows, width), bf16),
            jax.ShapeDtypeStruct((8, 2 * HEAD_DIM), f32),
            jax.ShapeDtypeStruct((8, width), f32),
        ],
        compiler_params=vmem(48),
        cost_estimate=cost(2 * count * rows * width * columns, 12e6),
    )(place, even, odd, angles, gains, qkv_rows, *query_grad, kv_grad, *weights)


def stack_heads(block):
    return jnp.concatenate(
        [block[:, i * HEAD_DIM : (i + 1) * HEAD_DIM] for i in range(GROUP)], axis=0
    )


def unstack_heads(turned, rows):
    return jnp.concatenate([turned[:, i * rows : (i + 1) * rows].T for i in range(GROUP)], axis=1)


def fill_turned(place_ref, kv_ref, turned_ref, chunk):
    @pl.when(pl.program_id(0) == 0)
    def _():
        def turn(n, _):
            start = pl.multiple_of(n * chunk, chunk)
            turned_ref[:, pl.ds(start, chunk)] = kv_ref[pl.ds(start, chunk), :].T
            return 0

        lax.fori_loop(0, (place_ref[1] + 1) * CELL, turn, 0)


def visible_keys(place_ref, chunk, rows):
    key_row = lax.broadcasted_iota(jnp.int32, (chunk, GROUP * rows), 0)
    row_at = lax.broadcasted_iota(jnp.int32, (chunk, GROUP * rows), 1) % rows
    count = chunk // rows
    owner = (place_ref[0] - key_row // rows + count) % count
    return owner * rows + key_row % rows <= row_at + place_ref[0] * rows


def attention_kernel(
    chunk, place_ref, q_ref, kv_ref, even_ref, odd_ref, log_ref, turned_ref
):
    rows = q_ref.shape[0]
    fill_turned(place_ref, kv_ref, turned_ref, chunk)
    queries = stack_heads(q_ref[...].astype(f32) * score_scale).astype(bf16)
    queries = jnp.concatenate([queries, jnp.zeros_like(queries)], axis=1)

    def step(n, running, masked):
        total, summed = running
        start = pl.multiple_of(n * chunk, chunk)
        weights = jnp.exp(dot(kv_ref[pl.ds(start, chunk), :], queries, NT))
        if masked:
            weights = jnp.where(visible_keys(place_ref, chunk, rows), weights, 0.0)
        return (
            total + jnp.sum(weights, axis=0, keepdims=True),
            summed + dot(turned_ref[:, pl.ds(start, chunk)], weights.astype(bf16)),
        )

    last = place_ref[1] * CELL + token_block(pl.program_id(0), place_ref)
    running = (
        jnp.zeros((1, GROUP * rows), f32),
        jnp.zeros((2 * HEAD_DIM, GROUP * rows), f32),
    )
    running = lax.fori_loop(0, last, lambda n, r: step(n, r, False), running)
    total, summed = step(last, running, True)
    result = unstack_heads(summed[HEAD_DIM:] / total, rows).astype(bf16)

    @pl.when(pl.program_id(0) < 4)
    def _():
        even_ref[...] = result

    @pl.when(pl.program_id(0) >= 4)
    def _():
        odd_ref[...] = result

    log_ref[...] = jnp.log(total)[None]


def attention(place, queries, keys_values, rows, chunk):
    count = queries.shape[0] // rows
    keys = keys_values.shape[0]
    half = jax.ShapeDtypeStruct((4 * rows, GROUP_WIDTH), bf16)
    return pl.pallas_call(
        functools.partial(attention_kernel, chunk),
        grid_spec=pltpu.PrefetchScalarGridSpec(
            num_scalar_prefetch=1,
            grid=(count,),
            in_specs=[
                pl.BlockSpec((rows, GROUP_WIDTH), lambda i, place: (token_block(i, place), 0)),
                pl.BlockSpec((keys, 2 * HEAD_DIM), lambda i, place: (0, 0)),
            ],
            out_specs=[
                pl.BlockSpec((rows, GROUP_WIDTH), lambda i, place: (even_block(i), 0)),
                pl.BlockSpec((rows, GROUP_WIDTH), lambda i, place: (odd_block(i), 0)),
                pl.BlockSpec((1, 1, GROUP * rows), lambda i, place: (i, 0, 0)),
            ],
            scratch_shapes=[pltpu.VMEM((2 * HEAD_DIM, keys), bf16)],
        ),
        out_shape=[half, half, jax.ShapeDtypeStruct((count, 1, GROUP * rows), f32)],
        compiler_params=vmem(12, keys),
        cost_estimate=cost(16e9, 8e6, 1e7),
    )(place, queries, keys_values)


def attention_grad_kernel(
    chunk,
    other,
    place_ref,
    q_ref,
    branch_ref,
    out_ref,
    log_ref,
    weight_ref,
    kv_ref,
    *refs,
):
    q_grad_ref, kv_grad_ref, turned_ref = refs[-3:]
    rows = q_ref.shape[0]
    fill_turned(place_ref, kv_ref, turned_ref, chunk)

    @pl.when(pl.program_id(0) == 0)
    def _():
        kv_grad_ref[...] = refs[0][...] if other else jnp.zeros_like(kv_grad_ref)

    queries = stack_heads(q_ref[...].astype(f32) * score_scale).astype(bf16)
    queries = jnp.concatenate([queries, jnp.zeros_like(queries)], axis=1)
    out_grad = dot(branch_ref[...], weight_ref[...], NT).astype(bf16)
    grads = stack_heads(out_grad)
    attended = stack_heads(out_ref[...]).astype(f32)
    row_delta = jnp.sum((grads.astype(f32) * attended).T, axis=0, keepdims=True)
    grads = jnp.concatenate([jnp.zeros_like(grads), grads], axis=1)
    log_total = log_ref[0]

    def step(n, summed, masked):
        start = pl.multiple_of(n * chunk, chunk)
        block = kv_ref[pl.ds(start, chunk), :]
        weights = jnp.exp(dot(block, queries, NT) - log_total)
        if masked:
            weights = jnp.where(visible_keys(place_ref, chunk, rows), weights, 0.0)
        score_grad = (weights * (dot(block, grads, NT) - row_delta)).astype(bf16)
        kv_grad_ref[pl.ds(start, chunk), :] += dot(score_grad, queries) + dot(
            weights.astype(bf16), grads
        )
        return summed + dot(turned_ref[:, pl.ds(start, chunk)], score_grad)

    last = place_ref[1] * CELL + token_block(pl.program_id(0) + 4 * other, place_ref)
    summed = jnp.zeros((2 * HEAD_DIM, GROUP * rows), f32)
    summed = lax.fori_loop(0, last, lambda n, r: step(n, r, False), summed)
    summed = step(last, summed, True)
    q_grad_ref[...] = unstack_heads(summed[:HEAD_DIM] * score_scale, rows)


def attention_grad(
    place, queries, branch, attended, log_total, weight, keys_values, rows, chunk, other, kv_grad=None
):
    keys = keys_values.shape[0]
    width = weight.shape[1]
    whole_spec = pl.BlockSpec((keys, 2 * HEAD_DIM), lambda i, place: (0, 0))
    added = [] if kv_grad is None else [kv_grad]
    return pl.pallas_call(
        functools.partial(attention_grad_kernel, chunk, other),
        grid_spec=pltpu.PrefetchScalarGridSpec(
            num_scalar_prefetch=1,
            grid=(4,),
            in_specs=[
                pl.BlockSpec(
                    (rows, GROUP_WIDTH), lambda i, place: (token_block(i + 4 * other, place), 0)
                ),
                pl.BlockSpec((rows, width), lambda i, place: (i, 0)),
                pl.BlockSpec((rows, GROUP_WIDTH), lambda i, place: (i, 0)),
                pl.BlockSpec((1, 1, GROUP * rows), lambda i, place: (i + 4 * other, 0, 0)),
                pl.BlockSpec(weight.shape, lambda i, place: (0, 0)),
                whole_spec,
            ]
            + [whole_spec] * len(added),
            out_specs=[
                pl.BlockSpec((rows, GROUP_WIDTH), lambda i, place: (i, 0)),
                whole_spec,
            ],
            scratch_shapes=[pltpu.VMEM((2 * HEAD_DIM, keys), bf16)],
        ),
        out_shape=[
            jax.ShapeDtypeStruct((4 * rows, GROUP_WIDTH), f32),
            jax.ShapeDtypeStruct(keys_values.shape, f32),
        ],
        compiler_params=vmem(18, keys),
        cost_estimate=cost(18e9, 12e6, 5e6),
    )(place, queries, branch, attended, log_total, weight, keys_values, *added)


def feed_kernel(
    normed_ref, outer_ref, weight_ref, down_ref, active_ref, gate_grad_ref, part_ref, branch_ref
):
    units = active_ref.shape[1]
    both = dot(normed_ref[...], weight_ref[...])
    gate = both[:, :units]
    up = both[:, units:]
    act_grad = dot(outer_ref[...], down_ref[...], NT)
    logistic = 1.0 / (1.0 + jnp.exp(-gate))
    silu = gate * logistic
    active_ref[...] = (silu * up).astype(bf16)
    gate_part = act_grad * up * (logistic * (1.0 + gate * (1.0 - logistic)))
    gate_grad_ref[:, :units] = gate_part.astype(bf16)
    gate_grad_ref[:, units:] = (act_grad * silu).astype(bf16)
    part_ref[...] = dot(gate_grad_ref[...], weight_ref[...], NT).astype(bf16)
    branch_ref[...] = dot(active_ref[...], down_ref[...]).astype(bf16)


def feed(normed, outer, weight, down):
    tokens, width = normed.shape
    columns = weight.shape[1]
    rows = 256 if tokens % 256 == 0 else tokens

    def by_row(size):
        return pl.BlockSpec((rows, size), lambda i: (i, 0))

    def low(size):
        return jax.ShapeDtypeStruct((tokens, size), bf16)

    return pl.pallas_call(
        feed_kernel,
        grid=(tokens // rows,),
        in_specs=[
            by_row(width),
            by_row(width),
            pl.BlockSpec(weight.shape, lambda i: (0, 0)),
            pl.BlockSpec(down.shape, lambda i: (0, 0)),
        ],
        out_specs=[by_row(columns // 2), by_row(columns), by_row(width), by_row(width)],
        out_shape=[low(columns // 2), low(columns), low(width), low(width)],
        compiler_params=vmem(36),
        cost_estimate=cost(6 * tokens * width * columns, 16e6, tokens * columns),
    )(normed, outer, weight, down)


def weight_grad_kernel(count, place_ref, *refs):
    total = None
    for left_ref, right_ref in zip(refs[:count], refs[count : 2 * count]):
        term = dot(left_ref[...], right_ref[...], TN)
        total = term if total is None else total + term
    for n, ref in enumerate(refs[2 * count :]):

        @pl.when(pl.program_id(0) == n)
        def _(ref=ref):
            ref[...] = total.astype(bf16)


def weight_grad(lefts, rights, first, size, column, columns, count):
    tokens = lefts[0].shape[0]
    tile = size // count
    place = jnp.stack([first * count]).astype(jnp.int32)
    if tile % 128:
        tile, place = size, jnp.stack([first]).astype(jnp.int32)
    parts = size // tile
    made = pl.pallas_call(
        functools.partial(weight_grad_kernel, len(lefts)),
        grid_spec=pltpu.PrefetchScalarGridSpec(
            num_scalar_prefetch=1,
            grid=(parts,),
            in_specs=[pl.BlockSpec((tokens, tile), lambda i, at: (0, at[0] + i))] * len(lefts)
            + [pl.BlockSpec((tokens, columns), lambda i, at: (0, column))] * len(rights),
            out_specs=[pl.BlockSpec((tile, columns), lambda i, at: (0, 0))] * parts,
        ),
        out_shape=[jax.ShapeDtypeStruct((tile, columns), bf16)] * parts,
        compiler_params=vmem(36),
        cost_estimate=cost(2 * len(lefts) * tokens * size * columns, 12e6),
    )(place, *lefts, *rights)
    if parts == count:
        return list(made)
    return [lax.slice_in_dim(made[0], n * size // count, (n + 1) * size // count) for n in range(count)]


def norm_grad_kernel(hidden_ref, outer_ref, gain_ref, *refs):
    terms, (low_ref, grad_ref, gain_grad_ref) = refs[:-3], refs[-3:]
    normed_grad = terms[0][...]
    for term in terms[1:]:
        normed_grad = normed_grad + term[...]
    hidden = hidden_ref[...]
    scale = lax.rsqrt(jnp.mean(hidden * hidden, axis=1, keepdims=True) + epsilon)
    scaled = normed_grad * gain_ref[...]
    along = jnp.mean(scaled * hidden, axis=1, keepdims=True)
    grad = outer_ref[...].astype(f32) + scale * scaled - hidden * (scale * scale * scale * along)
    grad_ref[...] = grad
    low_ref[...] = grad.astype(bf16)

    @pl.when(pl.program_id(0) == 0)
    def _():
        gain_grad_ref[...] = jnp.zeros_like(gain_grad_ref)

    gain_grad_ref[0:1, :] += jnp.sum(normed_grad * hidden * scale, axis=0, keepdims=True)


def norm_grad(hidden, outer, gain, terms):
    tokens, width = hidden.shape
    rows = tokens // 4
    by_row = pl.BlockSpec((rows, width), lambda i: (i, 0))
    return pl.pallas_call(
        norm_grad_kernel,
        grid=(4,),
        in_specs=[by_row, by_row, pl.BlockSpec((1, width), lambda i: (0, 0))] + [by_row] * len(terms),
        out_specs=[by_row, by_row, pl.BlockSpec((8, width), lambda i: (0, 0))],
        out_shape=[
            jax.ShapeDtypeStruct((tokens, width), bf16),
            jax.ShapeDtypeStruct((tokens, width), f32),
            jax.ShapeDtypeStruct((8, width), f32),
        ],
        compiler_params=vmem(16),
        cost_estimate=cost(20 * tokens * width, 5e6),
    )(hidden, outer, gain[None, :], *terms)


def place_units_kernel(block_at, unit, columns, place_ref, source_ref, *refs):
    out_ref, wide_ref, sems = refs[-3:]
    rows = wide_ref.shape[1]
    copies = []
    for n in range(wide_ref.shape[0]):
        slot, column = n // columns, n % columns
        wide_ref[n] = source_ref[
            slot * rows : (slot + 1) * rows, column * unit : (column + 1) * unit
        ].astype(f32)
        start = pl.multiple_of(block_at(slot, column, place_ref) * unit, unit)
        copies.append(
            pltpu.make_async_copy(wide_ref.at[n], out_ref.at[:, pl.ds(start, unit)], sems.at[n])
        )
        copies[-1].start()
    for copy in copies:
        copy.wait()


def place_units(whole, shape, source, rows, unit, place, block_at):
    slots, columns = source.shape[0] // rows, source.shape[1] // unit
    count = slots * columns
    in_specs = [pl.BlockSpec(source.shape, lambda i, at: (0, 0))]
    operands = [place, source]
    aliases = {}
    if whole is not None:
        in_specs.append(pl.BlockSpec(memory_space=pl.ANY))
        operands.append(whole)
        aliases = {2: 0}
    return pl.pallas_call(
        functools.partial(place_units_kernel, block_at, unit, columns),
        grid_spec=pltpu.PrefetchScalarGridSpec(
            num_scalar_prefetch=1,
            grid=(1,),
            in_specs=in_specs,
            out_specs=pl.BlockSpec(memory_space=pl.ANY),
            scratch_shapes=[
                pltpu.VMEM((count, rows, unit), f32),
                pltpu.SemaphoreType.DMA((count,)),
            ],
        ),
        out_shape=jax.ShapeDtypeStruct(shape, f32),
        input_output_aliases=aliases,
        compiler_params=vmem(16),
        cost_estimate=cost(0, 6 * source.size),
    )(*operands)


def place_columns(halves, unit, place):
    whole = None
    rows = halves[0].shape[0] // 4
    for odd, half in enumerate(halves):
        whole = place_units(
            whole,
            (rows, CELL * unit),
            half,
            rows,
            unit,
            place,
            lambda slot, column, at, odd=odd: token_block(4 * odd + slot, at),
        )
    return whole


def place_rows_kernel(slot, place_ref, source_ref, *refs):
    out_ref, wide_ref, sems = refs[-3:]
    rows = wide_ref.shape[1]
    copies = []
    for n in range(wide_ref.shape[0]):
        wide_ref[n] = source_ref[n * rows : (n + 1) * rows].astype(f32)
        start = pl.multiple_of(token_block(slot + n, place_ref) * rows, rows)
        copies.append(
            pltpu.make_async_copy(wide_ref.at[n], out_ref.at[pl.ds(start, rows)], sems.at[n])
        )
        copies[-1].start()
    for copy in copies:
        copy.wait()


def place_rows(whole, slot, quarter, place):
    rows, columns = quarter.shape[0] // 2, quarter.shape[1]
    extra = [] if whole is None else [whole]
    return pl.pallas_call(
        functools.partial(place_rows_kernel, slot),
        grid_spec=pltpu.PrefetchScalarGridSpec(
            num_scalar_prefetch=1,
            grid=(1,),
            in_specs=[pl.BlockSpec(quarter.shape, lambda i, at: (0, 0))]
            + [pl.BlockSpec(memory_space=pl.ANY)] * len(extra),
            out_specs=pl.BlockSpec(memory_space=pl.ANY),
            scratch_shapes=[
                pltpu.VMEM((2, rows, columns), f32),
                pltpu.SemaphoreType.DMA((2,)),
            ],
        ),
        out_shape=jax.ShapeDtypeStruct((CELL * rows, columns), f32),
        input_output_aliases={2: 0} if extra else {},
        compiler_params=vmem(16),
        cost_estimate=cost(0, 6 * quarter.size),
    )(place, quarter, *extra)


def place_heads_kernel(place_ref, even_ref, odd_ref, out_ref):
    query_width = HEADS * HEAD_DIM
    key_width = KV_HEADS * HEAD_DIM
    even = even_ref[...].astype(f32)
    odd = odd_ref[...].astype(f32)
    first = lax.rem(place_ref[2], 2) == 0
    low = jnp.where(first, even, odd)
    high = jnp.where(first, odd, even)
    twins = token_block(pl.program_id(0), place_ref) // 2

    def at(start, size):
        return pl.ds(pl.multiple_of(start + twins * size, 128), size)

    out_ref[:, at(0, 2 * GROUP_WIDTH)] = jnp.concatenate(
        [low[:, :GROUP_WIDTH], high[:, :GROUP_WIDTH]], axis=1
    )
    middle = GROUP_WIDTH + HEAD_DIM
    out_ref[:, at(query_width, 2 * HEAD_DIM)] = jnp.concatenate(
        [low[:, GROUP_WIDTH:middle], high[:, GROUP_WIDTH:middle]], axis=1
    )
    out_ref[:, at(query_width + key_width, 2 * HEAD_DIM)] = jnp.concatenate(
        [low[:, middle:], high[:, middle:]], axis=1
    )


def place_heads(halves, place):
    rows, columns = halves[0].shape[0] // 4, halves[0].shape[1]
    shape = (rows, CELL * columns)
    return pl.pallas_call(
        place_heads_kernel,
        grid_spec=pltpu.PrefetchScalarGridSpec(
            num_scalar_prefetch=1,
            grid=(4,),
            in_specs=[
                pl.BlockSpec((rows, columns), lambda i, at: (i, 0)),
                pl.BlockSpec((rows, columns), lambda i, at: (i % 2 * 2 + i // 2, 0)),
            ],
            out_specs=pl.BlockSpec(shape, lambda i, at: (0, 0)),
        ),
        out_shape=jax.ShapeDtypeStruct(shape, f32),
        compiler_params=vmem(28),
        cost_estimate=cost(0, 6 * rows * CELL * columns),
    )(place, *halves)


def body(
    inputs,
    attention_gain,
    qkv_weight,
    query_gain,
    key_gain,
    out_weight,
    mlp_gain,
    gate_up_weight,
    down_weight,
    cotangent,
):
    rows, width = inputs.shape
    fsdp_count = lax.axis_size("fsdp")
    cell_count = lax.axis_size("ctx") // CELL
    pair = 2 if fsdp_count % 2 == 0 else 1
    pair_count = fsdp_count // pair
    fsdp_here = lax.axis_index("fsdp")
    ctx_here = lax.axis_index("ctx")
    head = ctx_here % CELL
    cell = ctx_here // CELL
    in_pair = fsdp_here % pair
    pair_here = fsdp_here // pair
    weight_rows = qkv_weight.shape[0]
    query_width = HEADS * HEAD_DIM
    key_width = KV_HEADS * HEAD_DIM
    hidden_width = gate_up_weight.shape[1] // 2
    unit = hidden_width // (fsdp_count * CELL)
    place = jnp.stack([fsdp_here, cell, head, in_pair]).astype(jnp.int32)

    def block(values, index, size, axis=0):
        return lax.dynamic_slice_in_dim(values, index * size, size, axis)

    def put(whole, part, index, axis=0):
        return lax.dynamic_update_slice_in_dim(whole, part, index * part.shape[axis], axis)

    def cell_sum(values):
        total = values.astype(f32)
        for step in range(1, cell_count):
            total = total + cell_send(values.astype(bf16), step).astype(f32)
        return total

    def cell_turn(values, split_axis, join_axis):
        groups = None
        if cell_count > 1:
            groups = [[c * CELL + i for i in range(CELL)] for c in range(cell_count)]
        return lax.all_to_all(
            values, "ctx", split_axis, join_axis, axis_index_groups=groups, tiled=True
        )

    blocks_here = cell * CELL + jnp.arange(CELL, dtype=jnp.int32)
    positions = (
        ((blocks_here * fsdp_count + fsdp_here) * rows)[:, None]
        + jnp.arange(rows, dtype=jnp.int32)[None, :]
    ).reshape(-1)
    cell_tokens = CELL * rows
    half_dim = HEAD_DIM // 2
    frequency = theta ** (-jnp.arange(half_dim, dtype=f32) * 2.0 / HEAD_DIM)

    def angle_table(here):
        turns = here.astype(f32)[:, None] * frequency[None, :]
        cosine = jnp.cos(turns)
        sine = jnp.sin(turns)
        return jnp.concatenate([cosine] * 4 + [-sine, sine] * 2, axis=1)

    gains = jnp.concatenate(
        [
            jnp.tile(query_gain, 2)[None, :],
            jnp.concatenate([key_gain, jnp.ones_like(key_gain)])[None, :],
            jnp.zeros((6, 2 * HEAD_DIM), f32),
        ],
        axis=0,
    )

    source = inputs.astype(f32)
    normed_attn_own = rms_scale(source, attention_gain).astype(bf16)
    def head_columns(start):
        both = lax.dynamic_slice_in_dim(
            qkv_weight, start + head // 2 * (2 * HEAD_DIM), 2 * HEAD_DIM, 1
        )
        return jnp.where(head % 2 == 0, both[:, :HEAD_DIM], both[:, HEAD_DIM:])

    qkv_own = jnp.concatenate(
        [
            block(qkv_weight, head, GROUP_WIDTH, 1),
            head_columns(query_width),
            head_columns(query_width + key_width),
        ],
        axis=1,
    )
    out_own = block(out_weight, head, width // CELL, 1)
    local_units = pair_count * unit
    pair_rows = pair * weight_rows

    def half_columns(weight, owner, n):
        size = weight_rows // 2
        return jnp.concatenate(
            [
                lax.dynamic_slice(
                    weight,
                    (
                        n * size,
                        side * hidden_width + ((p * pair + owner) * CELL + head) * unit,
                    ),
                    (size, unit),
                )
                for side in range(2)
                for p in range(pair_count)
            ],
            axis=1,
        )

    steps = Steps()
    sends = [functools.partial(fsdp_send, step=k) for k in range(fsdp_count)]

    pair_jobs, down_jobs, own_jobs, mate_jobs = [], [], [], []
    gate_up_parts, down_parts = [], []

    def cross_job(read, step, row):
        return (
            lambda begin: fsdp_send(begin(read()), step * pair),
            lambda got: gate_up_parts.append((got, (fsdp_here - step * pair) % fsdp_count, row)),
        )

    mates = {}

    def mate_job(j, n):
        def finish(got):
            mates[j, n] = got
            gate_up_parts.append((got, pair_here * pair + (in_pair - j) % pair, n))

        return (lambda begin: pair_send(begin(owned[j, n]), j, pair), finish)

    def mate_cross_job(j, n, step):
        def finish(got):
            layer = (pair_here - step) % pair_count * pair + (in_pair - j) % pair
            gate_up_parts.append((got, layer, n))

        return (lambda begin: fsdp_send(begin(mates[j, n]), step * pair), finish)

    def down_job(step, n):
        return (
            lambda begin: fsdp_send(begin(down_pieces[n]), step * pair),
            lambda got: down_parts.append((got, (pair_here - step) % pair_count, n)),
        )

    for n in range(2):
        for j in range(1, pair):
            pair_jobs.append(mate_job(j, n))
        for step in range(1, pair_count):
            own_jobs.append(cross_job(lambda n=n: owned[0, n], step, n))
            for j in range(1, pair):
                mate_jobs.append(mate_cross_job(j, n, step))
    for n in range(4):
        for step in range(1, pair_count):
            down_jobs.append(down_job(step, n))

    last = max(fsdp_count - 1, 3)
    got = steps.run(
        [(first_round, normed_attn_own), (angle_table, positions)]
        + [(send, qkv_own) for send in sends[1:2]]
    )
    angles = got[1]
    qkv_pieces = [qkv_own] + got[2:]
    two = rows_joined(normed_attn_own, got[0])
    got = steps.run(
        [
            (second_round, two),
            (
                lambda v: (
                    {
                        (j, n): half_columns(v[0], (in_pair + j) % pair, n)
                        for j in range(pair)
                        for n in range(2)
                    },
                    [
                        lax.dynamic_slice_in_dim(
                            v[1], head * unit + n * (unit // 4), unit // 4
                        )
                        for n in range(4)
                    ],
                ),
                (gate_up_weight, down_weight),
            ),
        ]
        + [(send, qkv_own) for send in sends[2:last]]
    )
    owned, down_pieces = got[1]
    for n in range(2):
        gate_up_parts.append((owned[0, n], fsdp_here, n))
    for n in range(4):
        down_parts.append((down_pieces[n], pair_here, n))
    qkv_pieces += got[2:]
    mine = rows_joined(two, got[0])
    got = steps.run([(twin_send, mine)] + [(send, qkv_own) for send in sends[last:]])
    qkv_pieces += got[1:]
    normed_attn = [mine, got[0]]

    queue = [pair_jobs, pair_jobs, own_jobs, down_jobs, own_jobs, down_jobs, down_jobs]
    for jobs in queue + [mate_jobs, down_jobs, mate_jobs]:
        if jobs:
            steps.jobs.append(jobs.pop(0))
    steps.jobs += pair_jobs + down_jobs + own_jobs + mate_jobs

    projected, outer_got, *out_got = steps.run(
        [
            (lambda v: project(place, *v, angles, gains, qkv_pieces, rows), normed_attn),
            (first_round, cotangent),
        ]
        + [(send, out_own) for send in sends[1:]],
        1,
    )
    qkv_rows, query_low, kv_own = projected
    outer_two = rows_joined(cotangent, outer_got)
    kv_own = kv_own.reshape(CELL, 1, rows, 2 * HEAD_DIM)
    out_columns = join([out_own] + out_got, [(fsdp_here - k) % fsdp_count for k in range(fsdp_count)])

    def send_then_turn(split_axis, join_axis):
        def act(v):
            got = sends[1](v[0])
            return got, cell_turn(after(v[1], got), split_axis, join_axis)

        return act

    (kv_next, out_rows), *got = steps.run(
        [(send_then_turn(0, 1), (kv_own, out_columns))]
        + [(send, kv_own) for send in sends[2:]]
        + [(second_round, outer_two)],
        1,
    )
    kv_pieces = [kv_own, kv_next] + got[:-1]
    outer_mine = rows_joined(outer_two, got[-1])
    kv_cells = jnp.concatenate(kv_pieces, axis=1)
    chunk = fsdp_count * rows
    kv_all = kv_cells.reshape(CELL * chunk, 2 * HEAD_DIM)
    if cell_count > 1:
        kv_cells = kv_all
        kv_all = put(
            blank((cell_count * CELL * chunk, 2 * HEAD_DIM), bf16), kv_cells, cell
        )
        for step in range(1, cell_count):
            kv_all = put(kv_all, cell_send(kv_cells, step), (cell - step) % cell_count)

    attended, outer_other, *outer_next = steps.run(
        [
            (lambda v: attention(place, *v, rows, chunk), (query_low, kv_all)),
            (twin_send, outer_mine),
        ]
        + [(lambda v, j=j: pair_send(v, -j, pair), cotangent) for j in range(1, pair)],
        1,
    )
    *attended, log_total = attended
    outer_parts = [[outer_mine, outer_other]]
    terms = [dot(half, out_rows).astype(bf16) for half in attended]
    got = steps.run([(twin_send, terms[1])] + [(first_round, shard) for shard in outer_next], 1)
    outer_twos = [rows_joined(shard, g) for shard, g in zip(outer_next, got[1:])]
    kept, sent = reduce_first(terms[0], got[0])
    got = steps.run([(second_round, sent)] + [(second_round, v) for v in outer_twos], 1)
    outer_mines = [rows_joined(v, g) for v, g in zip(outer_twos, got[1:])]
    kept, sent = reduce_second(kept, got[0])
    got = steps.run([(first_round, sent)] + [(twin_send, v) for v in outer_mines], 1)
    outer_parts += [[a, b] for a, b in zip(outer_mines, got[1:])]
    hidden_mid = source + kept.astype(f32) + got[0].astype(f32)
    normed_own = rms_scale(hidden_mid, mlp_gain).astype(bf16)

    got = steps.run(
        [(first_round, normed_own)]
        + [(lambda v, j=j: pair_send(v, -j, pair), normed_own) for j in range(1, pair)],
        1,
    )
    two = rows_joined(normed_own, got[0])
    normed_next = got[1:]
    got = steps.run([(second_round, two)] + [(first_round, v) for v in normed_next], 1)
    mine = rows_joined(two, got[0])
    twos = [rows_joined(v, g) for v, g in zip(normed_next, got[1:])]
    got = steps.run([(twin_send, mine)] + [(second_round, v) for v in twos], 1)
    normed_parts = [[mine, got[0]]]
    mines = [rows_joined(v, g) for v, g in zip(twos, got[1:])]
    if mines:
        got = steps.run([(twin_send, v) for v in mines], 1)
        normed_parts += [[a, b] for a, b in zip(mines, got)]
    steps.drain(lambda: False)
    gate_up_all = join(
        [part for part, _, _ in gate_up_parts], [layer * 2 + n for _, layer, n in gate_up_parts]
    )
    down_all = join([part for part, _, _ in down_parts], [p * 4 + n for _, p, n in down_parts])

    def feed_half(values):
        return feed(*values, gate_up_all, down_all)

    order = [(j, side) for j in reversed(range(pair)) for side in (1, 0)]
    results = {}
    waiting = []
    sums = {}

    def advance():
        return [(function, values) for function, values, _ in waiting]

    def settle(got):
        nonlocal waiting
        ongoing, waiting = waiting, []
        for (_, _, then), value in zip(ongoing, got):
            then(value)

    def reduce_start(j, mine, other):
        def ended(kept):
            def end(value):
                sums[j] = kept.astype(f32) + value.astype(f32)
                if j:
                    waiting.append(
                        (
                            lambda v: pair_send(v, j, pair),
                            sums[j].astype(bf16),
                            lambda value: sums.__setitem__(j, value.astype(f32)),
                        )
                    )

            return end

        def second(kept):
            def end(value):
                now, sent = reduce_second(kept, value)
                waiting.append((first_round, sent, ended(now)))

            return end

        def end(value):
            now, sent = reduce_first(mine(), value)
            waiting.append((second_round, sent, second(now)))

        waiting.append((twin_send, other, end))

    for j, side in order:
        ready = (normed_parts[j][side], outer_parts[j][side])
        result, *got = steps.run([(feed_half, ready)] + advance())
        results[j, side] = result
        settle(got)
        if side:
            reduce_start(j, lambda j=j: results[j, 0][2], result[2])
    keys = [(j, side) for j in range(pair) for side in range(2)]
    normed_flat = [normed_parts[j][side] for j, side in keys]
    outer_flat = [outer_parts[j][side] for j, side in keys]

    class PairTotal:
        def __init__(self, rows_of, operands, count):
            self.rows_of, self.operands, self.count = rows_of, operands, count
            self.pieces, self.got, self.left = None, [], count * (pair_count - 1)
            self.jobs = [
                (functools.partial(self.start, step, n), self.got.append)
                for step in range(1, pair_count)
                for n in range(count)
            ]

        def others(self):
            return (
                lambda v: [
                    self.rows_of(v, (pair_here + step) % pair_count) for step in range(1, pair_count)
                ],
                self.operands,
            )

        def own(self):
            return (lambda v: self.rows_of(v, pair_here), self.operands)

        def start(self, step, n, begin):
            if self.pieces is None:
                function, operands = self.others()
                self.pieces = function(operands)
            return fsdp_send(begin(self.pieces[step - 1][n]), step * pair)

        def complete(self):
            return len(self.got) == self.left

        def total(self, mine):
            steps.drain(self.complete)
            rows_here = [part.astype(f32) for part in mine]
            for k, value in enumerate(self.got):
                rows_here[k % self.count] += value.astype(f32)
            return join([cell_sum(part).astype(bf16) for part in rows_here])

    def side_total(side, count):
        return PairTotal(
            lambda v, p: weight_grad(*v, p, pair_rows, side, local_units, count),
            (normed_flat, [results[k][1] for k in keys]),
            count,
        )

    gate, up = side_total(0, 4), side_total(1, 2)
    down = PairTotal(
        lambda v, p: weight_grad(*v, p, unit, 0, width, 2),
        ([results[k][0] for k in keys], outer_flat),
        2,
    )

    def shares_sent(total):
        return [
            pair_send(block(total, (in_pair + j) % pair, weight_rows), j, pair)
            for j in range(1, pair)
        ]

    def shares(total, got):
        return jnp.concatenate([block(total, in_pair, weight_rows)] + got, axis=1)

    branch_terms = [tuple(results[j, side][3] for side in range(2)) for j in range(pair)]
    branch_twins = []
    steps.jobs = gate.jobs + up.jobs + down.jobs
    kernels = [gate.others(), gate.own()]
    made = []
    while waiting or len(branch_twins) < pair:
        parts = advance()
        count = len(parts)
        extra = []
        if len(branch_twins) < pair:
            extra.append((twin_send, branch_terms[pair - 1 - len(branch_twins)][1]))
        if kernels:
            extra.append(kernels.pop(0))
        got = steps.run(parts + extra, 1 if made else 0)
        settle(got[:count])
        got = got[count:]
        if len(branch_twins) < pair:
            branch_twins.append(got.pop(0))
        if got:
            made.append(got[0])
            gate.pieces = made[0]
    branch_own, hidden_grad, mlp_gain_grad = norm_grad(
        hidden_mid, cotangent, mlp_gain, [sums[j] for j in range(pair)]
    )
    mlp_gain_grad = mlp_gain_grad[0]
    branch_twins = branch_twins[::-1]
    got = steps.run(
        [
            (first_round, branch_own),
            up.others(),
            (
                lambda v: [reduce_first(mine, value) for mine, value in v],
                [(terms[0], value) for terms, value in zip(branch_terms, branch_twins)],
            ),
        ]
        + kernels,
        1,
    )
    made += got[3:]
    gate_mine = made[1]
    up.pieces = got[1]
    branch_kept, branch_sent = map(list, zip(*got[2]))
    two = rows_joined(branch_own, got[0])
    got = steps.run([(second_round, two), up.own()], 1)
    up_mine = got[1]
    mine = rows_joined(two, got[0])
    got = steps.run([(twin_send, mine), (second_round, branch_sent[-1]), down.others()], 1)
    branch_grad = [mine, got[0]]
    branch_kept[-1], branch_sent[-1] = reduce_second(branch_kept[-1], got[1])
    down.pieces = got[2]
    gate_total = gate.total(gate_mine)

    def attention_half(other, kv_grad=None):
        return lambda v: attention_grad(
            place, query_low, v, attended[other], log_total, out_rows, kv_all, rows, chunk, other, kv_grad
        )

    (query_grad_mine, kv_grad), gate_got, *got = steps.run(
        [
            (attention_half(0), branch_grad[0]),
            (shares_sent, gate_total),
        ]
        + [(second_round, sent) for sent in branch_sent[:-1]],
        1,
    )
    gate_share = shares(gate_total, gate_got)
    for j, value in enumerate(got):
        branch_kept[j], branch_sent[j] = reduce_second(branch_kept[j], value)
    (query_grad_other, kv_grad), gate_got, *branch_got = steps.run(
        [(attention_half(1, kv_grad), branch_grad[1]), (first_round, gate_share)]
        + [(first_round, sent) for sent in branch_sent],
        1,
    )
    gate_two = rows_joined(gate_share, gate_got)
    branch_sums = [
        kept.astype(f32) + value.astype(f32) for kept, value in zip(branch_kept, branch_got)
    ]
    outputs = hidden_mid + branch_sums[0]
    query_grad = (query_grad_mine, query_grad_other)
    kv_grad = kv_grad.astype(bf16)
    if cell_count > 1:
        kv_grad_cell = block(kv_grad, cell, CELL * chunk).astype(f32)
        for step in range(1, cell_count):
            piece = block(kv_grad, (cell + step) % cell_count, CELL * chunk)
            kv_grad_cell = kv_grad_cell + cell_send(piece, step).astype(f32)
        kv_grad = kv_grad_cell.astype(bf16)
    kv_grad = kv_grad.reshape(CELL, fsdp_count, rows, 2 * HEAD_DIM)

    def kv_piece(k):
        at = -k % fsdp_count
        return lax.slice_in_dim(kv_grad, at, at + 1, axis=1)

    def fsdp_piece(values, k):
        return block(values, (fsdp_here + k) % fsdp_count, weight_rows)

    up_total = up.total(up_mine)

    def send_then_share(v):
        got = sends[1](v[0])
        return got, shares_sent(after(v[1], got))

    (kv_next, up_got), *got = steps.run(
        [(send_then_share, (kv_piece(1), up_total))]
        + [(sends[k], kv_piece(k)) for k in range(2, fsdp_count)]
        + [
            (second_round, gate_two),
            (
                lambda v: sum(dot(half, branch, TN) for half, branch in zip(*v)).astype(bf16),
                (attended, branch_grad),
            ),
        ]
    )
    out_partial = got.pop()
    kv_total = kv_piece(0).astype(f32) + kv_next.astype(f32)
    for value in got[:-1]:
        kv_total = kv_total + value.astype(f32)
    kv_total = kv_total.reshape(cell_tokens, 2 * HEAD_DIM)
    gate_got = got[-1]
    up_share = shares(up_total, up_got)

    projected, gate_two_twin, up_got, out_partial, *branch_got = steps.run(
        [
            (
                lambda v: project_grad(
                    place, *normed_attn, angles, gains, qkv_rows, query_grad, v, qkv_pieces, rows
                ),
                kv_total,
            ),
            (twin_send, gate_two),
            (first_round, up_share),
            (lambda v: cell_turn(v, 1, 0), out_partial),
        ]
        + [
            (lambda v, j=j: pair_send(v, j, pair), value.astype(bf16))
            for j, value in enumerate(branch_sums[1:], 1)
        ],
        1,
    )
    *qkv_grad, attn_mine, attn_other, head_gain_grad, attention_gain_grad = projected
    up_two = rows_joined(up_share, up_got)
    gains_here = SumEverywhere(jnp.concatenate(
        [
            attention_gain_grad[0] / attention_gain,
            mlp_gain_grad,
            head_gain_grad[0],
            head_gain_grad[1],
        ]
    ).reshape(-1, 2 * HEAD_DIM))

    def gather_place(side, slot, part, whole):
        return place_units(
            whole,
            gate_up_weight.shape,
            part,
            weight_rows,
            unit,
            place,
            lambda i, g, at: (
                side * (hidden_width // unit)
                + ((g % pair_count) * pair + (at[3] - g // pair_count + pair) % pair) * CELL
                + token_block(slot + i, at)
            ),
        )

    def placing(parts):
        def place_all(v):
            whole, arrays = v
            for (side, slot, _), array in zip(parts, arrays):
                whole = gather_place(side, slot, array, whole)
            return whole

        return place_all, (grad_gate_up, [part for _, _, part in parts])

    def fsdp_sum(pieces, got):
        total = pieces[0].astype(f32)
        for value in got:
            total = total + value.astype(f32)
        return cell_sum(total).astype(bf16)

    def sent_pieces(pieces, distances):
        return [(sends[k], pieces[k]) for k in distances]

    def all_pieces(values):
        return [fsdp_piece(values, k) for k in range(fsdp_count)]

    odd_steps, even_steps = range(1, fsdp_count, 2), range(2, fsdp_count, 2)
    grad_gate_up = None
    got = steps.run(
        [
            (twin_send, attn_other),
            (second_round, up_two),
            (twin_send, up_two),
            (
                lambda v: all_pieces(
                    sum(dot(half, grad, TN) for half, grad in zip(*v)).astype(bf16)
                ),
                (normed_attn, qkv_grad),
            ),
            (all_pieces, out_partial),
            down.own(),
            (lambda v: gather_place(0, 0, v, None), gate_two),
            gains_here.part(),
        ],
        1,
    )
    kept, sent = reduce_first(attn_mine, got[0])
    up_got, up_two_twin = got[1:3]
    qkv_parts, out_parts, down_own_rows, grad_gate_up, gain_got = got[3:]
    gains_here.add(gain_got)
    down_share = down.total(down_own_rows)
    got = steps.run(
        [
            (second_round, sent),
            (first_round, down_share),
            (twin_send, gate_got),
            placing([(0, 4, gate_two_twin), (0, 2, gate_got), (1, 0, up_two)]),
        ]
        + sent_pieces(qkv_parts, odd_steps)
    )
    kept, sent = reduce_second(kept, got[0])
    down_two = rows_joined(down_share, got[1])
    gate_got_twin = got[2]
    grad_gate_up = got[3]
    qkv_got = got[4:]
    got = steps.run(
        [
            (first_round, sent),
            (second_round, down_two),
            placing([(0, 6, gate_got_twin), (1, 2, up_got), (1, 4, up_two_twin)]),
            (
                lambda v: sum([g.astype(f32) for g in v[1:]], v[0]).astype(bf16),
                [outputs] + branch_got,
            ),
        ]
        + sent_pieces(qkv_parts, even_steps)
        + sent_pieces(out_parts, odd_steps)
    )
    attn_normed_grad = kept.astype(f32) + got[0].astype(f32)
    down_got = got[1]
    grad_gate_up = got[2]
    outputs = got[3]
    qkv_share = fsdp_sum(qkv_parts, qkv_got + got[4 : 4 + len(even_steps)])
    out_got = got[4 + len(even_steps) :]
    got = steps.run(
        [
            (first_round, qkv_share),
            (twin_send, up_got),
            (twin_send, down_two),
            (lambda v: place_rows(place_rows(None, 0, v[0], place), 2, v[1], place), (down_two, down_got)),
            gains_here.part(),
            (
                lambda v: (
                    v[1] + jax.vjp(lambda u: rms_scale(u, attention_gain), source)[1](v[0])[0]
                ).astype(bf16),
                (attn_normed_grad, hidden_grad),
            ),
        ]
        + sent_pieces(out_parts, even_steps)
    )
    qkv_two = rows_joined(qkv_share, got[0])
    up_got_twin, down_two_twin, grad_down, gain_got, grad_inputs = got[1:6]
    gains_here.add(gain_got)
    out_share = fsdp_sum(out_parts, out_got + got[6:])
    got = steps.run(
        [
            (second_round, qkv_two),
            (first_round, out_share),
            (twin_send, down_got),
            placing([(1, 6, up_got_twin)]),
            (lambda v: place_rows(v[0], 4, v[1], place), (grad_down, down_two_twin)),
            gains_here.part(),
        ]
    )
    qkv_half = rows_joined(qkv_two, got[0])
    out_two = rows_joined(out_share, got[1])
    down_got_twin, grad_gate_up, grad_down, gain_got = got[2:]
    gains_here.add(gain_got)
    got = steps.run(
        [
            (second_round, out_two),
            (twin_send, qkv_half),
            (lambda v: place_rows(v[0], 6, v[1], place), (grad_down, down_got_twin)),
            gains_here.part(),
        ]
    )
    out_half = rows_joined(out_two, got[0])
    qkv_other, grad_down, gain_got = got[1:]
    gains_here.add(gain_got)
    got = steps.run(
        [
            (twin_send, out_half),
            gains_here.part(),
            (lambda v: place_heads(v, place), (qkv_half, qkv_other)),
        ]
    )
    gains_here.add(got[1])
    gain_sums = gains_here.finish().reshape(-1)
    grad_qkv = got[2]
    grad_out = place_columns((out_half, got[0]), width // CELL, place)
    attention_gain_sum, mlp_gain_sum = gain_sums[:width], gain_sums[width : 2 * width]
    head_sums = gain_sums[2 * width :].reshape(4, HEAD_DIM)

    gain_sums = (
        attention_gain_sum,
        head_sums[0] + head_sums[1],
        head_sums[2],
        mlp_gain_sum,
    )

    return (
        outputs,
        grad_inputs,
        gain_sums[0],
        grad_qkv,
        gain_sums[1],
        gain_sums[2],
        grad_out,
        gain_sums[3],
        grad_gate_up,
        grad_down,
    )


def solution(mesh):
    return jax.shard_map(
        body,
        mesh=mesh,
        in_specs=(
            P(("ctx", "fsdp"), None),
            P(),
            P("fsdp", None),
            P(),
            P(),
            P("fsdp", None),
            P(),
            P("fsdp", None),
            P("fsdp", None),
            P(("ctx", "fsdp"), None),
        ),
        out_specs=(
            P(("ctx", "fsdp"), None),
            P(("ctx", "fsdp"), None),
            P(),
            P("fsdp", None),
            P(),
            P(),
            P("fsdp", None),
            P(),
            P("fsdp", None),
            P("fsdp", None),
        ),
        check_vma=False,
    )
```

```python
import functools

import jax
import jax.numpy as jnp
from jax import lax
from jax.experimental import pallas as pl
from jax.experimental.pallas import tpu as pltpu
from jax.sharding import PartitionSpec as P

HEADS = 32
KV_HEADS = 8
HEAD_DIM = 64
GROUP = HEADS // KV_HEADS
GROUP_WIDTH = GROUP * HEAD_DIM

epsilon = 1e-05
theta = 1000000.0
score_scale = HEAD_DIM ** (-0.5)

f32 = jnp.float32
bf16 = jnp.bfloat16

CELL = KV_HEADS

NN = (((1,), (0,)), ((), ()))
NT = (((1,), (1,)), ((), ()))
TN = (((0,), (0,)), ((), ()))


def dot(left, right, dims=NN):
    return lax.dot_general(left, right, dims, preferred_element_type=f32)


def rms_scale(values, gain):
    return values * lax.rsqrt(jnp.mean(values * values, axis=-1, keepdims=True) + epsilon) * gain


def xor_send(values, distance):
    count = lax.axis_size("ctx")
    return lax.ppermute(values, "ctx", [(i, i ^ distance) for i in range(count)])


def cell_send(values, step):
    count = lax.axis_size("ctx")
    return lax.ppermute(values, "ctx", [(i, (i + step * CELL) % count) for i in range(count)])


def fsdp_send(values, step):
    count = lax.axis_size("fsdp")
    return lax.ppermute(values, "fsdp", [(i, (i + step) % count) for i in range(count)])


def pair_send(values, step, pair):
    count = lax.axis_size("fsdp")
    return lax.ppermute(
        values, "fsdp", [(i, i // pair * pair + (i % pair + step) % pair) for i in range(count)]
    )


def fsdp_relay(shard):
    count = lax.axis_size("fsdp")
    return [shard] + [fsdp_send(shard, step) for step in range(1, count)]


def fsdp_collect(piece_for):
    count = lax.axis_size("fsdp")
    total = piece_for(0).astype(f32)
    for step in range(1, count):
        total = total + fsdp_send(piece_for(step), step).astype(f32)
    return total


def round_send(values, odd_round):
    count = lax.axis_size("ctx")
    pairs = []
    for i in range(count):
        pairs.append((i, i ^ (2 if i % 2 == odd_round else 4)))
    return lax.ppermute(values, "ctx", pairs)


def add_low(left, right):
    return (left.astype(f32) + right.astype(f32)).astype(bf16)


def after(values, event):
    return lax.optimization_barrier((values, event))[0]


class Steps:
    def __init__(self):
        self.event = None
        self.jobs = []

    def begin(self, values):
        return values if self.event is None else after(values, self.event)

    def run(self, parts, spare=0):
        jobs, self.jobs = self.jobs[:spare], self.jobs[spare:]
        early = [start(self.begin) for start, _ in jobs]
        results = [function(self.begin(values)) for function, values in parts]
        early, results = lax.optimization_barrier((early, results))
        for (_, finish), value in zip(jobs, early):
            finish(value)
        self.event = results[0]
        return results

    def drain(self, done):
        while self.jobs and not done():
            self.run([(lambda v: v, self.event)], 2)


def first_round(values):
    return round_send(values, 0)


def second_round(values):
    return round_send(values, 1)


def twin_send(values):
    return xor_send(values, 1)


def join_kernel(place_ref, *refs):
    for n, ref in enumerate(refs[:-1]):

        @pl.when(pl.program_id(0) == n)
        def _(ref=ref):
            refs[-1][...] = ref[...]


def join(parts, places=None):
    shape, dtype = parts[0].shape, parts[0].dtype
    if places is None:
        places = list(range(len(parts)))
    size = parts[0].size * 2
    return pl.pallas_call(
        join_kernel,
        grid_spec=pltpu.PrefetchScalarGridSpec(
            num_scalar_prefetch=1,
            grid=(len(parts),),
            in_specs=[pl.BlockSpec(shape, lambda i, at: (0, 0))] * len(parts),
            out_specs=pl.BlockSpec(shape, lambda i, at: (at[i], 0)),
        ),
        out_shape=jax.ShapeDtypeStruct((len(parts) * shape[0], shape[1]), dtype),
        compiler_params=pltpu.CompilerParams(
            vmem_limit_bytes=(2 * len(parts) + 2) * size + 4 * 1024 * 1024
        ),
        cost_estimate=cost(0, 2 * size * len(parts)),
    )(jnp.stack([jnp.asarray(p, jnp.int32) for p in places]), *parts)


def rows_joined(*parts):
    return join(parts)


def add_kernel(left_ref, right_ref, first_ref, second_ref):
    total = (left_ref[...].astype(f32) + right_ref[...].astype(f32)).astype(bf16)

    @pl.when(pl.program_id(0) == 0)
    def _():
        first_ref[...] = total

    @pl.when(pl.program_id(0) == 1)
    def _():
        second_ref[...] = total


def add_halves(left, right):
    rows, columns = left.shape
    half = jax.ShapeDtypeStruct((rows // 2, columns), bf16)
    in_spec = pl.BlockSpec((rows // 2, columns), lambda i: (i, 0))
    out_spec = pl.BlockSpec((rows // 2, columns), lambda i: (0, 0))
    return pl.pallas_call(
        add_kernel,
        grid=(2,),
        in_specs=[in_spec] * 2,
        out_specs=[out_spec] * 2,
        out_shape=[half, half],
        compiler_params=pltpu.CompilerParams(vmem_limit_bytes=20 * 1024 * 1024),
        cost_estimate=cost(left.size, 6 * left.size),
    )(left, right)


def reduce_first(mine, from_twin):
    return add_halves(mine, from_twin)


def reduce_second(kept, received):
    return add_halves(kept, received)


class SumEverywhere:
    def __init__(self, values):
        self.total = values
        self.rounds = []
        for axis in ("ctx", "fsdp"):
            count = lax.axis_size(axis)
            if count & (count - 1):
                self.rounds.append(functools.partial(self.whole, axis))
                continue
            distance = 1
            while distance < count:
                self.rounds.append(functools.partial(self.exchange, axis, count, distance))
                distance *= 2

    def exchange(self, axis, count, distance, values):
        return lax.ppermute(values, axis, [(i, i ^ distance) for i in range(count)])

    def whole(self, axis, values):
        return lax.psum(values, axis) - values

    def part(self):
        return (self.rounds.pop(0), self.total)

    def add(self, got):
        self.total = self.total + got

    def finish(self):
        while self.rounds:
            function, values = self.part()
            self.add(function(values))
        return self.total


def blank(shape, dtype):
    return pl.pallas_call(
        lambda ref: None,
        out_specs=pl.BlockSpec(memory_space=pl.ANY),
        out_shape=jax.ShapeDtypeStruct(shape, dtype),
        cost_estimate=pl.CostEstimate(flops=0, bytes_accessed=0, transcendentals=0),
    )()


def vmem(mebibytes, keys=0):
    return pltpu.CompilerParams(vmem_limit_bytes=mebibytes * 1024 * 1024 + keys * 2560)


def cost(flops, moved, transcendentals=0):
    return pl.CostEstimate(
        flops=int(flops), bytes_accessed=int(moved), transcendentals=int(transcendentals)
    )


def own(i, place):
    slot = i % 4
    other = i // 4
    swapped = (place[2] + other) % 2
    return slot // 2 * (4 - 2 * swapped) + slot % 2 * (2 + 2 * swapped) + other


def token_block(i, place):
    return jnp.bitwise_xor(own(i, place), place[2])


def even_block(i):
    return jnp.minimum(i, 3)


def odd_block(i):
    return jnp.maximum(i - 4, 0)


def swap_halves(values):
    lane = lax.broadcasted_iota(jnp.int32, values.shape, 1) % HEAD_DIM
    return jnp.where(
        lane < HEAD_DIM // 2,
        pltpu.roll(values, values.shape[1] - HEAD_DIM // 2, 1),
        pltpu.roll(values, HEAD_DIM // 2, 1),
    )


def head_mean(values):
    first = lax.broadcasted_iota(jnp.int32, values.shape, 1) < HEAD_DIM
    low = jnp.sum(jnp.where(first, values, 0.0), axis=1, keepdims=True)
    high = jnp.sum(jnp.where(first, 0.0, values), axis=1, keepdims=True)
    return jnp.where(first, low, high) * (1.0 / HEAD_DIM)


def project_kernel(fsdp_count, place_ref, even_ref, odd_ref, angle_ref, gain_ref, *refs):
    weight_refs, (rows_ref, q_ref, kv_ref) = refs[:fsdp_count], refs[fsdp_count:]
    depth = weight_refs[0].shape[0]

    def project(left_ref):
        total = None
        for step in range(fsdp_count):
            owner = lax.rem(place_ref[0] - step + fsdp_count, fsdp_count)
            left = left_ref[:, pl.ds(pl.multiple_of(owner * depth, depth), depth)]
            term = dot(left, weight_refs[step][...])
            total = term if total is None else total + term
        rows_ref[...] = total

    @pl.when(pl.program_id(0) < 4)
    def _():
        project(even_ref)

    @pl.when(pl.program_id(0) >= 4)
    def _():
        project(odd_ref)

    cosine = angle_ref[:, : 2 * HEAD_DIM]
    sine = angle_ref[:, 2 * HEAD_DIM :]
    wide = 2 * HEAD_DIM
    for group in range(GROUP_WIDTH // wide + 1):
        values = rows_ref[:, group * wide : (group + 1) * wide]
        last = group == GROUP_WIDTH // wide
        normed = values * lax.rsqrt(head_mean(values * values) + epsilon)
        normed = normed * gain_ref[int(last) : int(last) + 1, :]
        turned = normed * cosine + swap_halves(normed) * sine
        if last:
            lane = lax.broadcasted_iota(jnp.int32, values.shape, 1)
            kv_ref[...] = jnp.where(lane < HEAD_DIM, turned, values).astype(bf16)
        else:
            q_ref[:, group * wide : (group + 1) * wide] = turned.astype(bf16)


def project(place, even, odd, angles, gains, weights, rows):
    count = CELL
    fsdp_count = len(weights)
    width = even.shape[1]
    columns = weights[0].shape[1]
    return pl.pallas_call(
        functools.partial(project_kernel, fsdp_count),
        grid_spec=pltpu.PrefetchScalarGridSpec(
            num_scalar_prefetch=1,
            grid=(count,),
            in_specs=[
                pl.BlockSpec((rows, width), lambda i, place: (even_block(i), 0)),
                pl.BlockSpec((rows, width), lambda i, place: (odd_block(i), 0)),
                pl.BlockSpec((rows, 4 * HEAD_DIM), lambda i, place: (token_block(i, place), 0)),
                pl.BlockSpec((8, 2 * HEAD_DIM), lambda i, place: (0, 0)),
            ]
            + [pl.BlockSpec(w.shape, lambda i, place: (0, 0)) for w in weights],
            out_specs=[
                pl.BlockSpec((rows, columns), lambda i, place: (token_block(i, place), 0)),
                pl.BlockSpec((rows, GROUP_WIDTH), lambda i, place: (token_block(i, place), 0)),
                pl.BlockSpec((rows, 2 * HEAD_DIM), lambda i, place: (token_block(i, place), 0)),
            ],
        ),
        out_shape=[
            jax.ShapeDtypeStruct((count * rows, columns), f32),
            jax.ShapeDtypeStruct((count * rows, GROUP_WIDTH), bf16),
            jax.ShapeDtypeStruct((count * rows, 2 * HEAD_DIM), bf16),
        ],
        compiler_params=vmem(20),
        cost_estimate=cost(2 * count * rows * width * columns, 8e6),
    )(place, even, odd, angles, gains, *weights)


def project_grad_kernel(
    fsdp_count,
    place_ref,
    even_ref,
    odd_ref,
    angle_ref,
    gain_ref,
    rows_ref,
    q_even_ref,
    q_odd_ref,
    kv_ref,
    *refs,
):
    weight_refs = refs[:fsdp_count]
    (grad_even_ref, grad_odd_ref, part_even_ref, part_odd_ref, head_gain_ref, gain_grad_ref) = refs[
        fsdp_count:
    ]
    depth = weight_refs[0].shape[0]
    step_here = pl.program_id(0)

    @pl.when(step_here == 0)
    def _():
        head_gain_ref[...] = jnp.zeros_like(head_gain_ref)
        gain_grad_ref[...] = jnp.zeros_like(gain_grad_ref)

    cosine = angle_ref[:, : 2 * HEAD_DIM]
    sine = angle_ref[:, 2 * HEAD_DIM :]
    wide = 2 * HEAD_DIM
    pieces = []
    for group in range(GROUP_WIDTH // wide + 1):
        last = group == GROUP_WIDTH // wide
        values = rows_ref[:, group * wide : (group + 1) * wide]
        at = pl.ds(group * wide, wide)
        if last:
            grad = kv_ref[...]
        else:
            grad = jnp.where(step_here < 4, q_even_ref[:, at], q_odd_ref[:, at])
        scale = lax.rsqrt(head_mean(values * values) + epsilon)
        gain = gain_ref[int(last) : int(last) + 1, :]
        unturned = grad * cosine + swap_halves(grad * sine)
        head_gain_ref[int(last) : int(last) + 1, :] += jnp.sum(
            unturned * values * scale, axis=0, keepdims=True
        )
        scaled = unturned * gain
        piece = scale * scaled - values * (scale * scale * scale) * head_mean(scaled * values)
        if last:
            lane = lax.broadcasted_iota(jnp.int32, values.shape, 1)
            piece = jnp.where(lane < HEAD_DIM, piece, grad)
        pieces.append(piece.astype(bf16))
    low = jnp.concatenate(pieces, axis=1)

    def finish(normed_ref, grad_out_ref, part_ref):
        grad_out_ref[...] = low
        for step in range(fsdp_count):
            owner = lax.rem(place_ref[0] - step + fsdp_count, fsdp_count)
            at = pl.ds(pl.multiple_of(owner * depth, depth), depth)
            part = dot(low, weight_refs[step][...], NT)
            part_ref[:, at] = part.astype(bf16)
            gain_grad_ref[0:1, at] += jnp.sum(
                part * normed_ref[:, at].astype(f32), axis=0, keepdims=True
            )

    @pl.when(step_here < 4)
    def _():
        finish(even_ref, grad_even_ref, part_even_ref)

    @pl.when(step_here >= 4)
    def _():
        finish(odd_ref, grad_odd_ref, part_odd_ref)


def project_grad(place, even, odd, angles, gains, qkv_rows, query_grad, kv_grad, weights, rows):
    count = CELL
    fsdp_count = len(weights)
    width = even.shape[1]
    columns = weights[0].shape[1]

    def by_token(size):
        return pl.BlockSpec((rows, size), lambda i, place: (token_block(i, place), 0))

    def halves(size):
        return [
            pl.BlockSpec((rows, size), lambda i, place: (even_block(i), 0)),
            pl.BlockSpec((rows, size), lambda i, place: (odd_block(i), 0)),
        ]

    return pl.pallas_call(
        functools.partial(project_grad_kernel, fsdp_count),
        grid_spec=pltpu.PrefetchScalarGridSpec(
            num_scalar_prefetch=1,
            grid=(count,),
            in_specs=halves(width)
            + [
                by_token(4 * HEAD_DIM),
                pl.BlockSpec((8, 2 * HEAD_DIM), lambda i, place: (0, 0)),
                by_token(columns),
                *halves(GROUP_WIDTH),
                by_token(2 * HEAD_DIM),
            ]
            + [pl.BlockSpec(w.shape, lambda i, place: (0, 0)) for w in weights],
            out_specs=halves(columns)
            + halves(width)
            + [
                pl.BlockSpec((8, 2 * HEAD_DIM), lambda i, place: (0, 0)),
                pl.BlockSpec((8, width), lambda i, place: (0, 0)),
            ],
        ),
        out_shape=[
            jax.ShapeDtypeStruct((4 * rows, columns), bf16),
            jax.ShapeDtypeStruct((4 * rows, columns), bf16),
            jax.ShapeDtypeStruct((4 * rows, width), bf16),
            jax.ShapeDtypeStruct((4 * rows, width), bf16),
            jax.ShapeDtypeStruct((8, 2 * HEAD_DIM), f32),
            jax.ShapeDtypeStruct((8, width), f32),
        ],
        compiler_params=vmem(48),
        cost_estimate=cost(2 * count * rows * width * columns, 12e6),
    )(place, even, odd, angles, gains, qkv_rows, *query_grad, kv_grad, *weights)


def stack_heads(block):
    return jnp.concatenate(
        [block[:, i * HEAD_DIM : (i + 1) * HEAD_DIM] for i in range(GROUP)], axis=0
    )


def unstack_heads(turned, rows):
    return jnp.concatenate([turned[:, i * rows : (i + 1) * rows].T for i in range(GROUP)], axis=1)


def fill_turned(place_ref, kv_ref, turned_ref, chunk):
    @pl.when(pl.program_id(0) == 0)
    def _():
        def turn(n, _):
            start = pl.multiple_of(n * chunk, chunk)
            turned_ref[:, pl.ds(start, chunk)] = kv_ref[pl.ds(start, chunk), :].T
            return 0

        lax.fori_loop(0, (place_ref[1] + 1) * CELL, turn, 0)


def visible_keys(place_ref, chunk, rows):
    key_row = lax.broadcasted_iota(jnp.int32, (chunk, GROUP * rows), 0)
    row_at = lax.broadcasted_iota(jnp.int32, (chunk, GROUP * rows), 1) % rows
    count = chunk // rows
    owner = (place_ref[0] - key_row // rows + count) % count
    return owner * rows + key_row % rows <= row_at + place_ref[0] * rows


def attention_kernel(
    chunk, place_ref, q_ref, kv_ref, even_ref, odd_ref, log_ref, turned_ref
):
    rows = q_ref.shape[0]
    fill_turned(place_ref, kv_ref, turned_ref, chunk)
    queries = stack_heads(q_ref[...].astype(f32) * score_scale).astype(bf16)
    queries = jnp.concatenate([queries, jnp.zeros_like(queries)], axis=1)

    def step(n, running, masked):
        total, summed = running
        start = pl.multiple_of(n * chunk, chunk)
        weights = jnp.exp(dot(kv_ref[pl.ds(start, chunk), :], queries, NT))
        if masked:
            weights = jnp.where(visible_keys(place_ref, chunk, rows), weights, 0.0)
        return (
            total + jnp.sum(weights, axis=0, keepdims=True),
            summed + dot(turned_ref[:, pl.ds(start, chunk)], weights.astype(bf16)),
        )

    last = place_ref[1] * CELL + token_block(pl.program_id(0), place_ref)
    running = (
        jnp.zeros((1, GROUP * rows), f32),
        jnp.zeros((2 * HEAD_DIM, GROUP * rows), f32),
    )
    running = lax.fori_loop(0, last, lambda n, r: step(n, r, False), running)
    total, summed = step(last, running, True)
    result = unstack_heads(summed[HEAD_DIM:] / total, rows).astype(bf16)

    @pl.when(pl.program_id(0) < 4)
    def _():
        even_ref[...] = result

    @pl.when(pl.program_id(0) >= 4)
    def _():
        odd_ref[...] = result

    log_ref[...] = jnp.log(total)[None]


def attention(place, queries, keys_values, rows, chunk):
    count = queries.shape[0] // rows
    keys = keys_values.shape[0]
    half = jax.ShapeDtypeStruct((4 * rows, GROUP_WIDTH), bf16)
    return pl.pallas_call(
        functools.partial(attention_kernel, chunk),
        grid_spec=pltpu.PrefetchScalarGridSpec(
            num_scalar_prefetch=1,
            grid=(count,),
            in_specs=[
                pl.BlockSpec((rows, GROUP_WIDTH), lambda i, place: (token_block(i, place), 0)),
                pl.BlockSpec((keys, 2 * HEAD_DIM), lambda i, place: (0, 0)),
            ],
            out_specs=[
                pl.BlockSpec((rows, GROUP_WIDTH), lambda i, place: (even_block(i), 0)),
                pl.BlockSpec((rows, GROUP_WIDTH), lambda i, place: (odd_block(i), 0)),
                pl.BlockSpec((1, 1, GROUP * rows), lambda i, place: (i, 0, 0)),
            ],
            scratch_shapes=[pltpu.VMEM((2 * HEAD_DIM, keys), bf16)],
        ),
        out_shape=[half, half, jax.ShapeDtypeStruct((count, 1, GROUP * rows), f32)],
        compiler_params=vmem(12, keys),
        cost_estimate=cost(16e9, 8e6, 1e7),
    )(place, queries, keys_values)


def attention_grad_kernel(
    chunk,
    other,
    place_ref,
    q_ref,
    branch_ref,
    out_ref,
    log_ref,
    weight_ref,
    kv_ref,
    *refs,
):
    q_grad_ref, kv_grad_ref, turned_ref = refs[-3:]
    rows = q_ref.shape[0]
    fill_turned(place_ref, kv_ref, turned_ref, chunk)

    @pl.when(pl.program_id(0) == 0)
    def _():
        kv_grad_ref[...] = refs[0][...] if other else jnp.zeros_like(kv_grad_ref)

    queries = stack_heads(q_ref[...].astype(f32) * score_scale).astype(bf16)
    queries = jnp.concatenate([queries, jnp.zeros_like(queries)], axis=1)
    out_grad = dot(branch_ref[...], weight_ref[...], NT).astype(bf16)
    grads = stack_heads(out_grad)
    attended = stack_heads(out_ref[...]).astype(f32)
    row_delta = jnp.sum((grads.astype(f32) * attended).T, axis=0, keepdims=True)
    grads = jnp.concatenate([jnp.zeros_like(grads), grads], axis=1)
    log_total = log_ref[0]

    def step(n, summed, masked):
        start = pl.multiple_of(n * chunk, chunk)
        block = kv_ref[pl.ds(start, chunk), :]
        weights = jnp.exp(dot(block, queries, NT) - log_total)
        if masked:
            weights = jnp.where(visible_keys(place_ref, chunk, rows), weights, 0.0)
        score_grad = (weights * (dot(block, grads, NT) - row_delta)).astype(bf16)
        kv_grad_ref[pl.ds(start, chunk), :] += dot(score_grad, queries) + dot(
            weights.astype(bf16), grads
        )
        return summed + dot(turned_ref[:, pl.ds(start, chunk)], score_grad)

    last = place_ref[1] * CELL + token_block(pl.program_id(0) + 4 * other, place_ref)
    summed = jnp.zeros((2 * HEAD_DIM, GROUP * rows), f32)
    summed = lax.fori_loop(0, last, lambda n, r: step(n, r, False), summed)
    summed = step(last, summed, True)
    q_grad_ref[...] = unstack_heads(summed[:HEAD_DIM] * score_scale, rows)


def attention_grad(
    place, queries, branch, attended, log_total, weight, keys_values, rows, chunk, other, kv_grad=None
):
    keys = keys_values.shape[0]
    width = weight.shape[1]
    whole_spec = pl.BlockSpec((keys, 2 * HEAD_DIM), lambda i, place: (0, 0))
    added = [] if kv_grad is None else [kv_grad]
    return pl.pallas_call(
        functools.partial(attention_grad_kernel, chunk, other),
        grid_spec=pltpu.PrefetchScalarGridSpec(
            num_scalar_prefetch=1,
            grid=(4,),
            in_specs=[
                pl.BlockSpec(
                    (rows, GROUP_WIDTH), lambda i, place: (token_block(i + 4 * other, place), 0)
                ),
                pl.BlockSpec((rows, width), lambda i, place: (i, 0)),
                pl.BlockSpec((rows, GROUP_WIDTH), lambda i, place: (i, 0)),
                pl.BlockSpec((1, 1, GROUP * rows), lambda i, place: (i + 4 * other, 0, 0)),
                pl.BlockSpec(weight.shape, lambda i, place: (0, 0)),
                whole_spec,
            ]
            + [whole_spec] * len(added),
            out_specs=[
                pl.BlockSpec((rows, GROUP_WIDTH), lambda i, place: (i, 0)),
                whole_spec,
            ],
            scratch_shapes=[pltpu.VMEM((2 * HEAD_DIM, keys), bf16)],
        ),
        out_shape=[
            jax.ShapeDtypeStruct((4 * rows, GROUP_WIDTH), f32),
            jax.ShapeDtypeStruct(keys_values.shape, f32),
        ],
        compiler_params=vmem(18, keys),
        cost_estimate=cost(18e9, 12e6, 5e6),
    )(place, queries, branch, attended, log_total, weight, keys_values, *added)


def feed_kernel(
    normed_ref, outer_ref, weight_ref, down_ref, active_ref, gate_grad_ref, part_ref, branch_ref
):
    units = active_ref.shape[1]
    both = dot(normed_ref[...], weight_ref[...])
    gate = both[:, :units]
    up = both[:, units:]
    act_grad = dot(outer_ref[...], down_ref[...], NT)
    logistic = 1.0 / (1.0 + jnp.exp(-gate))
    silu = gate * logistic
    active_ref[...] = (silu * up).astype(bf16)
    gate_part = act_grad * up * (logistic * (1.0 + gate * (1.0 - logistic)))
    gate_grad_ref[:, :units] = gate_part.astype(bf16)
    gate_grad_ref[:, units:] = (act_grad * silu).astype(bf16)
    part_ref[...] = dot(gate_grad_ref[...], weight_ref[...], NT).astype(bf16)
    branch_ref[...] = dot(active_ref[...], down_ref[...]).astype(bf16)


def feed(normed, outer, weight, down):
    tokens, width = normed.shape
    columns = weight.shape[1]
    rows = 256 if tokens % 256 == 0 else tokens

    def by_row(size):
        return pl.BlockSpec((rows, size), lambda i: (i, 0))

    def low(size):
        return jax.ShapeDtypeStruct((tokens, size), bf16)

    return pl.pallas_call(
        feed_kernel,
        grid=(tokens // rows,),
        in_specs=[
            by_row(width),
            by_row(width),
            pl.BlockSpec(weight.shape, lambda i: (0, 0)),
            pl.BlockSpec(down.shape, lambda i: (0, 0)),
        ],
        out_specs=[by_row(columns // 2), by_row(columns), by_row(width), by_row(width)],
        out_shape=[low(columns // 2), low(columns), low(width), low(width)],
        compiler_params=vmem(36),
        cost_estimate=cost(6 * tokens * width * columns, 16e6, tokens * columns),
    )(normed, outer, weight, down)


def weight_grad_kernel(count, place_ref, *refs):
    total = None
    for left_ref, right_ref in zip(refs[:count], refs[count : 2 * count]):
        term = dot(left_ref[...], right_ref[...], TN)
        total = term if total is None else total + term
    for n, ref in enumerate(refs[2 * count :]):

        @pl.when(pl.program_id(0) == n)
        def _(ref=ref):
            ref[...] = total.astype(bf16)


def weight_grad(lefts, rights, first, size, column, columns, count):
    tokens = lefts[0].shape[0]
    tile = size // count
    place = jnp.stack([first * count]).astype(jnp.int32)
    if tile % 128:
        tile, place = size, jnp.stack([first]).astype(jnp.int32)
    parts = size // tile
    made = pl.pallas_call(
        functools.partial(weight_grad_kernel, len(lefts)),
        grid_spec=pltpu.PrefetchScalarGridSpec(
            num_scalar_prefetch=1,
            grid=(parts,),
            in_specs=[pl.BlockSpec((tokens, tile), lambda i, at: (0, at[0] + i))] * len(lefts)
            + [pl.BlockSpec((tokens, columns), lambda i, at: (0, column))] * len(rights),
            out_specs=[pl.BlockSpec((tile, columns), lambda i, at: (0, 0))] * parts,
        ),
        out_shape=[jax.ShapeDtypeStruct((tile, columns), bf16)] * parts,
        compiler_params=vmem(36),
        cost_estimate=cost(2 * len(lefts) * tokens * size * columns, 12e6),
    )(place, *lefts, *rights)
    if parts == count:
        return list(made)
    return [lax.slice_in_dim(made[0], n * size // count, (n + 1) * size // count) for n in range(count)]


def norm_grad_kernel(hidden_ref, outer_ref, gain_ref, *refs):
    terms, (low_ref, grad_ref, gain_grad_ref) = refs[:-3], refs[-3:]
    normed_grad = terms[0][...]
    for term in terms[1:]:
        normed_grad = normed_grad + term[...]
    hidden = hidden_ref[...]
    scale = lax.rsqrt(jnp.mean(hidden * hidden, axis=1, keepdims=True) + epsilon)
    scaled = normed_grad * gain_ref[...]
    along = jnp.mean(scaled * hidden, axis=1, keepdims=True)
    grad = outer_ref[...].astype(f32) + scale * scaled - hidden * (scale * scale * scale * along)
    grad_ref[...] = grad
    low_ref[...] = grad.astype(bf16)

    @pl.when(pl.program_id(0) == 0)
    def _():
        gain_grad_ref[...] = jnp.zeros_like(gain_grad_ref)

    gain_grad_ref[0:1, :] += jnp.sum(normed_grad * hidden * scale, axis=0, keepdims=True)


def norm_grad(hidden, outer, gain, terms):
    tokens, width = hidden.shape
    rows = tokens // 4
    by_row = pl.BlockSpec((rows, width), lambda i: (i, 0))
    return pl.pallas_call(
        norm_grad_kernel,
        grid=(4,),
        in_specs=[by_row, by_row, pl.BlockSpec((1, width), lambda i: (0, 0))] + [by_row] * len(terms),
        out_specs=[by_row, by_row, pl.BlockSpec((8, width), lambda i: (0, 0))],
        out_shape=[
            jax.ShapeDtypeStruct((tokens, width), bf16),
            jax.ShapeDtypeStruct((tokens, width), f32),
            jax.ShapeDtypeStruct((8, width), f32),
        ],
        compiler_params=vmem(16),
        cost_estimate=cost(20 * tokens * width, 5e6),
    )(hidden, outer, gain[None, :], *terms)


def place_units_kernel(block_at, unit, columns, place_ref, source_ref, *refs):
    out_ref, wide_ref, sems = refs[-3:]
    rows = wide_ref.shape[1]
    copies = []
    for n in range(wide_ref.shape[0]):
        slot, column = n // columns, n % columns
        wide_ref[n] = source_ref[
            slot * rows : (slot + 1) * rows, column * unit : (column + 1) * unit
        ].astype(f32)
        start = pl.multiple_of(block_at(slot, column, place_ref) * unit, unit)
        copies.append(
            pltpu.make_async_copy(wide_ref.at[n], out_ref.at[:, pl.ds(start, unit)], sems.at[n])
        )
        copies[-1].start()
    for copy in copies:
        copy.wait()


def place_units(whole, shape, source, rows, unit, place, block_at):
    slots, columns = source.shape[0] // rows, source.shape[1] // unit
    count = slots * columns
    in_specs = [pl.BlockSpec(source.shape, lambda i, at: (0, 0))]
    operands = [place, source]
    aliases = {}
    if whole is not None:
        in_specs.append(pl.BlockSpec(memory_space=pl.ANY))
        operands.append(whole)
        aliases = {2: 0}
    return pl.pallas_call(
        functools.partial(place_units_kernel, block_at, unit, columns),
        grid_spec=pltpu.PrefetchScalarGridSpec(
            num_scalar_prefetch=1,
            grid=(1,),
            in_specs=in_specs,
            out_specs=pl.BlockSpec(memory_space=pl.ANY),
            scratch_shapes=[
                pltpu.VMEM((count, rows, unit), f32),
                pltpu.SemaphoreType.DMA((count,)),
            ],
        ),
        out_shape=jax.ShapeDtypeStruct(shape, f32),
        input_output_aliases=aliases,
        compiler_params=vmem(16),
        cost_estimate=cost(0, 6 * source.size),
    )(*operands)


def place_columns(halves, unit, place):
    whole = None
    rows = halves[0].shape[0] // 4
    for odd, half in enumerate(halves):
        whole = place_units(
            whole,
            (rows, CELL * unit),
            half,
            rows,
            unit,
            place,
            lambda slot, column, at, odd=odd: token_block(4 * odd + slot, at),
        )
    return whole


def place_rows_kernel(slot, place_ref, source_ref, *refs):
    out_ref, wide_ref, sems = refs[-3:]
    rows = wide_ref.shape[1]
    copies = []
    for n in range(wide_ref.shape[0]):
        wide_ref[n] = source_ref[n * rows : (n + 1) * rows].astype(f32)
        start = pl.multiple_of(token_block(slot + n, place_ref) * rows, rows)
        copies.append(
            pltpu.make_async_copy(wide_ref.at[n], out_ref.at[pl.ds(start, rows)], sems.at[n])
        )
        copies[-1].start()
    for copy in copies:
        copy.wait()


def place_rows(whole, slot, quarter, place):
    rows, columns = quarter.shape[0] // 2, quarter.shape[1]
    extra = [] if whole is None else [whole]
    return pl.pallas_call(
        functools.partial(place_rows_kernel, slot),
        grid_spec=pltpu.PrefetchScalarGridSpec(
            num_scalar_prefetch=1,
            grid=(1,),
            in_specs=[pl.BlockSpec(quarter.shape, lambda i, at: (0, 0))]
            + [pl.BlockSpec(memory_space=pl.ANY)] * len(extra),
            out_specs=pl.BlockSpec(memory_space=pl.ANY),
            scratch_shapes=[
                pltpu.VMEM((2, rows, columns), f32),
                pltpu.SemaphoreType.DMA((2,)),
            ],
        ),
        out_shape=jax.ShapeDtypeStruct((CELL * rows, columns), f32),
        input_output_aliases={2: 0} if extra else {},
        compiler_params=vmem(16),
        cost_estimate=cost(0, 6 * quarter.size),
    )(place, quarter, *extra)


def place_heads_kernel(place_ref, even_ref, odd_ref, out_ref):
    query_width = HEADS * HEAD_DIM
    key_width = KV_HEADS * HEAD_DIM
    even = even_ref[...].astype(f32)
    odd = odd_ref[...].astype(f32)
    first = lax.rem(place_ref[2], 2) == 0
    low = jnp.where(first, even, odd)
    high = jnp.where(first, odd, even)
    twins = token_block(pl.program_id(0), place_ref) // 2

    def at(start, size):
        return pl.ds(pl.multiple_of(start + twins * size, 128), size)

    out_ref[:, at(0, 2 * GROUP_WIDTH)] = jnp.concatenate(
        [low[:, :GROUP_WIDTH], high[:, :GROUP_WIDTH]], axis=1
    )
    middle = GROUP_WIDTH + HEAD_DIM
    out_ref[:, at(query_width, 2 * HEAD_DIM)] = jnp.concatenate(
        [low[:, GROUP_WIDTH:middle], high[:, GROUP_WIDTH:middle]], axis=1
    )
    out_ref[:, at(query_width + key_width, 2 * HEAD_DIM)] = jnp.concatenate(
        [low[:, middle:], high[:, middle:]], axis=1
    )


def place_heads(halves, place):
    rows, columns = halves[0].shape[0] // 4, halves[0].shape[1]
    shape = (rows, CELL * columns)
    return pl.pallas_call(
        place_heads_kernel,
        grid_spec=pltpu.PrefetchScalarGridSpec(
            num_scalar_prefetch=1,
            grid=(4,),
            in_specs=[
                pl.BlockSpec((rows, columns), lambda i, at: (i, 0)),
                pl.BlockSpec((rows, columns), lambda i, at: (i % 2 * 2 + i // 2, 0)),
            ],
            out_specs=pl.BlockSpec(shape, lambda i, at: (0, 0)),
        ),
        out_shape=jax.ShapeDtypeStruct(shape, f32),
        compiler_params=vmem(28),
        cost_estimate=cost(0, 6 * rows * CELL * columns),
    )(place, *halves)


def body(
    inputs,
    attention_gain,
    qkv_weight,
    query_gain,
    key_gain,
    out_weight,
    mlp_gain,
    gate_up_weight,
    down_weight,
    cotangent,
):
    rows, width = inputs.shape
    fsdp_count = lax.axis_size("fsdp")
    cell_count = lax.axis_size("ctx") // CELL
    pair = 2 if fsdp_count % 2 == 0 else 1
    pair_count = fsdp_count // pair
    fsdp_here = lax.axis_index("fsdp")
    ctx_here = lax.axis_index("ctx")
    head = ctx_here % CELL
    cell = ctx_here // CELL
    in_pair = fsdp_here % pair
    pair_here = fsdp_here // pair
    weight_rows = qkv_weight.shape[0]
    query_width = HEADS * HEAD_DIM
    key_width = KV_HEADS * HEAD_DIM
    hidden_width = gate_up_weight.shape[1] // 2
    unit = hidden_width // (fsdp_count * CELL)
    place = jnp.stack([fsdp_here, cell, head, in_pair]).astype(jnp.int32)

    def block(values, index, size, axis=0):
        return lax.dynamic_slice_in_dim(values, index * size, size, axis)

    def put(whole, part, index, axis=0):
        return lax.dynamic_update_slice_in_dim(whole, part, index * part.shape[axis], axis)

    def cell_sum(values):
        total = values.astype(f32)
        for step in range(1, cell_count):
            total = total + cell_send(values.astype(bf16), step).astype(f32)
        return total

    def cell_turn(values, split_axis, join_axis):
        groups = None
        if cell_count > 1:
            groups = [[c * CELL + i for i in range(CELL)] for c in range(cell_count)]
        return lax.all_to_all(
            values, "ctx", split_axis, join_axis, axis_index_groups=groups, tiled=True
        )

    blocks_here = cell * CELL + jnp.arange(CELL, dtype=jnp.int32)
    positions = (
        ((blocks_here * fsdp_count + fsdp_here) * rows)[:, None]
        + jnp.arange(rows, dtype=jnp.int32)[None, :]
    ).reshape(-1)
    cell_tokens = CELL * rows
    half_dim = HEAD_DIM // 2
    frequency = theta ** (-jnp.arange(half_dim, dtype=f32) * 2.0 / HEAD_DIM)

    def angle_table(here):
        turns = here.astype(f32)[:, None] * frequency[None, :]
        cosine = jnp.cos(turns)
        sine = jnp.sin(turns)
        return jnp.concatenate([cosine] * 4 + [-sine, sine] * 2, axis=1)

    gains = jnp.concatenate(
        [
            jnp.tile(query_gain, 2)[None, :],
            jnp.concatenate([key_gain, jnp.ones_like(key_gain)])[None, :],
            jnp.zeros((6, 2 * HEAD_DIM), f32),
        ],
        axis=0,
    )

    source = inputs.astype(f32)
    normed_attn_own = rms_scale(source, attention_gain).astype(bf16)
    def head_columns(start):
        both = lax.dynamic_slice_in_dim(
            qkv_weight, start + head // 2 * (2 * HEAD_DIM), 2 * HEAD_DIM, 1
        )
        return jnp.where(head % 2 == 0, both[:, :HEAD_DIM], both[:, HEAD_DIM:])

    qkv_own = jnp.concatenate(
        [
            block(qkv_weight, head, GROUP_WIDTH, 1),
            head_columns(query_width),
            head_columns(query_width + key_width),
        ],
        axis=1,
    )
    out_own = block(out_weight, head, width // CELL, 1)
    local_units = pair_count * unit
    pair_rows = pair * weight_rows

    def half_columns(weight, owner, n):
        size = weight_rows // 2
        return jnp.concatenate(
            [
                lax.dynamic_slice(
                    weight,
                    (
                        n * size,
                        side * hidden_width + ((p * pair + owner) * CELL + head) * unit,
                    ),
                    (size, unit),
                )
                for side in range(2)
                for p in range(pair_count)
            ],
            axis=1,
        )

    steps = Steps()
    sends = [functools.partial(fsdp_send, step=k) for k in range(fsdp_count)]

    pair_jobs, down_jobs, own_jobs, mate_jobs = [], [], [], []
    gate_up_parts, down_parts = [], []

    def cross_job(read, step, row):
        return (
            lambda begin: fsdp_send(begin(read()), step * pair),
            lambda got: gate_up_parts.append((got, (fsdp_here - step * pair) % fsdp_count, row)),
        )

    mates = {}

    def mate_job(j, n):
        def finish(got):
            mates[j, n] = got
            gate_up_parts.append((got, pair_here * pair + (in_pair - j) % pair, n))

        return (lambda begin: pair_send(begin(owned[j, n]), j, pair), finish)

    def mate_cross_job(j, n, step):
        def finish(got):
            layer = (pair_here - step) % pair_count * pair + (in_pair - j) % pair
            gate_up_parts.append((got, layer, n))

        return (lambda begin: fsdp_send(begin(mates[j, n]), step * pair), finish)

    def down_job(step, n):
        return (
            lambda begin: fsdp_send(begin(down_pieces[n]), step * pair),
            lambda got: down_parts.append((got, (pair_here - step) % pair_count, n)),
        )

    for n in range(2):
        for j in range(1, pair):
            pair_jobs.append(mate_job(j, n))
        for step in range(1, pair_count):
            own_jobs.append(cross_job(lambda n=n: owned[0, n], step, n))
            for j in range(1, pair):
                mate_jobs.append(mate_cross_job(j, n, step))
    for n in range(4):
        for step in range(1, pair_count):
            down_jobs.append(down_job(step, n))

    last = max(fsdp_count - 1, 3)
    got = steps.run(
        [(first_round, normed_attn_own), (angle_table, positions)]
        + [(send, qkv_own) for send in sends[1:2]]
    )
    angles = got[1]
    qkv_pieces = [qkv_own] + got[2:]
    from_first = got[0]
    got = steps.run(
        [
            (second_round, normed_attn_own),
            (second_round, from_first),
            (
                lambda v: (
                    {
                        (j, n): half_columns(v[0], (in_pair + j) % pair, n)
                        for j in range(pair)
                        for n in range(2)
                    },
                    [
                        lax.dynamic_slice_in_dim(
                            v[1], head * unit + n * (unit // 4), unit // 4
                        )
                        for n in range(4)
                    ],
                ),
                (gate_up_weight, down_weight),
            ),
        ]
        + [(send, qkv_own) for send in sends[2:last]]
    )
    owned, down_pieces = got[2]
    for n in range(2):
        gate_up_parts.append((owned[0, n], fsdp_here, n))
    for n in range(4):
        down_parts.append((down_pieces[n], pair_here, n))
    qkv_pieces += got[3:]
    mine = rows_joined(normed_attn_own, from_first, got[0], got[1])
    got = steps.run([(twin_send, mine)] + [(send, qkv_own) for send in sends[last:]])
    qkv_pieces += got[1:]
    normed_attn = [mine, got[0]]

    queue = [pair_jobs, pair_jobs, own_jobs, down_jobs, own_jobs, down_jobs, down_jobs]
    for jobs in queue + [mate_jobs, down_jobs, mate_jobs]:
        if jobs:
            steps.jobs.append(jobs.pop(0))
    steps.jobs += pair_jobs + down_jobs + own_jobs + mate_jobs

    projected, outer_got, *out_got = steps.run(
        [
            (lambda v: project(place, *v, angles, gains, qkv_pieces, rows), normed_attn),
            (first_round, cotangent),
        ]
        + [(send, out_own) for send in sends[1:]],
        1,
    )
    qkv_rows, query_low, kv_own = projected
    outer_two = rows_joined(cotangent, outer_got)
    kv_own = kv_own.reshape(CELL, 1, rows, 2 * HEAD_DIM)
    out_columns = join([out_own] + out_got, [(fsdp_here - k) % fsdp_count for k in range(fsdp_count)])

    def send_then_turn(split_axis, join_axis):
        def act(v):
            got = sends[1](v[0])
            return got, cell_turn(after(v[1], got), split_axis, join_axis)

        return act

    (kv_next, out_rows), *got = steps.run(
        [(send_then_turn(0, 1), (kv_own, out_columns))]
        + [(send, kv_own) for send in sends[2:]]
        + [(second_round, outer_two)],
        1,
    )
    kv_pieces = [kv_own, kv_next] + got[:-1]
    outer_mine = rows_joined(outer_two, got[-1])
    kv_cells = jnp.concatenate(kv_pieces, axis=1)
    chunk = fsdp_count * rows
    kv_all = kv_cells.reshape(CELL * chunk, 2 * HEAD_DIM)
    if cell_count > 1:
        kv_cells = kv_all
        kv_all = put(
            blank((cell_count * CELL * chunk, 2 * HEAD_DIM), bf16), kv_cells, cell
        )
        for step in range(1, cell_count):
            kv_all = put(kv_all, cell_send(kv_cells, step), (cell - step) % cell_count)

    attended, outer_other, *outer_next = steps.run(
        [
            (lambda v: attention(place, *v, rows, chunk), (query_low, kv_all)),
            (twin_send, outer_mine),
        ]
        + [(lambda v, j=j: pair_send(v, -j, pair), cotangent) for j in range(1, pair)],
        1,
    )
    *attended, log_total = attended
    outer_parts = [[outer_mine, outer_other]]
    terms = [dot(half, out_rows).astype(bf16) for half in attended]
    got = steps.run([(twin_send, terms[1])] + [(first_round, shard) for shard in outer_next], 1)
    outer_twos = [rows_joined(shard, g) for shard, g in zip(outer_next, got[1:])]
    kept, sent = reduce_first(terms[0], got[0])
    got = steps.run([(second_round, sent)] + [(second_round, v) for v in outer_twos], 1)
    outer_mines = [rows_joined(v, g) for v, g in zip(outer_twos, got[1:])]
    kept, sent = reduce_second(kept, got[0])
    got = steps.run([(first_round, sent)] + [(twin_send, v) for v in outer_mines], 1)
    outer_parts += [[a, b] for a, b in zip(outer_mines, got[1:])]
    hidden_mid = source + kept.astype(f32) + got[0].astype(f32)
    normed_own = rms_scale(hidden_mid, mlp_gain).astype(bf16)

    got = steps.run(
        [(first_round, normed_own)]
        + [(lambda v, j=j: pair_send(v, -j, pair), normed_own) for j in range(1, pair)],
        1,
    )
    two = rows_joined(normed_own, got[0])
    normed_next = got[1:]
    got = steps.run([(second_round, two)] + [(first_round, v) for v in normed_next], 1)
    mine = rows_joined(two, got[0])
    twos = [rows_joined(v, g) for v, g in zip(normed_next, got[1:])]
    got = steps.run([(twin_send, mine)] + [(second_round, v) for v in twos], 1)
    normed_parts = [[mine, got[0]]]
    mines = [rows_joined(v, g) for v, g in zip(twos, got[1:])]
    if mines:
        got = steps.run([(twin_send, v) for v in mines], 1)
        normed_parts += [[a, b] for a, b in zip(mines, got)]
    steps.drain(lambda: False)
    gate_up_all = join(
        [part for part, _, _ in gate_up_parts], [layer * 2 + n for _, layer, n in gate_up_parts]
    )
    down_all = join([part for part, _, _ in down_parts], [p * 4 + n for _, p, n in down_parts])

    def feed_half(values):
        return feed(*values, gate_up_all, down_all)

    order = [(j, side) for j in reversed(range(pair)) for side in (1, 0)]
    results = {}
    waiting = []
    sums = {}

    def advance():
        return [(function, values) for function, values, _ in waiting]

    def settle(got):
        nonlocal waiting
        ongoing, waiting = waiting, []
        for (_, _, then), value in zip(ongoing, got):
            then(value)

    def reduce_start(j, mine, other):
        def ended(kept):
            def end(value):
                sums[j] = kept.astype(f32) + value.astype(f32)
                if j:
                    waiting.append(
                        (
                            lambda v: pair_send(v, j, pair),
                            sums[j].astype(bf16),
                            lambda value: sums.__setitem__(j, value.astype(f32)),
                        )
                    )

            return end

        def second(kept):
            def end(value):
                now, sent = reduce_second(kept, value)
                waiting.append((first_round, sent, ended(now)))

            return end

        def end(value):
            now, sent = reduce_first(mine(), value)
            waiting.append((second_round, sent, second(now)))

        waiting.append((twin_send, other, end))

    for j, side in order:
        ready = (normed_parts[j][side], outer_parts[j][side])
        result, *got = steps.run([(feed_half, ready)] + advance())
        results[j, side] = result
        settle(got)
        if side:
            reduce_start(j, lambda j=j: results[j, 0][2], result[2])
    keys = [(j, side) for j in range(pair) for side in range(2)]
    normed_flat = [normed_parts[j][side] for j, side in keys]
    outer_flat = [outer_parts[j][side] for j, side in keys]

    class PairTotal:
        def __init__(self, rows_of, operands, count):
            self.rows_of, self.operands, self.count = rows_of, operands, count
            self.pieces, self.got, self.left = None, [], count * (pair_count - 1)
            self.jobs = [
                (functools.partial(self.start, step, n), self.got.append)
                for step in range(1, pair_count)
                for n in range(count)
            ]

        def others(self):
            return (
                lambda v: [
                    self.rows_of(v, (pair_here + step) % pair_count) for step in range(1, pair_count)
                ],
                self.operands,
            )

        def own(self):
            return (lambda v: self.rows_of(v, pair_here), self.operands)

        def start(self, step, n, begin):
            if self.pieces is None:
                function, operands = self.others()
                self.pieces = function(operands)
            return fsdp_send(begin(self.pieces[step - 1][n]), step * pair)

        def complete(self):
            return len(self.got) == self.left

        def total(self, mine):
            steps.drain(self.complete)
            rows_here = [part.astype(f32) for part in mine]
            for k, value in enumerate(self.got):
                rows_here[k % self.count] += value.astype(f32)
            return join([cell_sum(part).astype(bf16) for part in rows_here])

    def side_total(side, count):
        return PairTotal(
            lambda v, p: weight_grad(*v, p, pair_rows, side, local_units, count),
            (normed_flat, [results[k][1] for k in keys]),
            count,
        )

    gate, up = side_total(0, 4), side_total(1, 2)
    down = PairTotal(
        lambda v, p: weight_grad(*v, p, unit, 0, width, 2),
        ([results[k][0] for k in keys], outer_flat),
        2,
    )

    def shares_sent(total):
        return [
            pair_send(block(total, (in_pair + j) % pair, weight_rows), j, pair)
            for j in range(1, pair)
        ]

    def shares(total, got):
        return jnp.concatenate([block(total, in_pair, weight_rows)] + got, axis=1)

    branch_terms = [tuple(results[j, side][3] for side in range(2)) for j in range(pair)]
    branch_twins = []
    steps.jobs = gate.jobs + up.jobs + down.jobs
    kernels = [gate.others(), gate.own()]
    made = []
    while waiting or len(branch_twins) < pair:
        parts = advance()
        count = len(parts)
        extra = []
        if len(branch_twins) < pair:
            extra.append((twin_send, branch_terms[pair - 1 - len(branch_twins)][1]))
        if kernels:
            extra.append(kernels.pop(0))
        got = steps.run(parts + extra, 1 if made else 0)
        settle(got[:count])
        got = got[count:]
        if len(branch_twins) < pair:
            branch_twins.append(got.pop(0))
        if got:
            made.append(got[0])
            gate.pieces = made[0]
    branch_own, hidden_grad, mlp_gain_grad = norm_grad(
        hidden_mid, cotangent, mlp_gain, [sums[j] for j in range(pair)]
    )
    mlp_gain_grad = mlp_gain_grad[0]
    branch_twins = branch_twins[::-1]
    got = steps.run(
        [
            (first_round, branch_own),
            up.others(),
            (
                lambda v: [reduce_first(mine, value) for mine, value in v],
                [(terms[0], value) for terms, value in zip(branch_terms, branch_twins)],
            ),
        ]
        + kernels,
        1,
    )
    made += got[3:]
    gate_mine = made[1]
    up.pieces = got[1]
    branch_kept, branch_sent = map(list, zip(*got[2]))
    two = rows_joined(branch_own, got[0])
    got = steps.run([(second_round, two), up.own()], 1)
    up_mine = got[1]
    mine = rows_joined(two, got[0])
    got = steps.run([(twin_send, mine), (second_round, branch_sent[-1]), down.others()], 1)
    branch_grad = [mine, got[0]]
    branch_kept[-1], branch_sent[-1] = reduce_second(branch_kept[-1], got[1])
    down.pieces = got[2]
    gate_total = gate.total(gate_mine)

    def attention_half(other, kv_grad=None):
        return lambda v: attention_grad(
            place, query_low, v, attended[other], log_total, out_rows, kv_all, rows, chunk, other, kv_grad
        )

    (query_grad_mine, kv_grad), gate_got, *got = steps.run(
        [
            (attention_half(0), branch_grad[0]),
            (shares_sent, gate_total),
        ]
        + [(second_round, sent) for sent in branch_sent[:-1]],
        1,
    )
    gate_share = shares(gate_total, gate_got)
    for j, value in enumerate(got):
        branch_kept[j], branch_sent[j] = reduce_second(branch_kept[j], value)
    (query_grad_other, kv_grad), gate_got, *branch_got = steps.run(
        [(attention_half(1, kv_grad), branch_grad[1]), (first_round, gate_share)]
        + [(first_round, sent) for sent in branch_sent],
        1,
    )
    gate_two = rows_joined(gate_share, gate_got)
    branch_sums = [
        kept.astype(f32) + value.astype(f32) for kept, value in zip(branch_kept, branch_got)
    ]
    outputs = hidden_mid + branch_sums[0]
    query_grad = (query_grad_mine, query_grad_other)
    kv_grad = kv_grad.astype(bf16)
    if cell_count > 1:
        kv_grad_cell = block(kv_grad, cell, CELL * chunk).astype(f32)
        for step in range(1, cell_count):
            piece = block(kv_grad, (cell + step) % cell_count, CELL * chunk)
            kv_grad_cell = kv_grad_cell + cell_send(piece, step).astype(f32)
        kv_grad = kv_grad_cell.astype(bf16)
    kv_grad = kv_grad.reshape(CELL, fsdp_count, rows, 2 * HEAD_DIM)

    def kv_piece(k):
        at = -k % fsdp_count
        return lax.slice_in_dim(kv_grad, at, at + 1, axis=1)

    def fsdp_piece(values, k):
        return block(values, (fsdp_here + k) % fsdp_count, weight_rows)

    up_total = up.total(up_mine)

    def send_then_share(v):
        got = sends[1](v[0])
        return got, shares_sent(after(v[1], got))

    (kv_next, up_got), *got = steps.run(
        [(send_then_share, (kv_piece(1), up_total))]
        + [(sends[k], kv_piece(k)) for k in range(2, fsdp_count)]
        + [
            (second_round, gate_two),
            (
                lambda v: sum(dot(half, branch, TN) for half, branch in zip(*v)).astype(bf16),
                (attended, branch_grad),
            ),
        ]
    )
    out_partial = got.pop()
    kv_total = kv_piece(0).astype(f32) + kv_next.astype(f32)
    for value in got[:-1]:
        kv_total = kv_total + value.astype(f32)
    kv_total = kv_total.reshape(cell_tokens, 2 * HEAD_DIM)
    gate_got = got[-1]
    up_share = shares(up_total, up_got)

    projected, gate_two_twin, up_got, out_partial, *branch_got = steps.run(
        [
            (
                lambda v: project_grad(
                    place, *normed_attn, angles, gains, qkv_rows, query_grad, v, qkv_pieces, rows
                ),
                kv_total,
            ),
            (twin_send, gate_two),
            (first_round, up_share),
            (lambda v: cell_turn(v, 1, 0), out_partial),
        ]
        + [
            (lambda v, j=j: pair_send(v, j, pair), value.astype(bf16))
            for j, value in enumerate(branch_sums[1:], 1)
        ],
        1,
    )
    *qkv_grad, attn_mine, attn_other, head_gain_grad, attention_gain_grad = projected
    up_two = rows_joined(up_share, up_got)
    gains_here = SumEverywhere(jnp.concatenate(
        [
            attention_gain_grad[0] / attention_gain,
            mlp_gain_grad,
            head_gain_grad[0],
            head_gain_grad[1],
        ]
    ).reshape(-1, 2 * HEAD_DIM))

    def gather_place(side, slot, part, whole):
        return place_units(
            whole,
            gate_up_weight.shape,
            part,
            weight_rows,
            unit,
            place,
            lambda i, g, at: (
                side * (hidden_width // unit)
                + ((g % pair_count) * pair + (at[3] - g // pair_count + pair) % pair) * CELL
                + token_block(slot + i, at)
            ),
        )

    def placing(parts):
        def place_all(v):
            whole, arrays = v
            for (side, slot, _), array in zip(parts, arrays):
                whole = gather_place(side, slot, array, whole)
            return whole

        return place_all, (grad_gate_up, [part for _, _, part in parts])

    def fsdp_sum(pieces, got):
        total = pieces[0].astype(f32)
        for value in got:
            total = total + value.astype(f32)
        return cell_sum(total).astype(bf16)

    def sent_pieces(pieces, distances):
        return [(sends[k], pieces[k]) for k in distances]

    def all_pieces(values):
        return [fsdp_piece(values, k) for k in range(fsdp_count)]

    odd_steps, even_steps = range(1, fsdp_count, 2), range(2, fsdp_count, 2)
    grad_gate_up = None
    got = steps.run(
        [
            (twin_send, attn_other),
            (second_round, up_two),
            (twin_send, up_two),
            (
                lambda v: all_pieces(
                    sum(dot(half, grad, TN) for half, grad in zip(*v)).astype(bf16)
                ),
                (normed_attn, qkv_grad),
            ),
            (all_pieces, out_partial),
            down.own(),
            (lambda v: gather_place(0, 0, v, None), gate_two),
            gains_here.part(),
        ],
        1,
    )
    kept, sent = reduce_first(attn_mine, got[0])
    up_got, up_two_twin = got[1:3]
    qkv_parts, out_parts, down_own_rows, grad_gate_up, gain_got = got[3:]
    gains_here.add(gain_got)
    down_share = down.total(down_own_rows)
    got = steps.run(
        [
            (second_round, sent),
            (first_round, down_share),
            (twin_send, gate_got),
            placing([(0, 4, gate_two_twin), (0, 2, gate_got), (1, 0, up_two)]),
        ]
        + sent_pieces(qkv_parts, odd_steps)
    )
    kept, sent = reduce_second(kept, got[0])
    down_two = rows_joined(down_share, got[1])
    gate_got_twin = got[2]
    grad_gate_up = got[3]
    qkv_got = got[4:]
    got = steps.run(
        [
            (first_round, sent),
            (second_round, down_two),
            placing([(0, 6, gate_got_twin), (1, 2, up_got), (1, 4, up_two_twin)]),
            (
                lambda v: sum([g.astype(f32) for g in v[1:]], v[0]).astype(bf16),
                [outputs] + branch_got,
            ),
        ]
        + sent_pieces(qkv_parts, even_steps)
        + sent_pieces(out_parts, odd_steps)
    )
    attn_normed_grad = kept.astype(f32) + got[0].astype(f32)
    down_got = got[1]
    grad_gate_up = got[2]
    outputs = got[3]
    qkv_share = fsdp_sum(qkv_parts, qkv_got + got[4 : 4 + len(even_steps)])
    out_got = got[4 + len(even_steps) :]
    got = steps.run(
        [
            (first_round, qkv_share),
            (twin_send, up_got),
            (twin_send, down_two),
            (lambda v: place_rows(place_rows(None, 0, v[0], place), 2, v[1], place), (down_two, down_got)),
            gains_here.part(),
            (
                lambda v: (
                    v[1] + jax.vjp(lambda u: rms_scale(u, attention_gain), source)[1](v[0])[0]
                ).astype(bf16),
                (attn_normed_grad, hidden_grad),
            ),
        ]
        + sent_pieces(out_parts, even_steps)
    )
    qkv_two = rows_joined(qkv_share, got[0])
    up_got_twin, down_two_twin, grad_down, gain_got, grad_inputs = got[1:6]
    gains_here.add(gain_got)
    out_share = fsdp_sum(out_parts, out_got + got[6:])
    got = steps.run(
        [
            (second_round, qkv_two),
            (first_round, out_share),
            (twin_send, down_got),
            placing([(1, 6, up_got_twin)]),
            (lambda v: place_rows(v[0], 4, v[1], place), (grad_down, down_two_twin)),
            gains_here.part(),
        ]
    )
    qkv_half = rows_joined(qkv_two, got[0])
    out_two = rows_joined(out_share, got[1])
    down_got_twin, grad_gate_up, grad_down, gain_got = got[2:]
    gains_here.add(gain_got)
    got = steps.run(
        [
            (second_round, out_two),
            (twin_send, qkv_half),
            (lambda v: place_rows(v[0], 6, v[1], place), (grad_down, down_got_twin)),
            gains_here.part(),
        ]
    )
    out_half = rows_joined(out_two, got[0])
    qkv_other, grad_down, gain_got = got[1:]
    gains_here.add(gain_got)
    got = steps.run(
        [
            (twin_send, out_half),
            gains_here.part(),
            (lambda v: place_heads(v, place), (qkv_half, qkv_other)),
        ]
    )
    gains_here.add(got[1])
    gain_sums = gains_here.finish().reshape(-1)
    grad_qkv = got[2]
    grad_out = place_columns((out_half, got[0]), width // CELL, place)
    attention_gain_sum, mlp_gain_sum = gain_sums[:width], gain_sums[width : 2 * width]
    head_sums = gain_sums[2 * width :].reshape(4, HEAD_DIM)

    gain_sums = (
        attention_gain_sum,
        head_sums[0] + head_sums[1],
        head_sums[2],
        mlp_gain_sum,
    )

    return (
        outputs,
        grad_inputs,
        gain_sums[0],
        grad_qkv,
        gain_sums[1],
        gain_sums[2],
        grad_out,
        gain_sums[3],
        grad_gate_up,
        grad_down,
    )


def solution(mesh):
    return jax.shard_map(
        body,
        mesh=mesh,
        in_specs=(
            P(("ctx", "fsdp"), None),
            P(),
            P("fsdp", None),
            P(),
            P(),
            P("fsdp", None),
            P(),
            P("fsdp", None),
            P("fsdp", None),
            P(("ctx", "fsdp"), None),
        ),
        out_specs=(
            P(("ctx", "fsdp"), None),
            P(("ctx", "fsdp"), None),
            P(),
            P("fsdp", None),
            P(),
            P(),
            P("fsdp", None),
            P(),
            P("fsdp", None),
            P("fsdp", None),
        ),
        check_vma=False,
    )
```
